32 devices in a mesh: rep: 8 (over y, x, core), shard: 4 (over z).
Axes of the slice: x: 2, y: 2, z: 4, core: 2. Of those that a mesh axis runs over, the one named last changes fastest.
Arguments:
- tokens: bfloat16 [8192, 2048], P(('rep', 'shard')), may hold values from -6 to 6
- cotangent: bfloat16 [8192, 2048], P(('rep', 'shard')), may hold values from -6 to 6
- token_order: int32 [8192], replicated, may hold values from 0 to 8191, as said below
- lengths: int32 [64, 4], P(('rep', 'shard')), may hold values from 1 to 64, 128 in all within a row
- query_weight: bfloat16 [2048, 2048], P('shard'), may hold values from -0.125 to 0.125
- key_weight: bfloat16 [2048, 2048], P('shard'), may hold values from -0.125 to 0.125
- value_weight: bfloat16 [2048, 4096], P('shard'), may hold values from -0.125 to 0.125
- gate_weight: bfloat16 [2048, 4096], P('shard'), may hold values from -0.125 to 0.125
- out_weight: bfloat16 [4096, 2048], P('shard'), may hold values from -0.1875 to 0.1875
- gelu_weight: bfloat16 [2048, 4096], P('shard'), may hold values from -0.125 to 0.125
- up_weight: bfloat16 [2048, 4096], P('shard'), may hold values from -0.125 to 0.125
- down_weight: bfloat16 [4096, 2048], P('shard'), may hold values from -0.1875 to 0.1875
- gain_one: bfloat16 [2048], P('shard'), may hold values from 0.099609375 to 1.8984375
- shift_one: bfloat16 [2048], P('shard'), may hold values from -1.1953125 to 1.1953125
- gain_two: bfloat16 [2048], P('shard'), may hold values from 0.099609375 to 1.8984375
- shift_two: bfloat16 [2048], P('shard'), may hold values from -1.1953125 to 1.1953125
Outputs:
- result: bfloat16 [8192, 2048], P(('rep', 'shard'))
- token_gradient: bfloat16 [8192, 2048], P(('rep', 'shard'))
- query_gradient: float32 [2048, 2048], P('shard')
- key_gradient: float32 [2048, 2048], P('shard')
- value_gradient: float32 [2048, 4096], P('shard')
- gate_gradient: float32 [2048, 4096], P('shard')
- out_gradient: float32 [4096, 2048], P('shard')
- gelu_gradient: float32 [2048, 4096], P('shard')
- up_gradient: float32 [2048, 4096], P('shard')
- down_gradient: float32 [4096, 2048], P('shard')
- gain_one_gradient: float32 [2048], P('shard')
- shift_one_gradient: float32 [2048], P('shard')
- gain_two_gradient: float32 [2048], P('shard')
- shift_two_gradient: float32 [2048], P('shard')
The draws below stay inside these ranges and needn't reach their ends.
Inputs may be any that keep to these rules, and one draw needn't show every extreme that they name: `token_order`: A permutation of the slots. The loader rows [s * 256, (s + 1) * 256) send exactly 8 rows into each block of 256 slots. `lengths`: each row sums to 128; its last entry is the padding at the pack's end, the others are sequences.
All inputs are finite; a program needn't handle non-finite values.
Results may differ from the reference program's by a relative error of at most 0.023.
Values may be sent and summed in bfloat16 or wider, within the bound.
A program may use at most 640 MiB of HBM per device.

```python
import math
import jax
import jax.numpy as jnp
import numpy as np
from jax import lax

D = 2048
HEADS = 8
KH = 256
VH = 512
FF = 4096
PACK = 128
SEQS = 4
KD = 2048
VD = 4096
MOST = 64
TOK_DEV = 256
PIECE = 8
TOKENS = 8192
PACKS = 64


def draw_token_order(key, part):
    device_count = TOK_DEV // PIECE
    key_list = jax.random.split(key, 2 * device_count)
    slot_orders = jax.vmap(lambda sub_key: jax.random.permutation(sub_key, TOK_DEV))(key_list[:device_count]).astype(jnp.int32)
    offsets = (jnp.arange(device_count, dtype=jnp.int32) * TOK_DEV)[:, None, None]
    grid = slot_orders.reshape(device_count, device_count, PIECE) + offsets
    by_source = jnp.transpose(grid, (1, 0, 2)).reshape(device_count, TOK_DEV)
    shuffles = jax.vmap(lambda sub_key: jax.random.permutation(sub_key, TOK_DEV))(key_list[device_count:]).astype(jnp.int32)
    dealt = jnp.take_along_axis(by_source, shuffles, axis=1)
    return dealt.reshape(-1).astype(jnp.int32)


def level_of(stream_key, extent, shards, low, top_value):
    loudness = 1.0
    for dim, parts in shards:
        heights = jax.random.uniform(jax.random.fold_in(jax.random.fold_in(stream_key, 6), dim), (parts,), jnp.float32, low / len(shards), top_value / len(shards))
        loudness = loudness * jnp.repeat(jnp.exp(heights), extent[dim] // parts).reshape((-1,) + (1,) * (len(extent) - 1 - dim))
    return loudness


def profile(amount, total, limit, lean):
    weights = [(1 << 20) // math.isqrt(grade ** lean) + 1 for grade in range(2, amount + 1)]
    spare, holding = total - limit - (amount - 1), [1] * (amount - 1)
    while spare > 0:
        candidates = [i for i in range(amount - 1) if holding[i] < limit]
        mass, left = sum([weights[i] for i in candidates]), spare
        for i in candidates:
            addition = min(limit - holding[i], max(1, left * weights[i] // mass), spare)
            holding[i] = holding[i] + addition
            spare = spare - addition
    return np.array([limit] + holding)


def ragged(stream_key, count, total, limit, lean):
    if count == 2:
        one = jax.random.randint(stream_key, (), max(1, total - limit), min(limit, total - 1) + 1)
        return jnp.stack([one, total - one])
    tallies = jnp.asarray(profile(count, total, limit, lean), jnp.int32)
    couples = (count - 1) // 2
    giver, sink = tallies[1:1 + 2 * couples:2], tallies[2:2 + 2 * couples:2]
    room = jnp.minimum(giver - 1, limit - sink)
    shifted = jax.random.randint(jax.random.fold_in(stream_key, 1), (couples,), 0, 1 << 20) % (room + 1)
    tallies = tallies.at[1:1 + 2 * couples:2].set(giver - shifted).at[2:2 + 2 * couples:2].set(sink + shifted)
    return tallies[jax.random.permutation(jax.random.fold_in(stream_key, 2), count)]


def scatter_about(stream_key, dims, scale, limit, cuts=(), held_as=jnp.bfloat16):
    values = jax.random.normal(stream_key, dims, jnp.float32) * scale
    if len(cuts) > 0:
        values = level_of(stream_key, dims, cuts, -0.22, 0.18) * values
    return jnp.clip(values, min=-limit, max=limit).astype(held_as)


def setup_inputs(seed: int = 0) -> dict:
    streams_of = jax.random.split(jax.random.key(seed), 17)
    return {
        "tokens": scatter_about(streams_of[0], (TOKENS, D), 1.0, 6.0, ((0, 32),)),
        "cotangent": scatter_about(streams_of[1], (TOKENS, D), 1.0, 6.0, ((0, 32),)),
        "token_order": draw_token_order(jax.random.fold_in(streams_of[16], 71), 0),
        "lengths": jax.vmap(lambda own: ragged(own, SEQS, PACK, MOST, 2))(jax.random.split(streams_of[3], PACKS)).reshape((PACKS, SEQS)).astype(jnp.int32),
        "query_weight": scatter_about(streams_of[4], (D, KD), D ** -0.5, 0.125, ((0, 4),)),
        "key_weight": scatter_about(streams_of[5], (D, KD), D ** -0.5, 0.125, ((0, 4),)),
        "value_weight": scatter_about(streams_of[6], (D, VD), D ** -0.5, 0.125, ((0, 4),)),
        "gate_weight": scatter_about(streams_of[7], (D, VD), D ** -0.5, 0.125, ((0, 4),)),
        "out_weight": scatter_about(streams_of[8], (VD, D), (VD // 4) ** -0.5, 0.1875, ((0, 4),)),
        "gelu_weight": scatter_about(streams_of[9], (D, FF), D ** -0.5, 0.125, ((0, 4),)),
        "up_weight": scatter_about(streams_of[10], (D, FF), D ** -0.5, 0.125, ((0, 4),)),
        "down_weight": scatter_about(streams_of[11], (FF, D), (FF // 4) ** -0.5, 0.1875, ((0, 4),)),
        "gain_one": jnp.clip(1.0 + 0.18 * jax.random.normal(streams_of[12], (D,), jnp.float32), 0.099609375, 1.8984375).astype(jnp.bfloat16),
        "shift_one": scatter_about(streams_of[13], (D,), 0.3, 1.1953125, ((0, 4),)),
        "gain_two": jnp.clip(1.0 + 0.18 * jax.random.normal(streams_of[14], (D,), jnp.float32), 0.099609375, 1.8984375).astype(jnp.bfloat16),
        "shift_two": scatter_about(streams_of[15], (D,), 0.3, 1.1953125, ((0, 4),)),
    }


@jax.custom_vjp
def low(v):
    return lax.optimization_barrier(v.astype(jnp.bfloat16)).astype(jnp.float32)

@jax.custom_vjp
def low_back(v):
    return v

def low_keep(v):
    return (low(v), None)

def low_pass(kept, grad):
    return (grad,)

def back_keep(v):
    return (v, None)

def back_low(kept, grad):
    return (low(grad),)
low.defvjp(low_keep, low_pass)
low_back.defvjp(back_keep, back_low)
layer_epsilon = 1e-05
head_epsilon = 1.0
rotary_base = 10000.0

def norm_rows(inputs, gain, shift):
    average = lax.optimization_barrier(jnp.mean(inputs, axis=-1, keepdims=True))
    centred = inputs - average
    spread = lax.optimization_barrier(jnp.mean(centred * centred, axis=-1, keepdims=True))
    return centred * lax.rsqrt(spread + layer_epsilon) * gain + shift

def head_norm(retained):
    shaped = retained.reshape(retained.shape[:-1] + (HEADS, -1))
    average = lax.optimization_barrier(jnp.mean(shaped, axis=-1, keepdims=True))
    centred = shaped - average
    spread = lax.optimization_barrier(jnp.mean(centred * centred, axis=-1, keepdims=True))
    return (centred * lax.rsqrt(spread + head_epsilon)).reshape(retained.shape)

def gate_mix(gating, retained):
    return jax.nn.silu(gating) * head_norm(retained)

def gelu_gate(gelu_in, up_proj):
    return jax.nn.gelu(gelu_in) * up_proj

def rotate(heads_in, cosine_table, sine_table):
    half_size = heads_in.shape[-1] // 2
    former = heads_in[..., :half_size]
    latter = heads_in[..., half_size:]
    return jnp.concatenate([former * cosine_table - latter * sine_table, former * sine_table + latter * cosine_table], axis=-1)

def pack_tables(length_row, pack_rows):
    entries = length_row.shape[0]
    length_int = length_row.astype(jnp.int32)
    slot_ids = jnp.arange(pack_rows, dtype=jnp.int32)
    seq_ends = jnp.cumsum(length_int, dtype=jnp.int32).astype(jnp.int32)
    seq_starts = (seq_ends - length_int).astype(jnp.int32)
    segment = lax.optimization_barrier(jnp.sum((slot_ids[:, None] >= seq_ends[None, :]).astype(jnp.int32), axis=1, dtype=jnp.int32)).astype(jnp.int32)
    owners = segment[:, None] == jnp.arange(entries, dtype=jnp.int32)[None, :]
    begins = lax.optimization_barrier(jnp.sum(jnp.where(owners, seq_starts[None, :], jnp.zeros((), jnp.int32)), axis=1, dtype=jnp.int32)).astype(jnp.int32)
    places = (slot_ids - begins).astype(jnp.float32)
    usable = segment < entries - 1
    half_size = KH // 2
    frequency = jnp.power(jnp.float32(rotary_base), -jnp.arange(half_size, dtype=jnp.float32) / jnp.float32(half_size - 1))
    angles = places[:, None] * frequency[None, :]
    cosine_table = jnp.cos(angles)[:, None, :]
    sine_table = jnp.sin(angles)[:, None, :]
    lag_steps = (slot_ids[:, None] - slot_ids[None, :]).astype(jnp.int32)
    linked = (segment[:, None] == segment[None, :]) & (lag_steps >= 0) & usable[None, :]
    log_rates = jnp.log(1.0 - jnp.power(jnp.float32(2.0), -5.0 - jnp.arange(HEADS, dtype=jnp.float32)))
    lag_float = jnp.where(linked, lag_steps, jnp.zeros((), jnp.int32)).astype(jnp.float32)
    decays = jnp.where(linked[None], jnp.exp(log_rates[:, None, None] * lag_float[None]), jnp.zeros((), jnp.float32))
    return (cosine_table, sine_table, decays, usable)

def layer_forward(inputs, params, cosine_table, sine_table, decays, usable):
    query_weight, key_weight, value_weight, gate_weight, out_weight, gelu_weight, up_weight, down_weight, gain_one, shift_one, gain_two, shift_two = params
    highest = lax.Precision.HIGHEST
    row_count = inputs.shape[0]
    normed = low(norm_rows(inputs, gain_one, shift_one))
    queries = low_back(jnp.dot(normed, query_weight, precision=highest))
    keys_in = low_back(jnp.dot(normed, key_weight, precision=highest))
    v_low = low(low_back(jnp.dot(normed, value_weight, precision=highest))).reshape(row_count, HEADS, VH)
    gating = low_back(jnp.dot(normed, gate_weight, precision=highest))
    q_rot = low(rotate(queries.reshape(row_count, HEADS, KH), cosine_table, sine_table))
    k_rot = low(rotate(keys_in.reshape(row_count, HEADS, KH), cosine_table, sine_table) * KH ** (-0.5))
    scores = low_back(jnp.einsum('ihd,jhd->hij', q_rot, k_rot, precision=highest))
    weights = low(scores * decays)
    retained = low_back(jnp.einsum('hij,jhe->ihe', weights, v_low, precision=highest)).reshape(row_count, HEADS * VH)
    branch = low(gate_mix(gating, retained))
    middle = inputs + low_back(jnp.dot(branch, out_weight, precision=highest))
    normed_two = low(norm_rows(middle, gain_two, shift_two))
    gelu_in = low_back(jnp.dot(normed_two, gelu_weight, precision=highest))
    up_proj = low_back(jnp.dot(normed_two, up_weight, precision=highest))
    hidden = low(gelu_gate(gelu_in, up_proj))
    ending = middle + low_back(jnp.dot(hidden, down_weight, precision=highest))
    return jnp.where(usable[:, None], ending, jnp.zeros((), ending.dtype))

def reference(tokens, cotangent, token_order, lengths, query_weight, key_weight, value_weight, gate_weight, out_weight, gelu_weight, up_weight, down_weight, gain_one, shift_one, gain_two, shift_two):
    total_rows = tokens.shape[0]
    width = tokens.shape[1]
    pack_count = lengths.shape[0]
    pack_rows = total_rows // pack_count
    group_packs = 4
    order_int = token_order.astype(jnp.int32)
    work_tokens = jnp.zeros(tokens.shape, jnp.float32).at[order_int].set(tokens.astype(jnp.float32))
    work_cotangent = jnp.zeros(cotangent.shape, jnp.float32).at[order_int].set(cotangent.astype(jnp.float32))
    params = tuple((matrix.astype(jnp.float32) for matrix in (query_weight, key_weight, value_weight, gate_weight, out_weight, gelu_weight, up_weight, down_weight, gain_one, shift_one, gain_two, shift_two)))
    group_shape = (pack_count // group_packs, group_packs, pack_rows, width)
    checked_forward = jax.checkpoint(layer_forward)

    def group_step(carried, scan_item):
        token_group, cotangent_group, length_group = scan_item
        tables = jax.vmap(lambda length_row: pack_tables(length_row, pack_rows))(length_group)

        def run_layer(inputs, weights_in):
            return jax.vmap(checked_forward, in_axes=(0, None, 0, 0, 0, 0))(inputs, weights_in, tables[0], tables[1], tables[2], tables[3])
        outputs, backward = jax.vjp(run_layer, token_group, params)
        input_grads, param_grads = backward(cotangent_group)
        carried = tuple((summed + adding.astype(summed.dtype) for summed, adding in zip(carried, param_grads)))
        return (carried, (outputs, input_grads))
    starting = tuple((jnp.zeros(matrix.shape, jnp.float32) for matrix in params))
    length_groups = lengths.astype(jnp.int32).reshape(pack_count // group_packs, group_packs, lengths.shape[1])
    totals, (outputs, input_grads) = lax.scan(group_step, starting, (work_tokens.reshape(group_shape), work_cotangent.reshape(group_shape), length_groups))
    result = outputs.reshape(total_rows, width)[order_int].astype(jnp.bfloat16)
    token_gradient = input_grads.reshape(total_rows, width)[order_int].astype(jnp.bfloat16)
    return (result, token_gradient, totals[0], totals[1], totals[2], totals[3], totals[4], totals[5], totals[6], totals[7], totals[8], totals[9], totals[10], totals[11])
```

```python
import functools
import math

import jax
import jax.numpy as jnp
from jax import lax
from jax.sharding import Mesh, PartitionSpec as P

HEADS = 8
KH = 256

layer_epsilon = 1e-05
head_epsilon = 1.0
rotary_base = 10000.0
bf16 = jnp.bfloat16
f32 = jnp.float32


def norm_rows(inputs, gain, shift):
    average = jnp.mean(inputs, axis=-1, keepdims=True)
    centred = inputs - average
    spread = jnp.mean(centred * centred, axis=-1, keepdims=True)
    return centred * lax.rsqrt(spread + layer_epsilon) * gain + shift


def norm_rows_back(inputs, gain, back):
    average = jnp.mean(inputs, axis=-1, keepdims=True)
    centred = inputs - average
    spread = jnp.mean(centred * centred, axis=-1, keepdims=True)
    root = lax.rsqrt(spread + layer_epsilon)
    unit = centred * root
    e = back * gain
    through = root * (
        e - jnp.mean(e, axis=-1, keepdims=True) - unit * jnp.mean(e * unit, axis=-1, keepdims=True)
    )
    return through, jnp.sum(back * unit, axis=0), jnp.sum(back, axis=0)


def head_norm(retained):
    average = jnp.mean(retained, axis=-1, keepdims=True)
    centred = retained - average
    spread = jnp.mean(centred * centred, axis=-1, keepdims=True)
    root = lax.rsqrt(spread + head_epsilon)
    return centred * root, root


def rotate(heads_in, cosine_table, sine_table):
    half_size = heads_in.shape[-1] // 2
    former = heads_in[..., :half_size]
    latter = heads_in[..., half_size:]
    return jnp.concatenate(
        [former * cosine_table - latter * sine_table, former * sine_table + latter * cosine_table],
        axis=-1,
    )


def rotate_back(heads_in, cosine_table, sine_table):
    return rotate(heads_in, cosine_table, -sine_table)


def pack_tables(lengths, pack_rows, head_ids):
    entries = lengths.shape[1]
    slot_ids = jnp.arange(pack_rows, dtype=jnp.int32)
    seq_ends = jnp.cumsum(lengths, axis=1, dtype=jnp.int32)
    seq_starts = seq_ends - lengths
    segment = jnp.sum(
        (slot_ids[None, :, None] >= seq_ends[:, None, :]).astype(jnp.int32), axis=2, dtype=jnp.int32
    )
    owners = segment[:, :, None] == jnp.arange(entries, dtype=jnp.int32)[None, None, :]
    begins = jnp.sum(jnp.where(owners, seq_starts[:, None, :], 0), axis=2, dtype=jnp.int32)
    places = (slot_ids[None, :] - begins).astype(f32)
    usable = segment < entries - 1
    half_size = KH // 2
    frequency = jnp.power(
        f32(rotary_base), -jnp.arange(half_size, dtype=f32) / f32(half_size - 1)
    )
    angles = places[:, :, None] * frequency
    cosine_table = jnp.cos(angles)
    sine_table = jnp.sin(angles)
    lag_steps = slot_ids[:, None] - slot_ids[None, :]
    linked = (
        (segment[:, :, None] == segment[:, None, :])
        & (lag_steps[None] >= 0)
        & usable[:, None, :]
    )
    log_rates = jnp.log(1.0 - jnp.power(f32(2.0), -5.0 - head_ids.astype(f32)))
    powers = jnp.exp(log_rates[:, None, None] * jnp.maximum(lag_steps, 0).astype(f32)[None])
    decays = jnp.where(linked[None], powers[:, None], f32(0.0))
    return cosine_table, sine_table, decays, usable


def gram_rows(leading, trailing):
    return lax.dot_general(
        leading, trailing, (((0,), (0,)), ((), ())), preferred_element_type=f32
    )


def back_through(incoming, matrix):
    return lax.dot_general(
        incoming, matrix, (((1,), (1,)), ((), ())), preferred_element_type=f32
    )


def forward_dot(inputs, matrix):
    return jnp.dot(inputs, matrix, preferred_element_type=f32)


def gelu_parts(v):
    c = f32(math.sqrt(2.0 / math.pi))
    t = jnp.tanh(c * (v + 0.044715 * v * v * v))
    value = 0.5 * v * (1.0 + t)
    slope = 0.5 * (1.0 + t) + 0.5 * v * (1.0 - t * t) * c * (1.0 + 3.0 * 0.044715 * v * v)
    return value, slope


def local(
    tokens,
    cotangent,
    token_order,
    lengths,
    query_weight,
    key_weight,
    value_weight,
    gate_weight,
    out_weight,
    gelu_weight,
    up_weight,
    down_weight,
    gain_one,
    shift_one,
    gain_two,
    shift_two,
):
    every = ("outer", "tp", "shard")
    device_count = lax.axis_size(every)
    device_index = lax.axis_index(every)
    outer, tp, shards = lax.axis_size("outer"), lax.axis_size("tp"), lax.axis_size("shard")
    t, z = lax.axis_index("tp"), lax.axis_index("shard")
    rows, width = tokens.shape
    packs = lengths.shape[0]
    pack_rows = rows // packs
    heads = HEADS // tp
    group_rows = tp * rows
    group_packs = tp * packs

    own_order = lax.dynamic_slice_in_dim(token_order, device_index * rows, rows)
    target = own_order // rows
    places = jnp.arange(rows, dtype=jnp.int32)
    before = (target[None, :] < target[:, None]) | (
        (target[None, :] == target[:, None]) & (places[None, :] < places[:, None])
    )
    send_place = jnp.sum(before.astype(jnp.int32), axis=1)
    send_mix = (send_place[None, :] == places[:, None]).astype(bf16)
    loader_ids = jnp.arange(token_order.shape[0], dtype=jnp.int32)
    slot_targets = device_index * rows + places
    origin = jnp.sum(
        jnp.where(token_order[None, :] == slot_targets[:, None], loader_ids[None, :], 0), axis=1
    )
    arrive_place = jnp.sum((origin[None, :] < origin[:, None]).astype(jnp.int32), axis=1)
    work_mix = (arrive_place[:, None] == places[None, :]).astype(bf16)

    def exchange(value):
        return lax.all_to_all(
            value.reshape(device_count, rows // device_count, width),
            every,
            split_axis=0,
            concat_axis=0,
            tiled=True,
        ).reshape(rows, width)

    work_tokens = forward_dot(work_mix, exchange(forward_dot(send_mix, tokens).astype(bf16)))
    work_cotangent = forward_dot(
        work_mix, exchange(forward_dot(send_mix, cotangent).astype(bf16))
    )

    def along_z(piece):
        return lax.all_gather(piece, "shard", axis=0, tiled=True)

    def columns(weight):
        part = weight.shape[1] // tp
        return along_z(lax.dynamic_slice_in_dim(weight, t * part, part, axis=1))

    small = along_z(jnp.stack([gain_one, shift_one, gain_two, shift_two])[None])
    small = jnp.transpose(small, (1, 0, 2)).reshape(4, width).astype(f32)
    gain_1, shift_1, gain_2, shift_2 = small[0], small[1], small[2], small[3]
    all_lengths = lax.all_gather(lengths, "tp", axis=0, tiled=True)
    head_ids = t * heads + jnp.arange(heads, dtype=jnp.int32)
    cosine, sine, decays, usable_all = pack_tables(all_lengths, pack_rows, head_ids)
    usable = lax.dynamic_slice_in_dim(usable_all, t * packs, packs).reshape(rows, 1)

    wq, wk, wv, wg = (columns(w) for w in (query_weight, key_weight, value_weight, gate_weight))
    out_local = out_weight.shape[0]
    out_all = out_local * shards
    out_part = out_all // tp
    spread_rows = jnp.arange(out_part, dtype=jnp.int32) + t * out_part
    held = jnp.clip(t * out_part - z * out_local, 0, max(out_local - out_part, 0))
    if out_part <= out_local:
        piece = lax.dynamic_slice_in_dim(out_weight, held, out_part, axis=0)
        mine = (t * out_part) // out_local == z
        wo = lax.psum(jnp.where(mine, piece, jnp.zeros((), bf16)), "shard")
    else:
        whole = jnp.zeros((out_all, out_weight.shape[1]), bf16)
        whole = lax.dynamic_update_slice_in_dim(whole, out_weight, z * out_local, axis=0)
        wo = lax.psum(lax.dynamic_slice_in_dim(whole, t * out_part, out_part, axis=0), "shard")

    unit_local = down_weight.shape[0]
    unit = unit_local // tp

    def unit_columns(weight):
        cut = weight.reshape(weight.shape[0], shards, tp, unit)
        cut = lax.dynamic_slice_in_dim(cut, t, 1, axis=2)
        return along_z(cut.reshape(weight.shape[0], shards * unit))

    w_gelu, w_up = unit_columns(gelu_weight), unit_columns(up_weight)
    w_down = along_z(lax.dynamic_slice_in_dim(down_weight, t * unit, unit, axis=0))

    def gather_rows(value):
        return lax.all_gather(value, "tp", axis=0, tiled=True)

    def scatter_rows(value):
        return lax.psum_scatter(
            value.astype(bf16), "tp", scatter_dimension=0, tiled=True
        ).astype(f32)

    def per_head(value):
        return value.reshape(group_packs, pack_rows, heads, -1)

    inputs = work_tokens
    normed = gather_rows(norm_rows(inputs, gain_1, shift_1).astype(bf16))
    cos_t, sin_t = cosine[:, :, None, :], sine[:, :, None, :]
    q_rot = rotate(per_head(forward_dot(normed, wq)), cos_t, sin_t).astype(bf16)
    k_rot = (rotate(per_head(forward_dot(normed, wk)), cos_t, sin_t) * KH ** (-0.5)).astype(bf16)
    v_low = per_head(forward_dot(normed, wv)).astype(bf16)
    gating = per_head(forward_dot(normed, wg))
    scores = jnp.einsum("bihd,bjhd->hbij", q_rot, k_rot, preferred_element_type=f32)
    weights_low = (scores * decays).astype(bf16)
    retained = jnp.einsum("hbij,bjhe->bihe", weights_low, v_low, preferred_element_type=f32)
    unit_retained, root_retained = head_norm(retained)
    sigma = jax.nn.sigmoid(gating)
    silu = gating * sigma
    branch = (silu * unit_retained).astype(bf16).reshape(group_rows, -1)
    middle = inputs + scatter_rows(forward_dot(branch, wo))
    normed_two = gather_rows(norm_rows(middle, gain_2, shift_2).astype(bf16))
    gelu_in = forward_dot(normed_two, w_gelu)
    up_proj = forward_dot(normed_two, w_up)
    gelu_value, gelu_slope = gelu_parts(gelu_in)
    hidden = (gelu_value * up_proj).astype(bf16)
    ending = jnp.where(usable, middle + scatter_rows(forward_dot(hidden, w_down)), 0.0).astype(bf16)

    back_out = jnp.where(usable, work_cotangent, 0.0)
    back_low = gather_rows(back_out.astype(bf16))
    back_hidden = back_through(back_low, w_down)
    gelu_low = (back_hidden * up_proj * gelu_slope).astype(bf16)
    up_low = (back_hidden * gelu_value).astype(bf16)
    back_normed_two = scatter_rows(back_through(gelu_low, w_gelu) + back_through(up_low, w_up))
    through_two, gain_two_part, shift_two_part = norm_rows_back(middle, gain_2, back_normed_two)
    back_middle = back_out + through_two
    middle_low = gather_rows(back_middle.astype(bf16))
    back_branch = back_through(middle_low, wo).reshape(group_packs, pack_rows, heads, -1)
    gating_low = (
        back_branch * unit_retained * (sigma * (1.0 + gating * (1.0 - sigma)))
    ).astype(bf16)
    e = back_branch * silu
    retained_low = (
        root_retained
        * (
            e
            - jnp.mean(e, axis=-1, keepdims=True)
            - unit_retained * jnp.mean(e * unit_retained, axis=-1, keepdims=True)
        )
    ).astype(bf16)
    back_weights = jnp.einsum("bihe,bjhe->hbij", retained_low, v_low, preferred_element_type=f32)
    values_low = jnp.einsum(
        "hbij,bihe->bjhe", weights_low, retained_low, preferred_element_type=f32
    ).astype(bf16)
    back_scores = (back_weights * decays).astype(bf16)
    back_queries = jnp.einsum("hbij,bjhd->bihd", back_scores, k_rot, preferred_element_type=f32)
    back_keys = jnp.einsum("hbij,bihd->bjhd", back_scores, q_rot, preferred_element_type=f32)
    queries_low = rotate_back(back_queries, cos_t, sin_t).astype(bf16)
    keys_low = (rotate_back(back_keys, cos_t, sin_t) * KH ** (-0.5)).astype(bf16)
    queries_low, keys_low, values_low, gating_low = (
        v.reshape(group_rows, -1) for v in (queries_low, keys_low, values_low, gating_low)
    )
    back_normed = scatter_rows(
        back_through(queries_low, wq)
        + back_through(keys_low, wk)
        + back_through(values_low, wv)
        + back_through(gating_low, wg)
    )
    through_one, gain_one_part, shift_one_part = norm_rows_back(inputs, gain_1, back_normed)
    back_inputs = (back_middle + through_one).astype(bf16)

    def settle(value):
        return lax.psum(value, "outer") if outer > 1 else value

    def column_gradient(left, right):
        part = lax.psum_scatter(
            gram_rows(left, right).astype(bf16), "shard", scatter_dimension=0, tiled=True
        )
        return settle(part)

    def by_columns(left, right):
        return lax.all_gather(
            column_gradient(left, right), "tp", axis=1, tiled=True
        ).astype(f32)

    def by_units(left, right):
        part = column_gradient(left, right).reshape(-1, shards, unit)
        gathered = lax.all_gather(part, "tp", axis=0)
        return jnp.transpose(gathered, (1, 2, 0, 3)).reshape(part.shape[0], -1).astype(f32)

    down_gradient = lax.all_gather(
        column_gradient(hidden, back_low), "tp", axis=0, tiled=True
    ).astype(f32)
    gelu_gradient = by_units(normed_two, gelu_low)
    up_gradient = by_units(normed_two, up_low)
    out_part_sum = settle(lax.psum(gram_rows(branch, middle_low).astype(bf16), "shard"))
    placed = jnp.zeros((out_all, width), bf16)
    placed = lax.dynamic_update_slice_in_dim(placed, out_part_sum, t * out_part, axis=0)
    out_gradient = lax.psum(
        lax.dynamic_slice_in_dim(placed, z * out_local, out_local, axis=0), "tp"
    ).astype(f32)
    query_gradient = by_columns(normed, queries_low)
    key_gradient = by_columns(normed, keys_low)
    value_gradient = by_columns(normed, values_low)
    gate_gradient = by_columns(normed, gating_low)
    smalls = jnp.stack([gain_one_part, shift_one_part, gain_two_part, shift_two_part])
    smalls = lax.psum(smalls, every)
    smalls = lax.dynamic_slice_in_dim(smalls, z * (width // shards), width // shards, axis=1)

    def give_back(value):
        home = exchange(gram_rows(work_mix, value).astype(bf16))
        return gram_rows(send_mix, home).astype(bf16)

    result = give_back(ending)
    token_gradient = give_back(back_inputs)
    return (
        result,
        token_gradient,
        query_gradient,
        key_gradient,
        value_gradient,
        gate_gradient,
        out_gradient,
        gelu_gradient,
        up_gradient,
        down_gradient,
        smalls[0],
        smalls[1],
        smalls[2],
        smalls[3],
    )


def solution(mesh):
    tp = math.gcd(mesh.shape["rep"], HEADS)
    grid = mesh.devices.reshape(mesh.shape["rep"] // tp, tp, mesh.shape["shard"])
    cube = Mesh(grid, ("outer", "tp", "shard"))
    tokens_at = P(("outer", "tp", "shard"), None)
    weights_at = P("shard", None)
    vectors_at = P("shard")
    in_specs = (tokens_at, tokens_at, P(), tokens_at) + (weights_at,) * 8 + (vectors_at,) * 4
    out_specs = (tokens_at, tokens_at) + (weights_at,) * 8 + (vectors_at,) * 4
    return jax.shard_map(local, mesh=cube, in_specs=in_specs, out_specs=out_specs, check_vma=False)
```

```python
import functools
import math

import jax
import jax.numpy as jnp
from jax import lax
from jax.experimental import pallas as pl
from jax.experimental.pallas import tpu as pltpu
from jax.sharding import Mesh, PartitionSpec as P

HEADS = 8
KH = 256

layer_epsilon = 1e-05
head_epsilon = 1.0
rotary_base = 10000.0
bf16 = jnp.bfloat16
f32 = jnp.float32
MESHID = pl.DeviceIdType.MESH


def pack_tables(lengths, pack_rows, head_ids):
    entries = lengths.shape[1]
    slot_ids = jnp.arange(pack_rows, dtype=jnp.int32)
    seq_ends = jnp.cumsum(lengths, axis=1, dtype=jnp.int32)
    seq_starts = seq_ends - lengths
    segment = jnp.sum(
        (slot_ids[None, :, None] >= seq_ends[:, None, :]).astype(jnp.int32), axis=2, dtype=jnp.int32
    )
    owners = segment[:, :, None] == jnp.arange(entries, dtype=jnp.int32)[None, None, :]
    begins = jnp.sum(jnp.where(owners, seq_starts[:, None, :], 0), axis=2, dtype=jnp.int32)
    places = (slot_ids[None, :] - begins).astype(f32)
    usable = segment < entries - 1
    half_size = KH // 2
    frequency = jnp.power(
        f32(rotary_base), -jnp.arange(half_size, dtype=f32) / f32(half_size - 1)
    )
    angles = places[:, :, None] * frequency
    cosine_table = jnp.cos(angles)
    sine_table = jnp.sin(angles)
    lag_steps = slot_ids[:, None] - slot_ids[None, :]
    linked = (
        (segment[:, :, None] == segment[:, None, :])
        & (lag_steps[None] >= 0)
        & usable[:, None, :]
    )
    log_rates = jnp.log(1.0 - jnp.power(f32(2.0), -5.0 - head_ids.astype(f32)))
    powers = jnp.exp(log_rates[:, None, None] * jnp.maximum(lag_steps, 0).astype(f32)[None])
    decays = jnp.where(linked[None], powers[:, None], f32(0.0))
    return cosine_table, sine_table, decays, usable


def gram_rows(leading, trailing):
    return lax.dot_general(
        leading, trailing, (((0,), (0,)), ((), ())), preferred_element_type=f32
    )


def back_through(incoming, matrix):
    return lax.dot_general(
        incoming, matrix, (((1,), (1,)), ((), ())), preferred_element_type=f32
    )


def forward_dot(inputs, matrix):
    return jnp.dot(inputs, matrix, preferred_element_type=f32)


def gelu_parts(v):
    c = f32(math.sqrt(2.0 / math.pi))
    t = jnp.tanh(c * (v + 0.044715 * v * v * v))
    value = 0.5 * v * (1.0 + t)
    slope = 0.5 * (1.0 + t) + 0.5 * v * (1.0 - t * t) * c * (1.0 + 3.0 * 0.044715 * v * v)
    return value, slope


def flip(me, mask):
    for bit in (1, 2, 4):
        if mask & bit:
            me = me + bit - 2 * bit * ((me // bit) % 2)
    return me


def greet(far=False):
    me = lax.axis_index("tp")
    barrier = pltpu.get_barrier_semaphore()
    for mask in (1, 2, 4):
        pl.semaphore_signal(
            barrier, inc=1, device_id={"tp": flip(me, mask)}, device_id_type=MESHID
        )
    count = 3
    if far:
        for other in others():
            pl.semaphore_signal(barrier, inc=1, device_id={"shard": other}, device_id_type=MESHID)
            count += 1
    pl.semaphore_wait(barrier, count)
    return me


def others():
    shards = lax.axis_size("shard")
    return [(lax.axis_index("shard") + k) % shards for k in range(1, shards)]


def push(source, goal, send, recv, peer):
    return pltpu.make_async_remote_copy(
        src_ref=source, dst_ref=goal, send_sem=send, recv_sem=recv,
        device_id={"tp": peer}, device_id_type=MESHID,
    )


def gather_steps(me, own, out, send, recv):
    rows = own.shape[0]
    half = rows // 2
    sib, xn, yn, dn = flip(me, 1), flip(me, 2), flip(me, 4), flip(me, 6)

    def cp(i, src, goal, peer):
        return push(src, goal, send.at[i], recv.at[i], peer)

    low, high = pl.ds(0, half), pl.ds(half, half)
    first = [
        cp(0, own, out.at[me], xn),
        cp(1, own, out.at[me], yn),
        cp(2, own, out.at[me], sib),
    ]
    for c in first:
        c.start()
    first[0].wait_recv()
    c3 = cp(3, out.at[xn, low], out.at[xn, low], yn)
    c3.start()
    c4 = cp(4, out.at[xn], out.at[xn], sib)
    c4.start()
    first[1].wait_recv()
    c5 = cp(5, out.at[yn, high], out.at[yn, high], xn)
    c5.start()
    c6 = cp(6, out.at[yn], out.at[yn], sib)
    c6.start()
    c3.wait_recv()
    c7 = cp(7, out.at[dn, low], out.at[dn, low], sib)
    c7.start()
    c5.wait_recv()
    c8 = cp(8, out.at[dn, high], out.at[dn, high], sib)
    c8.start()
    first[2].wait_recv()
    for c in (c4, c6, c7, c8):
        c.wait_recv()
    for c in first + [c3, c4, c5, c6, c7, c8]:
        c.wait_send()


COLS = 512


def reduce_steps(me, pairs, transposed, tosib, fromsib, hold, hop, final, total, send, recv, between=None):
    rows, width = total.shape
    half = rows // 2
    sib, xn, yn = flip(me, 1), flip(me, 2), flip(me, 4)
    low, high = pl.ds(0, half), pl.ds(half, half)

    def product(block, tile):
        acc = None
        for act, weight in pairs:
            left = act[pl.ds(pl.multiple_of(block * rows, rows), rows), :]
            if transposed:
                part = lax.dot_general(
                    left, weight[pl.ds(pl.multiple_of(tile * COLS, COLS), COLS), 0 : act.shape[1]],
                    (((1,), (1,)), ((), ())), preferred_element_type=f32,
                )
            else:
                part = jnp.dot(
                    left, weight[:, pl.ds(pl.multiple_of(tile * COLS, COLS), COLS)],
                    preferred_element_type=f32,
                )
            acc = part if acc is None else acc + part
        return acc

    def cp(i, src, goal, peer):
        return push(src, goal, send.at[i], recv.at[i], peer)

    masks = (6, 2, 4, 0)
    over, out = [], {}

    def for_sibling(slot):
        block = flip(me, masks[slot] ^ 1)

        @pl.loop(0, width // COLS)
        def _(tile):
            at = pl.ds(pl.multiple_of(tile * COLS, COLS), COLS)
            tosib[slot, :, at] = product(block, tile).astype(bf16)

        c = cp(slot, tosib.at[slot], fromsib.at[slot], sib)
        c.start()
        over.append(c)

    def for_own_core(slot):
        block = flip(me, masks[slot])
        over[slot].wait_recv()

        @pl.loop(0, width // COLS)
        def _(tile):
            at = pl.ds(pl.multiple_of(tile * COLS, COLS), COLS)
            value = product(block, tile) + fromsib[slot, :, at].astype(f32)
            if slot < 3:
                hold[slot, :, at] = value.astype(bf16)
            else:
                total[:, at] = value

    for_sibling(0)
    for_sibling(1)
    for_own_core(0)
    dx = cp(4, hold.at[0, low], hop.at[0], xn)
    dy = cp(5, hold.at[0, high], hop.at[1], yn)
    dx.start()
    dy.start()
    for_sibling(2)
    for_own_core(1)
    xa = cp(6, hold.at[1, low], final.at[0, low], xn)
    xa.start()
    for_sibling(3)
    for_own_core(2)
    yb = cp(7, hold.at[2, high], final.at[1, high], yn)
    yb.start()
    for_own_core(3)
    if between is not None:
        between()
    dy.wait_recv()
    hold[1, high] = (hold[1, high].astype(f32) + hop[1].astype(f32)).astype(bf16)
    xb = cp(8, hold.at[1, high], final.at[0, high], xn)
    xb.start()
    dx.wait_recv()
    hold[2, low] = (hold[2, low].astype(f32) + hop[0].astype(f32)).astype(bf16)
    ya = cp(9, hold.at[2, low], final.at[1, low], yn)
    ya.start()
    xa.wait_recv()
    yb.wait_recv()
    xb.wait_recv()
    ya.wait_recv()
    for c in over + [dx, dy, xa, yb, xb, ya]:
        c.wait_send()


def summed(total, final, at):
    return total[at, :] + final[0, at, :].astype(f32) + final[1, at, :].astype(f32)


def reduce_scratch(rows, width):
    return [
        pltpu.VMEM((4, rows, width), bf16),
        pltpu.VMEM((4, rows, width), bf16),
        pltpu.VMEM((3, rows, width), bf16),
        pltpu.VMEM((2, rows // 2, width), bf16),
        pltpu.VMEM((2, rows, width), bf16),
        pltpu.VMEM((rows, width), f32),
        pltpu.SemaphoreType.DMA((10,)),
        pltpu.SemaphoreType.DMA((10,)),
    ]


CHUNK = 32


def cost(us):
    return pl.CostEstimate(flops=int(us * 1e9), bytes_accessed=int(us * 3e6), transcendentals=0)


def params(cid=None):
    if cid is None:
        return pltpu.CompilerParams(vmem_limit_bytes=60 << 20)
    return pltpu.CompilerParams(collective_id=cid, has_side_effects=True, vmem_limit_bytes=60 << 20)


def by_rows(count):
    def run(body):
        @pl.loop(0, count // CHUNK)
        def _(i):
            body(pl.ds(pl.multiple_of(i * CHUNK, CHUNK), CHUNK))

    return run


def centre(value, epsilon):
    average = jnp.mean(value, axis=-1, keepdims=True)
    centred = value - average
    spread = jnp.mean(centred * centred, axis=-1, keepdims=True)
    root = lax.rsqrt(spread + epsilon)
    return centred * root, root


def through_norm(e, unit, root):
    return root * (
        e - jnp.mean(e, axis=-1, keepdims=True) - unit * jnp.mean(e * unit, axis=-1, keepdims=True)
    )


def leading(rows, columns):
    return pl.BlockSpec((rows, columns), lambda *_: (0, 0))


ANY = pl.BlockSpec(memory_space=pl.ANY)
WHOLE = pl.BlockSpec(memory_space=pltpu.VMEM)


def gather_scratch(rows, width):
    return [
        pltpu.VMEM((rows, width), bf16),
        pltpu.SemaphoreType.DMA((9,)),
        pltpu.SemaphoreType.DMA((9,)),
        pltpu.SemaphoreType.DMA,
    ]


def gather_all(me, own, out, send, recv, local_sem):
    mine = pltpu.make_async_copy(own, out.at[me], local_sem)
    mine.start()
    gather_steps(me, own, out, send, recv)
    mine.wait()


def entry_kernel(
    came, mix, gains, lens, x_out, normed_all, lens_all, small,
    own, send, recv, sem, send2, recv2, sem2, all_gains, send3, recv3,
):
    me = greet(True)
    z = lax.axis_index("shard")
    copies = []
    for k, other in enumerate(others()):
        c = pltpu.make_async_remote_copy(
            src_ref=gains,
            dst_ref=all_gains.at[z],
            send_sem=send3.at[k],
            recv_sem=recv3.at[k],
            device_id={"shard": other},
            device_id_type=MESHID,
        )
        c.start()
        copies.append(c)
    all_gains[z] = gains[...]
    gather_all(me, lens, lens_all, send2, recv2, sem2)
    for c in copies:
        c.wait()
    part = gains.shape[1]
    for i in range(all_gains.shape[0]):
        small[:, i * part : (i + 1) * part] = all_gains[i]

    @by_rows(came.shape[0])
    def _(at):
        value = jnp.dot(mix[at, :], came[...], preferred_element_type=f32)
        x_out[at, :] = value.astype(bf16)
        unit, _ = centre(value, layer_epsilon)
        own[at, :] = (unit * small[0:1, :] + small[1:2, :]).astype(bf16)

    gather_all(me, own, normed_all, send, recv, sem)


def entry(came, mix, gains, lens, cid):
    rows, width = came.shape
    shards = lax.axis_size("shard")
    return pl.pallas_call(
        entry_kernel,
        out_shape=(
            jax.ShapeDtypeStruct((rows, width), bf16),
            jax.ShapeDtypeStruct((8, rows, width), bf16),
            jax.ShapeDtypeStruct((8,) + lens.shape, lens.dtype),
            jax.ShapeDtypeStruct((8, width), f32),
        ),
        in_specs=[WHOLE] * 3 + [ANY],
        out_specs=(WHOLE, ANY, ANY, WHOLE),
        scratch_shapes=gather_scratch(rows, width)
        + gather_scratch(rows, width)[1:]
        + [
            pltpu.VMEM((shards, 8, width // shards), f32),
            pltpu.SemaphoreType.DMA((shards - 1,)),
            pltpu.SemaphoreType.DMA((shards - 1,)),
        ],
        compiler_params=params(cid),
        cost_estimate=cost(50),
        name="entry",
    )(came, mix, gains, lens)


def entry_back_kernel(came, mix, usable, _after, back_out, back_all, own, send, recv, sem):
    me = greet()

    @by_rows(came.shape[0])
    def _(at):
        value = jnp.dot(mix[at, :], came[...], preferred_element_type=f32)
        value = jnp.where(usable[at, :] > 0.5, value, 0.0).astype(bf16)
        back_out[at, :] = value
        own[at, :] = value

    gather_all(me, own, back_all, send, recv, sem)


def entry_back(came, mix, usable, after, cid):
    rows, width = came.shape
    return pl.pallas_call(
        entry_back_kernel,
        out_shape=(
            jax.ShapeDtypeStruct((rows, width), bf16),
            jax.ShapeDtypeStruct((8, rows, width), bf16),
        ),
        in_specs=[WHOLE] * 3 + [ANY],
        out_specs=(WHOLE, ANY),
        scratch_shapes=gather_scratch(rows, width),
        compiler_params=params(cid),
        cost_estimate=cost(45),
        name="entry_back",
    )(came, mix, usable, after)


def deal_plan(back, count):
    heads = HEADS // count
    me = lax.axis_index("tp")
    spread = [i * heads + me // count for i in range(count)]
    packed = [(me % heads) * count + i for i in range(count)]
    goals, sources = (packed, spread) if back else (spread, packed)
    return me, goals, sources, (me // heads if back else me % count), me // count == me % heads


def deal_start(back, pieces, out, send, recv, local_sem):
    count = pieces.shape[0]
    me, goals, sources, slot, inside = deal_plan(back, count)
    barrier = pltpu.get_barrier_semaphore()
    for i in range(count):

        @pl.when(sources[i] != me)
        def _():
            pl.semaphore_signal(
                barrier, inc=1, device_id={"tp": sources[i]}, device_id_type=MESHID
            )

    pl.semaphore_wait(barrier, jnp.where(inside, count - 1, count))
    for i in range(count):

        @pl.when(goals[i] == me)
        def _():
            pltpu.make_async_copy(pieces.at[i], out.at[slot], local_sem).start()

        @pl.when(goals[i] != me)
        def _():
            push(pieces.at[i], out.at[slot], send.at[i], recv.at[slot], goals[i]).start()


def deal_wait(back, pieces, out, send, recv, local_sem):
    count = pieces.shape[0]
    me, goals, sources, slot, _ = deal_plan(back, count)
    for i in range(count):

        @pl.when(goals[i] == me)
        def _():
            pltpu.make_async_copy(pieces.at[i], out.at[slot], local_sem).wait()

        @pl.when(goals[i] != me)
        def _():
            push(pieces.at[i], out.at[slot], send.at[i], recv.at[slot], goals[i]).wait_send()

        @pl.when(sources[i] != me)
        def _():
            push(pieces.at[i], out.at[i], send.at[i], recv.at[i], sources[i]).wait_recv()


def deal_scratch(count):
    return [
        pltpu.SemaphoreType.DMA((count,)),
        pltpu.SemaphoreType.DMA((count,)),
        pltpu.SemaphoreType.DMA,
    ]


def turn(value, cosine, sine):
    half = value.shape[-1] // 2
    a, b = value[:, :half], value[:, half:]
    return jnp.concatenate([a * cosine - b * sine, a * sine + b * cosine], axis=1)


def retain_kernel(
    normed, weight, cosine, sine, decays, pieces,
    q_out, k_out, v_out, w_out, g_out, r_out, branch, wo, *sems
):
    @pl.when(pl.program_id(0) == 0)
    def _():
        deal_start(False, pieces, wo, *sems)

    packs, span = decays.shape[0], decays.shape[1]
    value_at = 2 * KH
    gate_at = value_at + v_out.shape[1]
    rows = normed[...]

    def project(begin, size):
        return jnp.dot(rows, weight[:, begin : begin + size], preferred_element_type=f32)

    q_out[...] = turn(project(0, KH), cosine[...], sine[...]).astype(bf16)
    k_out[...] = (turn(project(KH, KH), cosine[...], sine[...]) * KH ** (-0.5)).astype(bf16)
    v_out[...] = project(value_at, v_out.shape[1]).astype(bf16)
    g_out[...] = project(gate_at, g_out.shape[1])
    for p in range(packs):
        at = pl.ds(p * span, span)
        scores = lax.dot_general(
            q_out[at, :], k_out[at, :], (((1,), (1,)), ((), ())), preferred_element_type=f32
        )
        low = (scores * decays[p]).astype(bf16)
        w_out[p] = low
        retained = jnp.dot(low, v_out[at, :], preferred_element_type=f32)
        r_out[at, :] = retained
        unit, _ = centre(retained, head_epsilon)
        gating = g_out[at, :]
        branch[at, :] = (gating * jax.nn.sigmoid(gating) * unit).astype(bf16)

    @pl.when(pl.program_id(0) == pl.num_programs(0) - 1)
    def _():
        deal_wait(False, pieces, wo, *sems)


def retain(normed, weight, value_size, cosine, sine, decays, pieces, block, cid):
    total, width = normed.shape
    span = decays.shape[1]
    grid = total // block
    row = lambda w: pl.BlockSpec((block, w), lambda i: (i, 0))
    square = pl.BlockSpec((block // span, span, span), lambda i: (i, 0, 0))
    flat = lambda w, kind: jax.ShapeDtypeStruct((total, w), kind)
    return pl.pallas_call(
        retain_kernel,
        grid=(grid,),
        in_specs=[
            row(width), leading(width, 2 * KH + 2 * value_size), row(KH // 2), row(KH // 2), square,
            ANY,
        ],
        out_specs=(
            row(KH), row(KH), row(value_size), square, row(value_size), row(value_size),
            row(value_size), ANY,
        ),
        out_shape=(
            flat(KH, bf16), flat(KH, bf16), flat(value_size, bf16),
            jax.ShapeDtypeStruct(decays.shape, bf16), flat(value_size, f32),
            flat(value_size, f32), flat(value_size, bf16),
            jax.ShapeDtypeStruct(pieces.shape, bf16),
        ),
        scratch_shapes=deal_scratch(pieces.shape[0]),
        compiler_params=params(cid),
        cost_estimate=cost(24),
        name="retain",
    )(normed, weight, cosine, sine, decays, pieces)


def retain_back_kernel(
    middle_low, wo, q_in, k_in, v_in, w_in, g_in, r_in, cosine, sine, decays, pieces,
    low, dealt, *sems
):
    @pl.when(pl.program_id(0) == 0)
    def _():
        deal_start(True, pieces, dealt, *sems)

    packs, span = decays.shape[0], decays.shape[1]
    value_at = 2 * KH
    value_size = v_in.shape[1]
    gate_at = value_at + value_size
    back_branch = lax.dot_general(
        middle_low[...], wo[...], (((1,), (1,)), ((), ())), preferred_element_type=f32
    )
    cols = (((0,), (0,)), ((), ()))
    last = (((1,), (1,)), ((), ()))
    for p in range(packs):
        at = pl.ds(p * span, span)
        bb = back_branch[p * span : (p + 1) * span]
        unit, root = centre(r_in[at, :], head_epsilon)
        gating = g_in[at, :]
        sigma = jax.nn.sigmoid(gating)
        low[at, gate_at:] = (bb * unit * (sigma * (1.0 + gating * (1.0 - sigma)))).astype(bf16)
        retained_low = through_norm(bb * (gating * sigma), unit, root).astype(bf16)
        back_weights = lax.dot_general(retained_low, v_in[at, :], last, preferred_element_type=f32)
        low[at, value_at:gate_at] = lax.dot_general(
            w_in[p], retained_low, cols, preferred_element_type=f32
        ).astype(bf16)
        back_scores = (back_weights * decays[p]).astype(bf16)
        back_q = jnp.dot(back_scores, k_in[at, :], preferred_element_type=f32)
        back_k = lax.dot_general(back_scores, q_in[at, :], cols, preferred_element_type=f32)
        low[at, :KH] = turn(back_q, cosine[at, :], -sine[at, :]).astype(bf16)
        low[at, KH:value_at] = (turn(back_k, cosine[at, :], -sine[at, :]) * KH ** (-0.5)).astype(bf16)

    @pl.when(pl.program_id(0) == pl.num_programs(0) - 1)
    def _():
        deal_wait(True, pieces, dealt, *sems)


def retain_back(middle_low, wo, q, k, v, w, g, r, cosine, sine, decays, pieces, block, cid):
    total, width = middle_low.shape
    span = decays.shape[1]
    value_size = v.shape[1]
    row = lambda w: pl.BlockSpec((block, w), lambda i: (i, 0))
    square = pl.BlockSpec((block // span, span, span), lambda i: (i, 0, 0))
    return pl.pallas_call(
        retain_back_kernel,
        grid=(total // block,),
        in_specs=[
            row(width), WHOLE, row(KH), row(KH), row(value_size), square, row(value_size),
            row(value_size), row(KH // 2), row(KH // 2), square, ANY,
        ],
        out_specs=(row(2 * KH + 2 * value_size), ANY),
        out_shape=(
            jax.ShapeDtypeStruct((total, 2 * KH + 2 * value_size), bf16),
            jax.ShapeDtypeStruct(pieces.shape, bf16),
        ),
        scratch_shapes=deal_scratch(pieces.shape[0]),
        compiler_params=params(cid),
        cost_estimate=cost(20),
        name="retain_back",
    )(middle_low, wo, q, k, v, w, g, r, cosine, sine, decays, pieces)


def feed_kernel(shards, normed_two, back_low, w_two, hidden, low, w_down):
    size = hidden.shape[1]

    @pl.when(pl.program_id(0) == 0)
    def _():
        unit = size // shards
        span = w_two.shape[0] // shards
        part = w_two.shape[1] - 2 * size
        for z in range(shards):
            for c in range(span // unit):
                begin = z * span + c * unit
                w_down[z * unit : (z + 1) * unit, c * part : (c + 1) * part] = w_two[
                    begin : begin + unit, 2 * size :
                ]

    both = jnp.dot(normed_two[...], w_two[:, : 2 * size], preferred_element_type=f32)
    back = lax.dot_general(
        back_low[...], w_down[...], (((1,), (1,)), ((), ())), preferred_element_type=f32
    )
    up = both[:, size:]
    value, slope = gelu_parts(both[:, :size])
    hidden[...] = (value * up).astype(bf16)
    low[:, :size] = (back * up * slope).astype(bf16)
    low[:, size:] = (back * value).astype(bf16)


def feed(normed_two, back_low, w_two, size, shards, block):
    total, width = normed_two.shape
    row = lambda w: pl.BlockSpec((block, w), lambda i: (i, 0))
    return pl.pallas_call(
        functools.partial(feed_kernel, shards),
        grid=(total // block,),
        in_specs=[row(width), row(width), WHOLE],
        out_specs=(row(size), row(2 * size), pl.BlockSpec((size, width), lambda i: (0, 0))),
        out_shape=(
            jax.ShapeDtypeStruct((total, size), bf16),
            jax.ShapeDtypeStruct((total, 2 * size), bf16),
            jax.ShapeDtypeStruct((size, width), bf16),
        ),
        compiler_params=params(),
        cost_estimate=cost(18),
        name="feed",
    )(normed_two, back_low, w_two)


def middle_kernel(branch, wo, x, small, middle, normed_all, own, send1, recv1, sem1, *scratch):
    me = greet()
    reduce_steps(me, [(branch, wo)], False, *scratch)
    final, total = scratch[4], scratch[5]

    @by_rows(x.shape[0])
    def _(at):
        value = x[at, :].astype(f32) + summed(total, final, at)
        middle[at, :] = value
        unit, _ = centre(value, layer_epsilon)
        own[at, :] = (unit * small[2:3, :] + small[3:4, :]).astype(bf16)

    gather_all(me, own, normed_all, send1, recv1, sem1)


def make_middle(branch, wo, x, small, cid):
    rows, width = x.shape
    return pl.pallas_call(
        middle_kernel,
        out_shape=(
            jax.ShapeDtypeStruct((rows, width), f32),
            jax.ShapeDtypeStruct((8, rows, width), bf16),
        ),
        in_specs=[WHOLE] * 4,
        out_specs=(WHOLE, ANY),
        scratch_shapes=gather_scratch(rows, width) + reduce_scratch(rows, width),
        compiler_params=params(cid),
        cost_estimate=cost(85),
        name="make_middle",
    )(branch, wo, x, small)


def column_sums(out, row, value, first):
    total = jnp.sum(value, axis=0, keepdims=True)

    @pl.when(first)
    def _():
        out[row : row + 1, :] = total

    @pl.when(jnp.logical_not(first))
    def _():
        out[row : row + 1, :] += total


def back_middle_kernel(
    low, weight, middle, back_out, small, _after, _more, back_middle, parts, middle_all,
    own, send1, recv1, sem1, *scratch,
):
    me = greet()
    reduce_steps(me, [(low, weight)], True, *scratch)
    final, total = scratch[4], scratch[5]
    parts[...] = jnp.zeros_like(parts)

    @by_rows(middle.shape[0])
    def _(at):
        back = summed(total, final, at)
        unit, root = centre(middle[at, :], layer_epsilon)
        parts[0:1, :] += jnp.sum(back * unit, axis=0, keepdims=True)
        parts[1:2, :] += jnp.sum(back, axis=0, keepdims=True)
        value = back_out[at, :].astype(f32) + through_norm(back * small[2:3, :], unit, root)
        back_middle[at, :] = value
        own[at, :] = value.astype(bf16)

    gather_all(me, own, middle_all, send1, recv1, sem1)


def make_back_middle(low, weight, middle, back_out, small, after, more, cid):
    rows, width = middle.shape
    return pl.pallas_call(
        back_middle_kernel,
        out_shape=(
            jax.ShapeDtypeStruct((rows, width), f32),
            jax.ShapeDtypeStruct((8, width), f32),
            jax.ShapeDtypeStruct((8, rows, width), bf16),
        ),
        in_specs=[WHOLE] * 5 + [ANY, ANY],
        out_specs=(WHOLE, WHOLE, ANY),
        scratch_shapes=gather_scratch(rows, width) + reduce_scratch(rows, width),
        compiler_params=params(cid),
        cost_estimate=cost(90),
        name="make_back_middle",
    )(low, weight, middle, back_out, small, after, more)


def phase_one(me, values, by_x, by_y, by_sib, send, recv):
    copies = []
    for k, value in enumerate(values):
        for i, (goal, mask) in enumerate(((by_x, 2), (by_y, 4), (by_sib, 1))):
            n = 3 * k + i
            copies.append(push(value, goal[k], send.at[n], recv.at[n], flip(me, mask)))
    for c in copies:
        c.start()
    return copies


def phase_two(me, by_x, by_y, low, high, sib_x, sib_y, send, recv):
    copies = []
    for k in range(len(by_x)):
        half = by_x[k].shape[0] // 2
        for i, (source, goal, mask) in enumerate(
            (
                (by_x[k].at[pl.ds(0, half)], low[k], 4),
                (by_y[k].at[pl.ds(half, half)], high[k], 2),
                (by_x[k], sib_x[k], 1),
                (by_y[k], sib_y[k], 1),
            )
        ):
            n = 4 * k + i
            copies.append(push(source, goal, send.at[n], recv.at[n], flip(me, mask)))
    for c in copies:
        c.start()
    return copies


def phase_three(me, low, high, sib_low, sib_high, send, recv):
    copies = []
    for k in range(len(low)):
        for i, (source, goal) in enumerate(((low[k], sib_low[k]), (high[k], sib_high[k]))):
            n = 2 * k + i
            copies.append(push(source, goal, send.at[n], recv.at[n], flip(me, 1)))
    for c in copies:
        c.start()
    return copies


def pair(count):
    return [pltpu.SemaphoreType.DMA((count,)), pltpu.SemaphoreType.DMA((count,))]


def same(values, halves=False):
    return [
        jax.ShapeDtypeStruct((v.shape[0] // 2 if halves else v.shape[0], v.shape[1]), v.dtype)
        for v in values
    ]


def back_input_kernel(count, low, weight, x, back_middle, small, *refs):
    values = refs[:count]
    out, parts = refs[count : count + 2]
    by = refs[count + 2 : 4 * count + 2]
    send, recv = refs[4 * count + 2 : 4 * count + 4]
    scratch = refs[4 * count + 4 :]
    me = greet()
    copies = phase_one(
        me, values, by[:count], by[count : 2 * count], by[2 * count :], send, recv
    )
    reduce_steps(me, [(low, weight)], True, *scratch)
    final, total = scratch[4], scratch[5]
    parts[...] = jnp.zeros_like(parts)

    @by_rows(x.shape[0])
    def _(at):
        back = summed(total, final, at)
        unit, root = centre(x[at, :].astype(f32), layer_epsilon)
        parts[0:1, :] += jnp.sum(back * unit, axis=0, keepdims=True)
        parts[1:2, :] += jnp.sum(back, axis=0, keepdims=True)
        value = back_middle[at, :] + through_norm(back * small[0:1, :], unit, root)
        out[at, :] = value.astype(bf16)

    for c in copies:
        c.wait()


def make_back_input(low, weight, x, back_middle, small, values, cid):
    rows, width = x.shape
    count = len(values)
    out = pl.pallas_call(
        functools.partial(back_input_kernel, count),
        out_shape=[
            jax.ShapeDtypeStruct((rows, width), bf16),
            jax.ShapeDtypeStruct((8, width), f32),
        ]
        + same(values) * 3,
        in_specs=[WHOLE] * 5 + [ANY] * count,
        out_specs=[WHOLE] * 2 + [ANY] * (3 * count),
        scratch_shapes=pair(3 * count) + reduce_scratch(rows, width),
        compiler_params=params(cid),
        cost_estimate=cost(80),
        name="make_back_input",
    )(low, weight, x, back_middle, small, *values)
    by = out[2:]
    return out[0], out[1], by[:count], by[count : 2 * count], by[2 * count :]


def ending_kernel(count, hidden, weight, middle, usable, parts_one, parts_two, *refs):
    refs = list(refs)

    def take(n):
        got = refs[:n]
        del refs[:n]
        return got

    by_x, by_y, fresh = take(count), take(count), take(1)
    out, sums = take(2)
    low, high, sib_x, sib_y, sib_low, sib_high = (take(count) for _ in range(6))
    f_x, f_y, f_sib, f_low, f_high, f_sib_x, f_sib_y, f_sib_low, f_sib_high = (
        take(1) for _ in range(9)
    )
    parts, turned, far = take(3)
    send_s, recv_s, send_f, recv_f = take(4)
    two, three, one_f, two_f, three_f = (take(2) for _ in range(5))
    scratch = refs
    me = greet(True)
    z = lax.axis_index("shard")
    shards = lax.axis_size("shard")
    started = phase_one(me, fresh, f_x, f_y, f_sib, *one_f)
    parts[...] = jnp.zeros_like(parts)
    parts[0:2, :] = parts_one[0:2, :]
    parts[2:4, :] = parts_two[0:2, :]
    steps = [
        push(parts, turned.at[i], send_s.at[i], recv_s.at[i], flip(me, mask))
        for i, mask in enumerate((1, 2, 4))
    ]
    waiting = []

    def between():
        for i, c in enumerate(steps):
            c.start()
            c.wait()
            parts[...] += turned[i]
        part = parts.shape[1] // shards
        for k, other in enumerate(others()):
            c = pltpu.make_async_remote_copy(
                src_ref=parts.at[:, pl.ds(pl.multiple_of(other * part, part), part)],
                dst_ref=far.at[k],
                send_sem=send_f.at[k],
                recv_sem=recv_f.at[k],
                device_id={"shard": other},
                device_id_type=MESHID,
            )
            c.start()
            waiting.append(c)
        for c in started:
            c.wait()
        started.clear()
        started.extend(phase_two(me, f_x, f_y, f_low, f_high, f_sib_x, f_sib_y, *two_f))
        started.extend(phase_two(me, by_x, by_y, low, high, sib_x, sib_y, *two))

    reduce_steps(me, [(hidden, weight)], False, *scratch, between=between)
    final, total = scratch[4], scratch[5]

    @by_rows(middle.shape[0])
    def _(at):
        value = middle[at, :] + summed(total, final, at)
        out[at, :] = jnp.where(usable[at, :] > 0.5, value, 0.0).astype(bf16)

    for c in started:
        c.wait()
    last = phase_three(me, f_low, f_high, f_sib_low, f_sib_high, *three_f)
    last += phase_three(me, low, high, sib_low, sib_high, *three)
    part = parts.shape[1] // shards
    value = parts[:, pl.ds(pl.multiple_of(z * part, part), part)]
    for k, c in enumerate(waiting):
        c.wait()
        value = value + far[k]
    sums[...] = value
    for c in last:
        c.wait()


def make_ending(hidden, weight, middle, usable, parts_one, parts_two, by_x, by_y, fresh, cid):
    rows, width = middle.shape
    shards = lax.axis_size("shard")
    count = len(by_x)
    shapes = (
        [
            jax.ShapeDtypeStruct((rows, width), bf16),
            jax.ShapeDtypeStruct((8, width // shards), f32),
        ]
        + same(by_x, True) * 2
        + same(by_x) * 2
        + same(by_x, True) * 2
        + same([fresh]) * 3
        + same([fresh], True) * 2
        + same([fresh]) * 2
        + same([fresh], True) * 2
    )
    out = pl.pallas_call(
        functools.partial(ending_kernel, count),
        out_shape=shapes,
        in_specs=[WHOLE] * 6 + [ANY] * (2 * count + 1),
        out_specs=[WHOLE] * 2 + [ANY] * (len(shapes) - 2),
        scratch_shapes=[
            pltpu.VMEM((8, width), f32),
            pltpu.VMEM((3, 8, width), f32),
            pltpu.VMEM((shards - 1, 8, width // shards), f32),
        ]
        + pair(3)
        + pair(shards - 1)
        + pair(4 * count)
        + pair(2 * count)
        + pair(3)
        + pair(4)
        + pair(2)
        + reduce_scratch(rows, width),
        compiler_params=params(cid),
        cost_estimate=cost(75),
        name="make_ending",
    )(hidden, weight, middle, usable, parts_one, parts_two, *by_x, *by_y, fresh)
    rest = out[2:]
    groups = [rest[i * count : (i + 1) * count] for i in range(6)]
    f_x, f_y, f_sib, f_low, f_high, f_sib_x, f_sib_y, f_sib_low, f_sib_high = rest[6 * count :]
    whole = [fresh, f_x, f_y, f_low, f_high, f_sib, f_sib_x, f_sib_y, f_sib_low, f_sib_high]
    return out[0], out[1], groups, whole


MASKS = (0, 2, 4, 6, 6, 1, 3, 5, 7, 7)
WHEN = (2, 2, 2, 0, 1, 2, 2, 2, 0, 1)


def in_order(parts):
    value, by_x, by_y, low, high, sib, sib_x, sib_y, sib_low, sib_high = parts
    corner, sib_corner = jnp.concatenate([low, high]), jnp.concatenate([sib_low, sib_high])
    stacked = jnp.stack([value, sib, by_x, sib_x, by_y, sib_y, corner, sib_corner])
    return jnp.take(stacked, jnp.arange(8) ^ lax.axis_index("tp"), axis=0)


def widen_two_kernel(steps, shards, *refs):
    t = lax.axis_index("tp")
    late = (pl.program_id(0) >= steps // 2).astype(jnp.int32)
    seconds, downs, outs = refs[:10], refs[10:20], refs[20:30]
    gelu, up, down, out = refs[30:]
    unit = gelu.shape[1] // (8 * shards)

    def store(i):
        place = flip(t, MASKS[i])
        down[place] = downs[i][...].astype(f32)
        out[place] = outs[i][...].astype(f32)
        for z in range(shards):
            at = pl.ds(pl.multiple_of((8 * z + place) * unit, unit), unit)
            gelu[:, at] = seconds[i][:, z * unit : (z + 1) * unit].astype(f32)
            up[:, at] = seconds[i][:, (shards + z) * unit : (shards + z + 1) * unit].astype(f32)

    for i in range(10):
        if WHEN[i] == 2:
            store(i)
        else:

            @pl.when(late == WHEN[i])
            def _():
                store(i)


def widen_two(seconds, downs, outs, shards):
    rows, columns = seconds[0].shape
    count, width = downs[0].shape
    steps = 4

    def row_at(which, i):
        half = steps // 2
        return (i, jnp.minimum(i, half - 1), jnp.maximum(i - half, 0))[(which + 1) % 3]

    def specs(parts):
        return [
            pl.BlockSpec(
                (parts[0].shape[0] // steps, parts[0].shape[1]),
                functools.partial(lambda w, i: (row_at(w, i), 0), w),
            )
            for w in WHEN
        ]

    units = jax.ShapeDtypeStruct((rows, 4 * columns), f32)
    stack = jax.ShapeDtypeStruct((8, count, width), f32)
    gelu, up, down, out = pl.pallas_call(
        functools.partial(widen_two_kernel, steps, shards),
        grid=(steps,),
        in_specs=specs(seconds) + specs(downs) + specs(outs),
        out_specs=[pl.BlockSpec((rows // steps, 4 * columns), lambda i: (i, 0))] * 2
        + [pl.BlockSpec((8, count // steps, width), lambda i: (0, i, 0))] * 2,
        out_shape=[units, units, stack, stack],
        compiler_params=params(),
        cost_estimate=cost(25),
        name="widen_two",
    )(*seconds, *downs, *outs)
    return gelu, up, down.reshape(8 * count, width), out.reshape(8 * count, width)


def widen_one_kernel(edges, parts, _after, *goals):
    for goal, (begin, end) in zip(goals, zip(edges, edges[1:])):
        size = end - begin
        for i in range(8):
            goal[:, i * size : (i + 1) * size] = parts[i, :, begin:end].astype(f32)


def widen_one(parts, edges, after):
    _, rows, columns = parts.shape
    sizes = [b - a for a, b in zip(edges, edges[1:])]
    block = 64
    return pl.pallas_call(
        functools.partial(widen_one_kernel, edges),
        grid=(rows // block,),
        in_specs=[pl.BlockSpec((8, block, columns), lambda i: (0, i, 0)), ANY],
        out_specs=[pl.BlockSpec((block, 8 * size), lambda i: (i, 0)) for size in sizes],
        out_shape=[jax.ShapeDtypeStruct((rows, 8 * size), f32) for size in sizes],
        compiler_params=params(),
        cost_estimate=cost(14),
        name="widen_one",
    )(parts, after)


def local(
    tokens,
    cotangent,
    token_order,
    lengths,
    query_weight,
    key_weight,
    value_weight,
    gate_weight,
    out_weight,
    gelu_weight,
    up_weight,
    down_weight,
    gain_one,
    shift_one,
    gain_two,
    shift_two,
):
    every = ("outer", "tp", "shard")
    device_count = lax.axis_size(every)
    device_index = lax.axis_index(every)
    outer, tp, shards = lax.axis_size("outer"), lax.axis_size("tp"), lax.axis_size("shard")
    t, z = lax.axis_index("tp"), lax.axis_index("shard")
    rows, width = tokens.shape
    packs = lengths.shape[0]
    pack_rows = rows // packs
    group_rows = tp * rows
    group_packs = tp * packs

    own_order = lax.dynamic_slice_in_dim(token_order, device_index * rows, rows)
    target = own_order // rows
    places = jnp.arange(rows, dtype=jnp.int32)
    before = (target[None, :] < target[:, None]) | (
        (target[None, :] == target[:, None]) & (places[None, :] < places[:, None])
    )
    send_place = jnp.sum(before.astype(jnp.int32), axis=1)
    send_mix = (send_place[None, :] == places[:, None]).astype(bf16)
    loader_ids = jnp.arange(token_order.shape[0], dtype=jnp.int32)
    slot_targets = device_index * rows + places
    origin = jnp.sum(
        jnp.where(token_order[None, :] == slot_targets[:, None], loader_ids[None, :], 0), axis=1
    )
    arrive_place = jnp.sum((origin[None, :] < origin[:, None]).astype(jnp.int32), axis=1)
    work_mix = (arrive_place[:, None] == places[None, :]).astype(bf16)

    def exchange(value):
        return lax.all_to_all(
            value.reshape(device_count, rows // device_count, width),
            every,
            split_axis=0,
            concat_axis=0,
            tiled=True,
        ).reshape(rows, width)

    def along_z(piece):
        return lax.all_gather(piece, "shard", axis=0, tiled=True)

    def cut(weight):
        part = weight.shape[1] // tp
        return lax.dynamic_slice_in_dim(weight, t * part, part, axis=1)

    out_unit = out_weight.shape[0] // tp
    unit = down_weight.shape[0] // tp
    piece_rows = query_weight.shape[0]
    key_part, value_part = query_weight.shape[1] // tp, value_weight.shape[1] // tp
    edges = (0, key_part, 2 * key_part, 2 * key_part + value_part)
    first_size = 2 * key_part + 2 * value_part
    hidden_part = shards * unit

    def fold(value):
        cuts = piece_rows // value.shape[0]
        value = value.reshape(value.shape[0], cuts, width // cuts)
        return jnp.transpose(value, (1, 0, 2)).reshape(piece_rows, width // cuts)

    def unfold(value, count):
        cuts = piece_rows // count
        value = value.reshape(shards, cuts, count, width // cuts)
        return jnp.transpose(value, (0, 2, 1, 3)).reshape(shards, count, width)

    out_piece = lax.dynamic_slice_in_dim(out_weight, t * out_unit, out_unit, axis=0)
    w_one = along_z(
        jnp.concatenate(
            [cut(w) for w in (query_weight, key_weight, value_weight, gate_weight)]
            + [fold(out_piece)],
            axis=1,
        )
    )
    ends = jnp.cumsum(lengths, axis=1, dtype=jnp.int32)[:, -2]
    usable = (jnp.arange(pack_rows, dtype=jnp.int32)[None, :] < ends[:, None]).astype(f32)
    usable = usable.reshape(rows, 1)
    lens = jnp.pad(lengths, ((0, 8 - packs), (0, 128 - lengths.shape[1])))
    came = exchange(forward_dot(send_mix, tokens).astype(bf16))
    came_back = exchange(forward_dot(send_mix, cotangent).astype(bf16))
    gains = jnp.stack([gain_one, shift_one, gain_two, shift_two]).astype(f32)
    gains = jnp.concatenate([gains, jnp.zeros_like(gains)], axis=0)
    x, normed, all_lengths, small = entry(came, work_mix, gains, lens, 0)
    t_late = t + jnp.minimum(all_lengths[0, 0, 0], 0)

    def unit_columns(weight):
        split = weight.reshape(weight.shape[0], shards, tp, unit)
        split = lax.dynamic_slice_in_dim(split, t_late, 1, axis=2)
        return split.reshape(weight.shape[0], hidden_part)

    down_piece = lax.dynamic_slice_in_dim(down_weight, t_late * unit, unit, axis=0)
    w_two = along_z(
        jnp.concatenate(
            [unit_columns(gelu_weight), unit_columns(up_weight), fold(down_piece)], axis=1
        )
    )
    back_out, back_low = entry_back(came_back, work_mix, usable, x, 7)
    normed, back_low = normed.reshape(group_rows, width), back_low.reshape(group_rows, width)
    all_lengths = all_lengths[:, :packs, : lengths.shape[1]].reshape(group_packs, -1)
    cosine, sine, decays, _ = pack_tables(all_lengths, pack_rows, t + jnp.arange(1))
    cosine, sine = cosine.reshape(group_rows, -1), sine.reshape(group_rows, -1)
    decays = decays[0]
    out_pieces = unfold(w_one[:, first_size:], out_unit)
    q_rot, k_rot, v_low, weights_low, gating, retained, branch, wo = retain(
        normed, w_one, value_part, cosine, sine, decays, out_pieces, rows, 1
    )
    wo = wo.reshape(shards * out_unit, width)
    middle, normed_two = make_middle(branch, wo, x, small, 2)
    normed_two = normed_two.reshape(group_rows, width)

    hidden, second_low, w_down = feed(normed_two, back_low, w_two, hidden_part, shards, rows)
    down_gram = gram_rows(hidden, back_low).astype(bf16)
    second_gram = gram_rows(normed_two, second_low).astype(bf16)

    def to_owner(value):
        part = lax.psum_scatter(value, "shard", scatter_dimension=0, tiled=True)
        return lax.psum(part, "outer") if outer > 1 else part

    down_sum, second_sum = to_owner(down_gram), to_owner(second_gram)
    back_middle, parts_two, middle_low = make_back_middle(
        second_low, w_two, middle, back_out, small, down_gram, second_gram, 3
    )
    middle_low = middle_low.reshape(group_rows, width)
    out_gram = gram_rows(branch, middle_low).astype(bf16).reshape(shards, out_unit, width)
    first_low, dealt = retain_back(
        middle_low, wo, q_rot, k_rot, v_low, weights_low, gating, retained, cosine, sine, decays,
        out_gram, rows, 8,
    )
    out_sum = to_owner(dealt.reshape(shards * out_unit, width))
    first_gram = gram_rows(normed, first_low).astype(bf16)
    first_gram, second_sum, down_sum = lax.optimization_barrier((first_gram, second_sum, down_sum))
    first_sum = to_owner(first_gram)
    values = [second_sum, down_sum]
    back_inputs, parts_one, by_x, by_y, by_sib = make_back_input(
        first_low, w_one, x, back_middle, small, values, 4
    )
    ending, sums, groups, outs = make_ending(
        hidden, w_down, middle, usable, parts_one, parts_two, by_x, by_y, out_sum, 5
    )
    low, high, sib_x, sib_y, sib_low, sib_high = groups
    seconds, downs = (
        [
            values[k], by_x[k], by_y[k], low[k], high[k],
            by_sib[k], sib_x[k], sib_y[k], sib_low[k], sib_high[k],
        ]
        for k in range(2)
    )

    if unit % 128 == 0:
        gelu_gradient, up_gradient, down_gradient, out_gradient = widen_two(
            seconds, downs, outs, shards
        )
    else:
        down_gradient = in_order(downs).reshape(-1, width).astype(f32)
        out_gradient = in_order(outs).reshape(-1, width).astype(f32)
        both = in_order(seconds).reshape(tp, piece_rows, 2, shards, unit)
        both = jnp.transpose(both, (2, 1, 3, 0, 4)).reshape(2, piece_rows, -1).astype(f32)
        gelu_gradient, up_gradient = both[0], both[1]
    firsts = lax.all_gather(first_sum + sums[5, 0].astype(bf16), "tp", axis=0)
    query_gradient, key_gradient, value_gradient, gate_gradient = widen_one(
        firsts, edges + (first_size,), down_gradient
    )
    smalls = lax.psum(sums, "outer") if outer > 1 else sums

    def give_back(value):
        home = exchange(gram_rows(work_mix, value).astype(bf16))
        return gram_rows(send_mix, home).astype(bf16)

    result = give_back(ending)
    token_gradient = give_back(back_inputs)
    return (
        result,
        token_gradient,
        query_gradient,
        key_gradient,
        value_gradient,
        gate_gradient,
        out_gradient,
        gelu_gradient,
        up_gradient,
        down_gradient,
        smalls[0],
        smalls[1],
        smalls[2],
        smalls[3],
    )


def solution(mesh):
    tp = math.gcd(mesh.shape["rep"], HEADS)
    grid = mesh.devices.reshape(mesh.shape["rep"] // tp, tp, mesh.shape["shard"])
    cube = Mesh(grid, ("outer", "tp", "shard"))
    tokens_at = P(("outer", "tp", "shard"), None)
    weights_at = P("shard", None)
    vectors_at = P("shard")
    in_specs = (tokens_at, tokens_at, P(), tokens_at) + (weights_at,) * 8 + (vectors_at,) * 4
    out_specs = (tokens_at, tokens_at) + (weights_at,) * 8 + (vectors_at,) * 4
    return jax.shard_map(local, mesh=cube, in_specs=in_specs, out_specs=out_specs, check_vma=False)
```

```python
import functools
import math

import jax
import jax.numpy as jnp
from jax import lax
from jax.experimental import pallas as pl
from jax.experimental.pallas import tpu as pltpu
from jax.sharding import Mesh, PartitionSpec as P

HEADS = 8
KH = 256

layer_epsilon = 1e-05
head_epsilon = 1.0
rotary_base = 10000.0
bf16 = jnp.bfloat16
f32 = jnp.float32
MESHID = pl.DeviceIdType.MESH


def pack_tables(lengths, pack_rows, head_ids):
    entries = lengths.shape[1]
    slot_ids = jnp.arange(pack_rows, dtype=jnp.int32)
    seq_ends = jnp.cumsum(lengths, axis=1, dtype=jnp.int32)
    seq_starts = seq_ends - lengths
    segment = jnp.sum(
        (slot_ids[None, :, None] >= seq_ends[:, None, :]).astype(jnp.int32), axis=2, dtype=jnp.int32
    )
    owners = segment[:, :, None] == jnp.arange(entries, dtype=jnp.int32)[None, None, :]
    begins = jnp.sum(jnp.where(owners, seq_starts[:, None, :], 0), axis=2, dtype=jnp.int32)
    places = (slot_ids[None, :] - begins).astype(f32)
    usable = segment < entries - 1
    half_size = KH // 2
    frequency = jnp.power(
        f32(rotary_base), -jnp.arange(half_size, dtype=f32) / f32(half_size - 1)
    )
    angles = places[:, :, None] * frequency
    cosine_table = jnp.cos(angles)
    sine_table = jnp.sin(angles)
    lag_steps = slot_ids[:, None] - slot_ids[None, :]
    linked = (
        (segment[:, :, None] == segment[:, None, :])
        & (lag_steps[None] >= 0)
        & usable[:, None, :]
    )
    log_rates = jnp.log(1.0 - jnp.power(f32(2.0), -5.0 - head_ids.astype(f32)))
    powers = jnp.exp(log_rates[:, None, None] * jnp.maximum(lag_steps, 0).astype(f32)[None])
    decays = jnp.where(linked[None], powers[:, None], f32(0.0))
    return cosine_table, sine_table, decays, usable


def gram_rows(leading, trailing):
    return lax.dot_general(
        leading, trailing, (((0,), (0,)), ((), ())), preferred_element_type=f32
    )


def back_through(incoming, matrix):
    return lax.dot_general(
        incoming, matrix, (((1,), (1,)), ((), ())), preferred_element_type=f32
    )


def forward_dot(inputs, matrix):
    return jnp.dot(inputs, matrix, preferred_element_type=f32)


def gelu_parts(v):
    c = f32(math.sqrt(2.0 / math.pi))
    t = jnp.tanh(c * (v + 0.044715 * v * v * v))
    value = 0.5 * v * (1.0 + t)
    slope = 0.5 * (1.0 + t) + 0.5 * v * (1.0 - t * t) * c * (1.0 + 3.0 * 0.044715 * v * v)
    return value, slope


def flip(me, mask):
    for bit in (1, 2, 4):
        if mask & bit:
            me = me + bit - 2 * bit * ((me // bit) % 2)
    return me


def greet(far=False):
    me = lax.axis_index("tp")
    barrier = pltpu.get_barrier_semaphore()
    for mask in (1, 2, 4):
        pl.semaphore_signal(
            barrier, inc=1, device_id={"tp": flip(me, mask)}, device_id_type=MESHID
        )
    count = 3
    if far:
        for other in others():
            pl.semaphore_signal(barrier, inc=1, device_id={"shard": other}, device_id_type=MESHID)
            count += 1
    pl.semaphore_wait(barrier, count)
    return me


def others():
    shards = lax.axis_size("shard")
    return [(lax.axis_index("shard") + k) % shards for k in range(1, shards)]


def push(source, goal, send, recv, peer):
    return pltpu.make_async_remote_copy(
        src_ref=source, dst_ref=goal, send_sem=send, recv_sem=recv,
        device_id={"tp": peer}, device_id_type=MESHID,
    )


def gather_begin(me, own, out, send, recv):
    half = own.shape[0] // 2
    xn, yn = flip(me, 2), flip(me, 4)
    low, high = pl.ds(0, half), pl.ds(half, half)
    first = [
        push(own.at[part], out.at[me, part], send.at[i], recv.at[i], peer)
        for i, (part, peer) in enumerate(((low, xn), (high, yn), (high, xn), (low, yn)))
    ]
    first.append(push(own, out.at[me], send.at[4], recv.at[4], flip(me, 1)))
    for c in first:
        c.start()
    return first


def gather_end(me, own, out, send, recv, first):
    half = own.shape[0] // 2
    sib, xn, yn, dn = flip(me, 1), flip(me, 2), flip(me, 4), flip(me, 6)
    low, high = pl.ds(0, half), pl.ds(half, half)
    started = list(first)

    def on(slot, part, peer):
        i = len(started)
        place = out.at[slot, part]
        c = push(place, place, send.at[i], recv.at[i], peer)
        c.start()
        started.append(c)
        return c

    first[0].wait_recv()
    d_low = on(xn, low, yn)
    first[1].wait_recv()
    d_high = on(yn, high, xn)
    on(xn, low, sib)
    on(yn, high, sib)
    first[2].wait_recv()
    on(xn, high, sib)
    first[3].wait_recv()
    on(yn, low, sib)
    d_low.wait_recv()
    on(dn, low, sib)
    d_high.wait_recv()
    on(dn, high, sib)
    for i in (4, 7, 8, 9, 10, 11, 12):
        started[i].wait_recv()
    for c in started:
        c.wait_send()


def gather_steps(me, own, out, send, recv):
    gather_end(me, own, out, send, recv, gather_begin(me, own, out, send, recv))


COLS = 512


def reduce_steps(me, pairs, transposed, tosib, fromsib, hold, hop, final, total, send, recv, hooks=()):
    rows, width = total.shape
    half = rows // 2
    sib, xn, yn = flip(me, 1), flip(me, 2), flip(me, 4)
    low, high = pl.ds(0, half), pl.ds(half, half)

    def product(block, tile):
        acc = None
        for act, weight in pairs:
            left = act[pl.ds(pl.multiple_of(block * rows, rows), rows), :]
            if transposed:
                part = lax.dot_general(
                    left, weight[pl.ds(pl.multiple_of(tile * COLS, COLS), COLS), 0 : act.shape[1]],
                    (((1,), (1,)), ((), ())), preferred_element_type=f32,
                )
            else:
                part = jnp.dot(
                    left, weight[:, pl.ds(pl.multiple_of(tile * COLS, COLS), COLS)],
                    preferred_element_type=f32,
                )
            acc = part if acc is None else acc + part
        return acc

    def cp(i, src, goal, peer):
        return push(src, goal, send.at[i], recv.at[i], peer)

    masks = (6, 2, 4, 0)
    over, out = [], {}

    def for_sibling(slot):
        block = flip(me, masks[slot] ^ 1)

        @pl.loop(0, width // COLS)
        def _(tile):
            at = pl.ds(pl.multiple_of(tile * COLS, COLS), COLS)
            tosib[slot, :, at] = product(block, tile).astype(bf16)

        c = cp(slot, tosib.at[slot], fromsib.at[slot], sib)
        c.start()
        over.append(c)

    def for_own_core(slot):
        block = flip(me, masks[slot])
        over[slot].wait_recv()

        @pl.loop(0, width // COLS)
        def _(tile):
            at = pl.ds(pl.multiple_of(tile * COLS, COLS), COLS)
            value = product(block, tile) + fromsib[slot, :, at].astype(f32)
            if slot < 3:
                hold[slot, :, at] = value.astype(bf16)
            else:
                total[:, at] = value

    def hook(i):
        if hooks:
            hooks[i]()

    for_sibling(0)
    for_sibling(1)
    for_own_core(0)
    dx = cp(4, hold.at[0, low], hop.at[0], xn)
    dy = cp(5, hold.at[0, high], hop.at[1], yn)
    dx.start()
    dy.start()
    hook(0)
    for_sibling(2)
    for_own_core(1)
    xa = cp(6, hold.at[1, low], final.at[0, low], xn)
    xa.start()
    for_sibling(3)
    for_own_core(2)
    yb = cp(7, hold.at[2, high], final.at[1, high], yn)
    yb.start()
    for_own_core(3)
    hook(1)
    dy.wait_recv()
    hold[1, high] = (hold[1, high].astype(f32) + hop[1].astype(f32)).astype(bf16)
    xb = cp(8, hold.at[1, high], final.at[0, high], xn)
    xb.start()
    dx.wait_recv()
    hold[2, low] = (hold[2, low].astype(f32) + hop[0].astype(f32)).astype(bf16)
    ya = cp(9, hold.at[2, low], final.at[1, low], yn)
    ya.start()
    hook(2)
    xa.wait_recv()
    yb.wait_recv()
    xb.wait_recv()
    ya.wait_recv()
    for c in over + [dx, dy, xa, yb, xb, ya]:
        c.wait_send()


def summed(total, final, at):
    return total[at, :] + final[0, at, :].astype(f32) + final[1, at, :].astype(f32)


def reduce_scratch(rows, width):
    return [
        pltpu.VMEM((4, rows, width), bf16),
        pltpu.VMEM((4, rows, width), bf16),
        pltpu.VMEM((3, rows, width), bf16),
        pltpu.VMEM((2, rows // 2, width), bf16),
        pltpu.VMEM((2, rows, width), bf16),
        pltpu.VMEM((rows, width), f32),
        pltpu.SemaphoreType.DMA((10,)),
        pltpu.SemaphoreType.DMA((10,)),
    ]


CHUNK = 32


def cost(us):
    return pl.CostEstimate(flops=int(us * 1e9), bytes_accessed=int(us * 3e6), transcendentals=0)


def params(cid=None):
    if cid is None:
        return pltpu.CompilerParams(vmem_limit_bytes=60 << 20)
    return pltpu.CompilerParams(collective_id=cid, has_side_effects=True, vmem_limit_bytes=60 << 20)


def by_rows(count):
    def run(body):
        @pl.loop(0, count // CHUNK)
        def _(i):
            body(pl.ds(pl.multiple_of(i * CHUNK, CHUNK), CHUNK))

    return run


def centre(value, epsilon):
    average = jnp.mean(value, axis=-1, keepdims=True)
    centred = value - average
    spread = jnp.mean(centred * centred, axis=-1, keepdims=True)
    root = lax.rsqrt(spread + epsilon)
    return centred * root, root


def through_norm(e, unit, root):
    return root * (
        e - jnp.mean(e, axis=-1, keepdims=True) - unit * jnp.mean(e * unit, axis=-1, keepdims=True)
    )


def leading(rows, columns):
    return pl.BlockSpec((rows, columns), lambda *_: (0, 0))


ANY = pl.BlockSpec(memory_space=pl.ANY)
WHOLE = pl.BlockSpec(memory_space=pltpu.VMEM)


def gather_scratch(rows, width):
    return [
        pltpu.VMEM((rows, width), bf16),
        pltpu.SemaphoreType.DMA((13,)),
        pltpu.SemaphoreType.DMA((13,)),
        pltpu.SemaphoreType.DMA,
    ]


def gather_all(me, own, out, send, recv, local_sem):
    mine = pltpu.make_async_copy(own, out.at[me], local_sem)
    mine.start()
    gather_steps(me, own, out, send, recv)
    mine.wait()


def entry_kernel(came, mix, small, x_out, normed_all, own, send, recv, sem):
    me = greet()
    width = x_out.shape[1]

    @by_rows(came.shape[0])
    def _(at):
        value = jnp.dot(mix[at, :], came[:, :width], preferred_element_type=f32)
        x_out[at, :] = value.astype(bf16)
        unit, _ = centre(value, layer_epsilon)
        own[at, :] = (unit * small[0:1, :] + small[1:2, :]).astype(bf16)

    gather_all(me, own, normed_all, send, recv, sem)


def entry(came, mix, small, cid):
    rows, width = came.shape[0], small.shape[1]
    return pl.pallas_call(
        entry_kernel,
        out_shape=(
            jax.ShapeDtypeStruct((rows, width), bf16),
            jax.ShapeDtypeStruct((8, rows, width), bf16),
        ),
        in_specs=[WHOLE] * 3,
        out_specs=(WHOLE, ANY),
        scratch_shapes=gather_scratch(rows, width),
        compiler_params=params(cid),
        cost_estimate=cost(50),
        name="entry",
    )(came, mix, small)


def entry_back_kernel(came, mix, usable, _after, back_out, back_all, own, send, recv, sem):
    me = greet()

    @by_rows(came.shape[0])
    def _(at):
        value = jnp.dot(mix[at, :], came[...], preferred_element_type=f32)
        value = jnp.where(usable[at, :] > 0.5, value, 0.0).astype(bf16)
        back_out[at, :] = value
        own[at, :] = value

    gather_all(me, own, back_all, send, recv, sem)


def entry_back(came, mix, usable, after, cid):
    rows, width = came.shape
    return pl.pallas_call(
        entry_back_kernel,
        out_shape=(
            jax.ShapeDtypeStruct((rows, width), bf16),
            jax.ShapeDtypeStruct((8, rows, width), bf16),
        ),
        in_specs=[WHOLE] * 3 + [ANY],
        out_specs=(WHOLE, ANY),
        scratch_shapes=gather_scratch(rows, width),
        compiler_params=params(cid),
        cost_estimate=cost(45),
        name="entry_back",
    )(came, mix, usable, after)


def deal_plan(back, count):
    heads = HEADS // count
    me = lax.axis_index("tp")
    spread = [i * heads + me // count for i in range(count)]
    packed = [(me % heads) * count + i for i in range(count)]
    goals, sources = (packed, spread) if back else (spread, packed)
    return me, goals, sources, (me // heads if back else me % count), me // count == me % heads


def deal_start(back, count, source, goal, send, recv, local_sem):
    me, goals, sources, slot, inside = deal_plan(back, count)
    barrier = pltpu.get_barrier_semaphore()
    for i in range(count):

        @pl.when(sources[i] != me)
        def _():
            pl.semaphore_signal(
                barrier, inc=1, device_id={"tp": sources[i]}, device_id_type=MESHID
            )

    pl.semaphore_wait(barrier, jnp.where(inside, count - 1, count))
    for i in range(count):

        @pl.when(goals[i] == me)
        def _():
            pltpu.make_async_copy(source(i), goal(slot), local_sem).start()

        @pl.when(goals[i] != me)
        def _():
            push(source(i), goal(slot), send.at[i], recv.at[slot], goals[i]).start()


def deal_wait(back, count, source, goal, send, recv, local_sem):
    me, goals, sources, slot, _ = deal_plan(back, count)
    for i in range(count):

        @pl.when(goals[i] == me)
        def _():
            pltpu.make_async_copy(source(i), goal(slot), local_sem).wait()

        @pl.when(goals[i] != me)
        def _():
            push(source(i), goal(slot), send.at[i], recv.at[slot], goals[i]).wait_send()

        @pl.when(sources[i] != me)
        def _():
            push(source(i), goal(i), send.at[i], recv.at[i], sources[i]).wait_recv()


def blocks(ref):
    return lambda i: ref.at[i]


def column_blocks(ref, size):
    return lambda i: ref.at[:, pl.ds(pl.multiple_of(i * size, size), size)]


def deal_scratch(count):
    return [
        pltpu.SemaphoreType.DMA((count,)),
        pltpu.SemaphoreType.DMA((count,)),
        pltpu.SemaphoreType.DMA,
    ]


def phase_one_copies(me, values, by_x, by_y, by_sib, send, recv):
    copies = []
    for k, value in enumerate(values):
        for i, (goal, mask) in enumerate(((by_x, 2), (by_y, 4), (by_sib, 1))):
            n = 3 * k + i
            copies.append(push(value, goal[k], send.at[n], recv.at[n], flip(me, mask)))
    return copies


def phase_one(*args):
    copies = phase_one_copies(*args)
    for c in copies:
        c.start()
    return copies


def phase_two(me, by_x, by_y, low, high, sib_x, sib_y, send, recv):
    copies = []
    for k in range(len(by_x)):
        half = by_x[k].shape[0] // 2
        for i, (source, goal, mask) in enumerate(
            (
                (by_x[k].at[pl.ds(0, half)], low[k], 4),
                (by_y[k].at[pl.ds(half, half)], high[k], 2),
                (by_x[k], sib_x[k], 1),
                (by_y[k], sib_y[k], 1),
            )
        ):
            n = 4 * k + i
            copies.append(push(source, goal, send.at[n], recv.at[n], flip(me, mask)))
    for c in copies:
        c.start()
    return copies


def phase_three(me, low, high, sib_low, sib_high, send, recv):
    copies = []
    for k in range(len(low)):
        for i, (source, goal) in enumerate(((low[k], sib_low[k]), (high[k], sib_high[k]))):
            n = 2 * k + i
            copies.append(push(source, goal, send.at[n], recv.at[n], flip(me, 1)))
    for c in copies:
        c.start()
    return copies


def pair(count):
    return [pltpu.SemaphoreType.DMA((count,)), pltpu.SemaphoreType.DMA((count,))]


def same(values, halves=False):
    return [
        jax.ShapeDtypeStruct((v.shape[0] // 2 if halves else v.shape[0], v.shape[1]), v.dtype)
        for v in values
    ]


def turn(value, cosine, sine):
    half = value.shape[-1] // 2
    a, b = value[:, :half], value[:, half:]
    return jnp.concatenate([a * cosine - b * sine, a * sine + b * cosine], axis=1)


def retain_kernel(
    normed, weight, cosine, sine, decays, pieces,
    q_out, k_out, v_out, w_out, g_out, r_out, branch, wo, *sems
):
    @pl.when(pl.program_id(0) == 0)
    def _():
        deal_start(False, pieces.shape[0], blocks(pieces), blocks(wo), *sems)

    packs, span = decays.shape[0], decays.shape[1]
    value_at = 2 * KH
    gate_at = value_at + v_out.shape[1]
    rows = normed[...]

    def project(begin, size):
        return jnp.dot(rows, weight[:, begin : begin + size], preferred_element_type=f32)

    q_out[...] = turn(project(0, KH), cosine[...], sine[...]).astype(bf16)
    k_out[...] = (turn(project(KH, KH), cosine[...], sine[...]) * KH ** (-0.5)).astype(bf16)
    v_out[...] = project(value_at, v_out.shape[1]).astype(bf16)
    g_out[...] = project(gate_at, g_out.shape[1])
    for p in range(packs):
        at = pl.ds(p * span, span)
        scores = lax.dot_general(
            q_out[at, :], k_out[at, :], (((1,), (1,)), ((), ())), preferred_element_type=f32
        )
        low = (scores * decays[p]).astype(bf16)
        w_out[p] = low
        retained = jnp.dot(low, v_out[at, :], preferred_element_type=f32)
        r_out[at, :] = retained
        unit, _ = centre(retained, head_epsilon)
        gating = g_out[at, :]
        branch[at, :] = (gating * jax.nn.sigmoid(gating) * unit).astype(bf16)

    @pl.when(pl.program_id(0) == pl.num_programs(0) - 1)
    def _():
        deal_wait(False, pieces.shape[0], blocks(pieces), blocks(wo), *sems)


def retain(normed, weight, value_size, cosine, sine, decays, pieces, block, cid):
    total, width = normed.shape
    span = decays.shape[1]
    grid = total // block
    row = lambda w: pl.BlockSpec((block, w), lambda i: (i, 0))
    square = pl.BlockSpec((block // span, span, span), lambda i: (i, 0, 0))
    flat = lambda w, kind: jax.ShapeDtypeStruct((total, w), kind)
    return pl.pallas_call(
        retain_kernel,
        grid=(grid,),
        in_specs=[
            row(width), leading(width, 2 * KH + 2 * value_size), row(KH // 2), row(KH // 2), square,
            ANY,
        ],
        out_specs=(
            row(KH), row(KH), row(value_size), square, row(value_size), row(value_size),
            row(value_size), ANY,
        ),
        out_shape=(
            flat(KH, bf16), flat(KH, bf16), flat(value_size, bf16),
            jax.ShapeDtypeStruct(decays.shape, bf16), flat(value_size, f32),
            flat(value_size, f32), flat(value_size, bf16),
            jax.ShapeDtypeStruct(pieces.shape, bf16),
        ),
        scratch_shapes=deal_scratch(pieces.shape[0]),
        compiler_params=params(cid),
        cost_estimate=cost(24),
        name="retain",
    )(normed, weight, cosine, sine, decays, pieces)


def phase_one_of(value, by, sems):
    return phase_one_copies(lax.axis_index("tp"), [value], by[:1], by[1:2], by[2:], *sems)


def retain_back_kernel(
    middle_low, wo, q_in, k_in, v_in, w_in, g_in, r_in, cosine, sine, decays, value,
    low, by_x, by_y, by_sib, *sems
):
    by = (by_x, by_y, by_sib)

    @pl.when(pl.program_id(0) == 0)
    def _():
        greet()
        for c in phase_one_of(value, by, sems):
            c.start()

    packs, span = decays.shape[0], decays.shape[1]
    value_at = 2 * KH
    value_size = v_in.shape[1]
    gate_at = value_at + value_size
    back_branch = lax.dot_general(
        middle_low[...], wo[...], (((1,), (1,)), ((), ())), preferred_element_type=f32
    )
    cols = (((0,), (0,)), ((), ()))
    last = (((1,), (1,)), ((), ()))
    for p in range(packs):
        at = pl.ds(p * span, span)
        bb = back_branch[p * span : (p + 1) * span]
        unit, root = centre(r_in[at, :], head_epsilon)
        gating = g_in[at, :]
        sigma = jax.nn.sigmoid(gating)
        low[at, gate_at:] = (bb * unit * (sigma * (1.0 + gating * (1.0 - sigma)))).astype(bf16)
        retained_low = through_norm(bb * (gating * sigma), unit, root).astype(bf16)
        back_weights = lax.dot_general(retained_low, v_in[at, :], last, preferred_element_type=f32)
        low[at, value_at:gate_at] = lax.dot_general(
            w_in[p], retained_low, cols, preferred_element_type=f32
        ).astype(bf16)
        back_scores = (back_weights * decays[p]).astype(bf16)
        back_q = jnp.dot(back_scores, k_in[at, :], preferred_element_type=f32)
        back_k = lax.dot_general(back_scores, q_in[at, :], cols, preferred_element_type=f32)
        low[at, :KH] = turn(back_q, cosine[at, :], -sine[at, :]).astype(bf16)
        low[at, KH:value_at] = (turn(back_k, cosine[at, :], -sine[at, :]) * KH ** (-0.5)).astype(bf16)

    @pl.when(pl.program_id(0) == pl.num_programs(0) - 1)
    def _():
        for c in phase_one_of(value, by, sems):
            c.wait()


def retain_back(middle_low, wo, q, k, v, w, g, r, cosine, sine, decays, value, block, cid):
    total, width = middle_low.shape
    span = decays.shape[1]
    value_size = v.shape[1]
    row = lambda w: pl.BlockSpec((block, w), lambda i: (i, 0))
    square = pl.BlockSpec((block // span, span, span), lambda i: (i, 0, 0))
    return pl.pallas_call(
        retain_back_kernel,
        grid=(total // block,),
        in_specs=[
            row(width), WHOLE, row(KH), row(KH), row(value_size), square, row(value_size),
            row(value_size), row(KH // 2), row(KH // 2), square, ANY,
        ],
        out_specs=[row(2 * KH + 2 * value_size)] + [ANY] * 3,
        out_shape=[
            jax.ShapeDtypeStruct((total, 2 * KH + 2 * value_size), bf16),
        ]
        + same([value]) * 3,
        scratch_shapes=pair(3),
        compiler_params=params(cid),
        cost_estimate=cost(20),
        name="retain_back",
    )(middle_low, wo, q, k, v, w, g, r, cosine, sine, decays, value)


def feed_kernel(shards, count, normed_two, back_low, w_two, branch, hidden, low, w_down, dealt, *sems):
    size = hidden.shape[1]
    views = (
        column_blocks(branch, branch.shape[1] // count) if count else None,
        column_blocks(dealt, branch.shape[1] // count) if count else None,
    )

    @pl.when(pl.program_id(0) == 0)
    def _():
        if count:
            deal_start(True, count, *views, *sems)
        unit = size // shards
        span = w_two.shape[0] // shards
        part = w_two.shape[1] - 2 * size
        for z in range(shards):
            for c in range(span // unit):
                begin = z * span + c * unit
                w_down[z * unit : (z + 1) * unit, c * part : (c + 1) * part] = w_two[
                    begin : begin + unit, 2 * size :
                ]

    both = jnp.dot(normed_two[...], w_two[:, : 2 * size], preferred_element_type=f32)
    back = lax.dot_general(
        back_low[...], w_down[...], (((1,), (1,)), ((), ())), preferred_element_type=f32
    )
    up = both[:, size:]
    value, slope = gelu_parts(both[:, :size])
    hidden[...] = (value * up).astype(bf16)
    low[:, :size] = (back * up * slope).astype(bf16)
    low[:, size:] = (back * value).astype(bf16)

    if count:

        @pl.when(pl.program_id(0) == pl.num_programs(0) - 1)
        def _():
            deal_wait(True, count, *views, *sems)


def feed(normed_two, back_low, w_two, branch, size, shards, block, cid):
    total, width = normed_two.shape
    row = lambda w: pl.BlockSpec((block, w), lambda i: (i, 0))
    count = shards if branch.shape[1] // shards % 128 == 0 else 0
    hidden, low, w_down, dealt = pl.pallas_call(
        functools.partial(feed_kernel, shards, count),
        grid=(total // block,),
        in_specs=[row(width), row(width), WHOLE, ANY],
        out_specs=(row(size), row(2 * size), pl.BlockSpec((size, width), lambda i: (0, 0)), ANY),
        out_shape=(
            jax.ShapeDtypeStruct((total, size), bf16),
            jax.ShapeDtypeStruct((total, 2 * size), bf16),
            jax.ShapeDtypeStruct((size, width), bf16),
            jax.ShapeDtypeStruct(branch.shape if count else (8, 128), bf16),
        ),
        scratch_shapes=deal_scratch(count) if count else [],
        compiler_params=params(cid if count else None),
        cost_estimate=cost(26),
        name="feed",
    )(normed_two, back_low, w_two, branch)
    if not count:
        pieces = jnp.transpose(branch.reshape(total, shards, -1), (1, 0, 2))
        pieces = lax.all_to_all(pieces, "tp", split_axis=0, concat_axis=0, tiled=True)
        dealt = jnp.transpose(pieces, (1, 0, 2)).reshape(total, -1)
    return hidden, low, w_down, dealt


def gram_kernel(left, right, value, out_a, out_b, by_x, by_y, by_sib, send, recv):
    by = (by_x, by_y, by_sib)

    @pl.when(pl.program_id(0) == 0)
    def _():
        greet()
        for c in phase_one_of(value, by, (send, recv)):
            c.start()

    both = lax.dot_general(
        left[...], right[...], (((0,), (0,)), ((), ())), preferred_element_type=f32
    ).astype(bf16)
    out_a[...] = both[:, : out_a.shape[1]]
    out_b[...] = both[:, out_a.shape[1] :]

    @pl.when(pl.program_id(0) == pl.num_programs(0) - 1)
    def _():
        for c in phase_one_of(value, by, (send, recv)):
            c.wait()


def gram_beside(left, right, value, first, block, cid):
    total, width = left.shape
    sizes = (first, right.shape[1] - first)
    return pl.pallas_call(
        gram_kernel,
        grid=(width // block,),
        in_specs=[pl.BlockSpec((total, block), lambda i: (0, i)), WHOLE, ANY],
        out_specs=[pl.BlockSpec((block, size), lambda i: (i, 0)) for size in sizes] + [ANY] * 3,
        out_shape=[jax.ShapeDtypeStruct((width, size), bf16) for size in sizes]
        + same([value]) * 3,
        scratch_shapes=pair(3),
        compiler_params=params(cid),
        cost_estimate=cost(28),
        name="gram_beside",
    )(left, right, value)


def middle_kernel(branch, wo, x, small, middle, normed_all, own, send1, recv1, sem1, *scratch):
    me = greet()
    reduce_steps(me, [(branch, wo)], False, *scratch)
    final, total = scratch[4], scratch[5]

    @by_rows(x.shape[0])
    def _(at):
        value = x[at, :].astype(f32) + summed(total, final, at)
        middle[at, :] = value
        unit, _ = centre(value, layer_epsilon)
        own[at, :] = (unit * small[2:3, :] + small[3:4, :]).astype(bf16)

    gather_all(me, own, normed_all, send1, recv1, sem1)


def make_middle(branch, wo, x, small, cid):
    rows, width = x.shape
    return pl.pallas_call(
        middle_kernel,
        out_shape=(
            jax.ShapeDtypeStruct((rows, width), f32),
            jax.ShapeDtypeStruct((8, rows, width), bf16),
        ),
        in_specs=[WHOLE] * 4,
        out_specs=(WHOLE, ANY),
        scratch_shapes=gather_scratch(rows, width) + reduce_scratch(rows, width),
        compiler_params=params(cid),
        cost_estimate=cost(85),
        name="make_middle",
    )(branch, wo, x, small)


def column_sums(out, row, value, first):
    total = jnp.sum(value, axis=0, keepdims=True)

    @pl.when(first)
    def _():
        out[row : row + 1, :] = total

    @pl.when(jnp.logical_not(first))
    def _():
        out[row : row + 1, :] += total


def back_middle_kernel(
    low, weight, middle, back_out, small, _after, _more, back_middle, parts, middle_all,
    own, send1, recv1, sem1, *scratch,
):
    me = greet()
    reduce_steps(me, [(low, weight)], True, *scratch)
    final, total = scratch[4], scratch[5]
    parts[...] = jnp.zeros_like(parts)

    @by_rows(middle.shape[0])
    def _(at):
        back = summed(total, final, at)
        unit, root = centre(middle[at, :], layer_epsilon)
        parts[0:1, :] += jnp.sum(back * unit, axis=0, keepdims=True)
        parts[1:2, :] += jnp.sum(back, axis=0, keepdims=True)
        value = back_out[at, :].astype(f32) + through_norm(back * small[2:3, :], unit, root)
        back_middle[at, :] = value
        own[at, :] = value.astype(bf16)

    gather_all(me, own, middle_all, send1, recv1, sem1)


def make_back_middle(low, weight, middle, back_out, small, after, more, cid):
    rows, width = middle.shape
    return pl.pallas_call(
        back_middle_kernel,
        out_shape=(
            jax.ShapeDtypeStruct((rows, width), f32),
            jax.ShapeDtypeStruct((8, width), f32),
            jax.ShapeDtypeStruct((8, rows, width), bf16),
        ),
        in_specs=[WHOLE] * 5 + [ANY, ANY],
        out_specs=(WHOLE, WHOLE, ANY),
        scratch_shapes=gather_scratch(rows, width) + reduce_scratch(rows, width),
        compiler_params=params(cid),
        cost_estimate=cost(90),
        name="make_back_middle",
    )(low, weight, middle, back_out, small, after, more)


def back_input_kernel(count, low, weight, x, back_middle, small, *refs):
    refs = list(refs)

    def take(n):
        got = refs[:n]
        del refs[:n]
        return got

    by_x, by_y = take(count), take(count)
    out, parts = take(2)
    half_low, half_high, sib_x, sib_y, sib_low, sib_high = (take(count) for _ in range(6))
    two, three = take(2), take(2)
    scratch = refs
    me = greet()
    started, last = [], []

    def early():
        started.extend(phase_two(me, by_x, by_y, half_low, half_high, sib_x, sib_y, *two))

    def late():
        for c in started:
            c.wait()
        last.extend(phase_three(me, half_low, half_high, sib_low, sib_high, *three))

    reduce_steps(me, [(low, weight)], True, *scratch, hooks=(early, lambda: None, late))
    final, total = scratch[4], scratch[5]
    parts[...] = jnp.zeros_like(parts)

    @by_rows(x.shape[0])
    def _(at):
        back = summed(total, final, at)
        unit, root = centre(x[at, :].astype(f32), layer_epsilon)
        parts[0:1, :] += jnp.sum(back * unit, axis=0, keepdims=True)
        parts[1:2, :] += jnp.sum(back, axis=0, keepdims=True)
        value = back_middle[at, :] + through_norm(back * small[0:1, :], unit, root)
        out[at, :] = value.astype(bf16)

    for c in last:
        c.wait()


def make_back_input(low, weight, x, back_middle, small, by_x, by_y, cid):
    rows, width = x.shape
    count = len(by_x)
    shapes = (
        [
            jax.ShapeDtypeStruct((rows, width), bf16),
            jax.ShapeDtypeStruct((8, width), f32),
        ]
        + same(by_x, True) * 2
        + same(by_x) * 2
        + same(by_x, True) * 2
    )
    out = pl.pallas_call(
        functools.partial(back_input_kernel, count),
        out_shape=shapes,
        in_specs=[WHOLE] * 5 + [ANY] * (2 * count),
        out_specs=[WHOLE] * 2 + [ANY] * (len(shapes) - 2),
        scratch_shapes=pair(4 * count) + pair(2 * count) + reduce_scratch(rows, width),
        compiler_params=params(cid),
        cost_estimate=cost(70),
        name="make_back_input",
    )(low, weight, x, back_middle, small, *by_x, *by_y)
    rest = out[2:]
    return out[0], out[1], [rest[i * count : (i + 1) * count] for i in range(6)]


def ending_kernel(count, hidden, weight, middle, usable, parts_one, parts_two, *refs):
    fresh, refs = refs[:count], refs[count:]
    out, sums = refs[:2]
    fresh_all, refs = refs[2 : 2 + count], refs[2 + count :]
    parts, turned, far, send_s, recv_s, send_f, recv_f = refs[:7]
    sems, scratch = [refs[7 + 3 * k : 10 + 3 * k] for k in range(count)], refs[7 + 3 * count :]
    me = greet(True)
    z = lax.axis_index("shard")
    shards = lax.axis_size("shard")
    parts[...] = jnp.zeros_like(parts)
    parts[0:2, :] = parts_one[0:2, :]
    parts[2:4, :] = parts_two[0:2, :]
    part = parts.shape[1] // shards
    turns = [
        push(parts, turned.at[i], send_s.at[i], recv_s.at[i], flip(me, mask))
        for i, mask in enumerate((1, 2, 4))
    ]
    mine = [pltpu.make_async_copy(a, b.at[me], s[2]) for a, b, s in zip(fresh, fresh_all, sems)]
    for c in mine:
        c.start()
    turns[0].start()
    started, waiting = [], []

    def add(i):
        turns[i].wait()
        parts[...] += turned[i]

    def early():
        add(0)
        turns[1].start()
        for a, b, s in zip(fresh, fresh_all, sems):
            started.append(gather_begin(me, a, b, s[0], s[1]))

    def between():
        add(1)
        turns[2].start()

    def late():
        add(2)
        for k, other in enumerate(others()):
            c = pltpu.make_async_remote_copy(
                src_ref=parts.at[:, pl.ds(pl.multiple_of(other * part, part), part)],
                dst_ref=far.at[k],
                send_sem=send_f.at[k],
                recv_sem=recv_f.at[k],
                device_id={"shard": other},
                device_id_type=MESHID,
            )
            c.start()
            waiting.append(c)
        for a, b, s, first in zip(fresh, fresh_all, sems, started):
            gather_end(me, a, b, s[0], s[1], first)

    reduce_steps(me, [(hidden, weight)], False, *scratch, hooks=(early, between, late))
    final, total = scratch[4], scratch[5]

    @by_rows(middle.shape[0])
    def _(at):
        value = middle[at, :] + summed(total, final, at)
        out[at, :] = jnp.where(usable[at, :] > 0.5, value, 0.0).astype(bf16)

    value = parts[:, pl.ds(pl.multiple_of(z * part, part), part)]
    for k, c in enumerate(waiting):
        c.wait()
        value = value + far[k]
    sums[...] = value
    for c in mine:
        c.wait()


def make_ending(hidden, weight, middle, usable, parts_one, parts_two, fresh, cid):
    rows, width = middle.shape
    shards = lax.axis_size("shard")
    count = len(fresh)
    out = pl.pallas_call(
        functools.partial(ending_kernel, count),
        out_shape=[
            jax.ShapeDtypeStruct((rows, width), bf16),
            jax.ShapeDtypeStruct((8, width // shards), f32),
        ]
        + [jax.ShapeDtypeStruct((8,) + a.shape, bf16) for a in fresh],
        in_specs=[WHOLE] * 6 + [ANY] * count,
        out_specs=[WHOLE, WHOLE] + [ANY] * count,
        scratch_shapes=[
            pltpu.VMEM((8, width), f32),
            pltpu.VMEM((3, 8, width), f32),
            pltpu.VMEM((shards - 1, 8, width // shards), f32),
        ]
        + pair(3)
        + pair(shards - 1)
        + gather_scratch(rows, width)[1:] * count
        + reduce_scratch(rows, width),
        compiler_params=params(cid),
        cost_estimate=cost(78),
        name="make_ending",
    )(hidden, weight, middle, usable, parts_one, parts_two, *fresh)
    return out[0], out[1], out[2:]


MASKS = (0, 2, 4, 6, 6, 1, 3, 5, 7, 7)
WHEN = (2, 2, 2, 0, 1, 2, 2, 2, 0, 1)


def in_order(parts):
    value, by_x, by_y, low, high, sib, sib_x, sib_y, sib_low, sib_high = parts
    corner, sib_corner = jnp.concatenate([low, high]), jnp.concatenate([sib_low, sib_high])
    stacked = jnp.stack([value, sib, by_x, sib_x, by_y, sib_y, corner, sib_corner])
    return jnp.take(stacked, jnp.arange(8) ^ lax.axis_index("tp"), axis=0)


def widen_two_kernel(steps, shards, *refs):
    t = lax.axis_index("tp")
    late = (pl.program_id(0) >= steps // 2).astype(jnp.int32)
    seconds, downs, outs = refs[:10], refs[10:20], refs[20]
    gelu, up, down, out = refs[21:]
    out[...] = outs[...].astype(f32)
    unit = gelu.shape[1] // (8 * shards)

    def store(i):
        place = flip(t, MASKS[i])
        down[place] = downs[i][...].astype(f32)
        for z in range(shards):
            at = pl.ds(pl.multiple_of((8 * z + place) * unit, unit), unit)
            gelu[:, at] = seconds[i][:, z * unit : (z + 1) * unit].astype(f32)
            up[:, at] = seconds[i][:, (shards + z) * unit : (shards + z + 1) * unit].astype(f32)

    for i in range(10):
        if WHEN[i] == 2:
            store(i)
        else:

            @pl.when(late == WHEN[i])
            def _():
                store(i)


def widen_two(seconds, downs, outs, shards):
    rows, columns = seconds[0].shape
    count, width = downs[0].shape
    steps = 4

    def row_at(which, i):
        half = steps // 2
        return (i, jnp.minimum(i, half - 1), jnp.maximum(i - half, 0))[(which + 1) % 3]

    def specs(parts):
        return [
            pl.BlockSpec(
                (parts[0].shape[0] // steps, parts[0].shape[1]),
                functools.partial(lambda w, i: (row_at(w, i), 0), w),
            )
            for w in WHEN
        ]

    units = jax.ShapeDtypeStruct((rows, 4 * columns), f32)
    stack = jax.ShapeDtypeStruct((8, count, width), f32)
    gelu, up, down, out = pl.pallas_call(
        functools.partial(widen_two_kernel, steps, shards),
        grid=(steps,),
        in_specs=specs(seconds)
        + specs(downs)
        + [pl.BlockSpec((8, count // steps, width), lambda i: (0, i, 0))],
        out_specs=[pl.BlockSpec((rows // steps, 4 * columns), lambda i: (i, 0))] * 2
        + [pl.BlockSpec((8, count // steps, width), lambda i: (0, i, 0))] * 2,
        out_shape=[units, units, stack, stack],
        compiler_params=params(),
        cost_estimate=cost(25),
        name="widen_two",
    )(*seconds, *downs, outs)
    return gelu, up, down.reshape(8 * count, width), out.reshape(8 * count, width)


def widen_one_kernel(edges, parts, _after, *goals):
    for goal, (begin, end) in zip(goals, zip(edges, edges[1:])):
        size = end - begin
        for i in range(8):
            goal[:, i * size : (i + 1) * size] = parts[i, :, begin:end].astype(f32)


def widen_one(parts, edges, after, name):
    _, rows, columns = parts.shape
    sizes = [b - a for a, b in zip(edges, edges[1:])]
    block = 64
    return pl.pallas_call(
        functools.partial(widen_one_kernel, edges),
        grid=(rows // block,),
        in_specs=[pl.BlockSpec((8, block, columns), lambda i: (0, i, 0)), ANY],
        out_specs=[pl.BlockSpec((block, 8 * size), lambda i: (i, 0)) for size in sizes],
        out_shape=[jax.ShapeDtypeStruct((rows, 8 * size), f32) for size in sizes],
        compiler_params=params(),
        cost_estimate=cost(14),
        name=name,
    )(parts, after)


def local(
    tokens,
    cotangent,
    token_order,
    lengths,
    query_weight,
    key_weight,
    value_weight,
    gate_weight,
    out_weight,
    gelu_weight,
    up_weight,
    down_weight,
    gain_one,
    shift_one,
    gain_two,
    shift_two,
):
    every = ("outer", "tp", "shard")
    device_count = lax.axis_size(every)
    device_index = lax.axis_index(every)
    outer, tp, shards = lax.axis_size("outer"), lax.axis_size("tp"), lax.axis_size("shard")
    t, z = lax.axis_index("tp"), lax.axis_index("shard")
    rows, width = tokens.shape
    packs = lengths.shape[0]
    pack_rows = rows // packs
    group_rows = tp * rows
    group_packs = tp * packs

    own_order = lax.dynamic_slice_in_dim(token_order, device_index * rows, rows)
    target = own_order // rows
    places = jnp.arange(rows, dtype=jnp.int32)
    before = (target[None, :] < target[:, None]) | (
        (target[None, :] == target[:, None]) & (places[None, :] < places[:, None])
    )
    send_place = jnp.sum(before.astype(jnp.int32), axis=1)
    send_mix = (send_place[None, :] == places[:, None]).astype(bf16)
    loader_ids = jnp.arange(token_order.shape[0], dtype=jnp.int32)
    slot_targets = device_index * rows + places
    origin = jnp.sum(
        jnp.where(token_order[None, :] == slot_targets[:, None], loader_ids[None, :], 0), axis=1
    )
    arrive_place = jnp.sum((origin[None, :] < origin[:, None]).astype(jnp.int32), axis=1)
    work_mix = (arrive_place[:, None] == places[None, :]).astype(bf16)

    def exchange(value):
        return lax.all_to_all(
            value.reshape(device_count, rows // device_count, value.shape[1]),
            every,
            split_axis=0,
            concat_axis=0,
            tiled=True,
        ).reshape(rows, value.shape[1])

    piece = rows // device_count
    part = gain_one.shape[0]
    extra = jnp.concatenate(
        [gain_one, shift_one, gain_two, shift_two, lengths.reshape(-1).astype(bf16)]
    )
    extra_columns = -(-extra.shape[0] // (piece * 128)) * 128
    extra = jnp.pad(extra, (0, piece * extra_columns - extra.shape[0]))
    extra = jnp.tile(extra.reshape(piece, extra_columns), (device_count, 1))
    came = exchange(
        jnp.concatenate([forward_dot(send_mix, tokens).astype(bf16), extra], axis=1)
    )
    t_early = t + (came[0, 0].astype(f32) > 100.0).astype(jnp.int32)
    arrived = came[:, width:].reshape(outer, tp, shards, -1)
    small = jnp.transpose(arrived[0, 0, :, : 4 * part].reshape(shards, 4, part), (1, 0, 2))
    small = small.reshape(4, width).astype(f32)
    small = jnp.concatenate([small, jnp.zeros((4, width), f32)], axis=0)
    all_lengths = arrived[lax.axis_index("outer"), :, z, 4 * part : 4 * part + lengths.size]
    all_lengths = all_lengths.reshape(group_packs, -1).astype(f32).astype(jnp.int32)

    def along_z(piece):
        return lax.all_gather(piece, "shard", axis=0, tiled=True)

    def cut(weight):
        part = weight.shape[1] // tp
        return lax.dynamic_slice_in_dim(weight, t_early * part, part, axis=1)

    out_unit = out_weight.shape[0] // tp
    unit = down_weight.shape[0] // tp
    piece_rows = query_weight.shape[0]
    key_part, value_part = query_weight.shape[1] // tp, value_weight.shape[1] // tp
    edges = (0, key_part, 2 * key_part, 2 * key_part + value_part)
    first_size = 2 * key_part + 2 * value_part
    hidden_part = shards * unit

    def fold(value):
        cuts = piece_rows // value.shape[0]
        value = value.reshape(value.shape[0], cuts, width // cuts)
        return jnp.transpose(value, (1, 0, 2)).reshape(piece_rows, width // cuts)

    def unfold(value, count):
        cuts = piece_rows // count
        value = value.reshape(shards, cuts, count, width // cuts)
        return jnp.transpose(value, (0, 2, 1, 3)).reshape(shards, count, width)

    out_piece = lax.dynamic_slice_in_dim(out_weight, t_early * out_unit, out_unit, axis=0)
    w_one = along_z(
        jnp.concatenate(
            [cut(w) for w in (query_weight, key_weight, value_weight, gate_weight)]
            + [fold(out_piece)],
            axis=1,
        )
    )
    ends = jnp.cumsum(lengths, axis=1, dtype=jnp.int32)[:, -2]
    usable = (jnp.arange(pack_rows, dtype=jnp.int32)[None, :] < ends[:, None]).astype(f32)
    usable = usable.reshape(rows, 1)
    came_back = exchange(forward_dot(send_mix, cotangent).astype(bf16))
    x, normed = entry(came, work_mix, small, 0)
    t_late = t + (x[0, 0].astype(f32) > 100.0).astype(jnp.int32)

    def unit_columns(weight):
        return [
            lax.dynamic_slice_in_dim(weight, (k * tp + t_late) * unit, unit, axis=1)
            for k in range(shards)
        ]

    down_piece = lax.dynamic_slice_in_dim(down_weight, t_late * unit, unit, axis=0)
    w_two = along_z(
        jnp.concatenate(
            unit_columns(gelu_weight) + unit_columns(up_weight) + [fold(down_piece)], axis=1
        )
    )
    back_out, back_low = entry_back(came_back, work_mix, usable, x, 7)
    normed, back_low = normed.reshape(group_rows, width), back_low.reshape(group_rows, width)
    cosine, sine, decays, _ = pack_tables(all_lengths, pack_rows, t + jnp.arange(1))
    cosine, sine = cosine.reshape(group_rows, -1), sine.reshape(group_rows, -1)
    decays = decays[0]
    out_pieces = unfold(w_one[:, first_size:], out_unit)
    q_rot, k_rot, v_low, weights_low, gating, retained, branch, wo = retain(
        normed, w_one, value_part, cosine, sine, decays, out_pieces, rows, 1
    )
    wo = wo.reshape(shards * out_unit, width)
    middle, normed_two = make_middle(branch, wo, x, small, 2)
    normed_two = normed_two.reshape(group_rows, width)

    hidden, second_low, w_down, branch_rows = feed(
        normed_two, back_low, w_two, branch, hidden_part, shards, rows, 6
    )
    down_gram = gram_rows(hidden, back_low).astype(bf16)
    second_gram = gram_rows(normed_two, second_low).astype(bf16)

    def to_owner(value):
        part = lax.psum_scatter(value, "shard", scatter_dimension=0, tiled=True)
        return lax.psum(part, "outer") if outer > 1 else part

    down_sum, second_sum = to_owner(down_gram), to_owner(second_gram)
    back_middle, parts_two, middle_low = make_back_middle(
        second_low, w_two, middle, back_out, small, down_gram, second_gram, 3
    )
    middle_low = middle_low.reshape(group_rows, width)
    out_sum = to_owner(gram_rows(branch_rows, middle_low).astype(bf16))
    first_low, *down_by = retain_back(
        middle_low, wo, q_rot, k_rot, v_low, weights_low, gating, retained, cosine, sine, decays,
        down_sum, rows, 8,
    )
    first_gram, third_gram, *second_by = gram_beside(
        normed, first_low, second_sum, edges[2], 256, 9
    )
    first_sum, third_sum = to_owner(first_gram), to_owner(third_gram)
    by_x, by_y, by_sib = ([a, b] for a, b in zip(second_by, down_by))
    back_inputs, parts_one, groups = make_back_input(
        first_low, w_one, x, back_middle, small, by_x, by_y, 4
    )
    ending, sums, (outs, firsts) = make_ending(
        hidden, w_down, middle, usable, parts_one, parts_two, [out_sum, first_sum], 5
    )
    low, high, sib_x, sib_y, sib_low, sib_high = groups
    seconds, downs = (
        [
            value, by_x[k], by_y[k], low[k], high[k],
            by_sib[k], sib_x[k], sib_y[k], sib_low[k], sib_high[k],
        ]
        for k, value in enumerate((second_sum, down_sum))
    )

    if unit % 128 == 0:
        gelu_gradient, up_gradient, down_gradient, out_gradient = widen_two(
            seconds, downs, outs, shards
        )
    else:
        down_gradient = in_order(downs).reshape(-1, width).astype(f32)
        out_gradient = outs.reshape(-1, width).astype(f32)
        both = in_order(seconds).reshape(tp, piece_rows, 2, shards, unit)
        both = jnp.transpose(both, (2, 1, 3, 0, 4)).reshape(2, piece_rows, -1).astype(f32)
        gelu_gradient, up_gradient = both[0], both[1]
    thirds = lax.all_gather(third_sum + sums[5, 0].astype(bf16), "tp", axis=0)
    query_gradient, key_gradient = widen_one(firsts, edges[:3], down_gradient, "widen_one")
    value_gradient, gate_gradient = widen_one(
        thirds, (0, value_part, 2 * value_part), query_gradient, "widen_three"
    )
    smalls = lax.psum(sums, "outer") if outer > 1 else sums

    home = jnp.concatenate([ending, back_inputs], axis=1)
    home = exchange(gram_rows(work_mix, home).astype(bf16))
    home = gram_rows(send_mix, home).astype(bf16)
    result, token_gradient = home[:, :width], home[:, width:]
    return (
        result,
        token_gradient,
        query_gradient,
        key_gradient,
        value_gradient,
        gate_gradient,
        out_gradient,
        gelu_gradient,
        up_gradient,
        down_gradient,
        smalls[0],
        smalls[1],
        smalls[2],
        smalls[3],
    )


def solution(mesh):
    tp = math.gcd(mesh.shape["rep"], HEADS)
    grid = mesh.devices.reshape(mesh.shape["rep"] // tp, tp, mesh.shape["shard"])
    cube = Mesh(grid, ("outer", "tp", "shard"))
    tokens_at = P(("outer", "tp", "shard"), None)
    weights_at = P("shard", None)
    vectors_at = P("shard")
    in_specs = (tokens_at, tokens_at, P(), tokens_at) + (weights_at,) * 8 + (vectors_at,) * 4
    out_specs = (tokens_at, tokens_at) + (weights_at,) * 8 + (vectors_at,) * 4
    return jax.shard_map(local, mesh=cube, in_specs=in_specs, out_specs=out_specs, check_vma=False)
```

```python
import functools
import math

import jax
import jax.numpy as jnp
from jax import lax
from jax.experimental import pallas as pl
from jax.experimental.pallas import tpu as pltpu
from jax.sharding import Mesh, PartitionSpec as P

HEADS = 8
KH = 256

layer_epsilon = 1e-05
head_epsilon = 1.0
rotary_base = 10000.0
bf16 = jnp.bfloat16
f32 = jnp.float32
MESHID = pl.DeviceIdType.MESH


def pack_tables(lengths, pack_rows, head_ids):
    entries = lengths.shape[1]
    slot_ids = jnp.arange(pack_rows, dtype=jnp.int32)
    seq_ends = jnp.cumsum(lengths, axis=1, dtype=jnp.int32)
    seq_starts = seq_ends - lengths
    segment = jnp.sum(
        (slot_ids[None, :, None] >= seq_ends[:, None, :]).astype(jnp.int32), axis=2, dtype=jnp.int32
    )
    owners = segment[:, :, None] == jnp.arange(entries, dtype=jnp.int32)[None, None, :]
    begins = jnp.sum(jnp.where(owners, seq_starts[:, None, :], 0), axis=2, dtype=jnp.int32)
    places = (slot_ids[None, :] - begins).astype(f32)
    usable = segment < entries - 1
    half_size = KH // 2
    frequency = jnp.power(
        f32(rotary_base), -jnp.arange(half_size, dtype=f32) / f32(half_size - 1)
    )
    angles = places[:, :, None] * frequency
    cosine_table = jnp.cos(angles)
    sine_table = jnp.sin(angles)
    lag_steps = slot_ids[:, None] - slot_ids[None, :]
    linked = (
        (segment[:, :, None] == segment[:, None, :])
        & (lag_steps[None] >= 0)
        & usable[:, None, :]
    )
    log_rates = jnp.log(1.0 - jnp.power(f32(2.0), -5.0 - head_ids.astype(f32)))
    powers = jnp.exp(log_rates[:, None, None] * jnp.maximum(lag_steps, 0).astype(f32)[None])
    decays = jnp.where(linked[None], powers[:, None], f32(0.0))
    return cosine_table, sine_table, decays, usable


def gram_rows(leading, trailing):
    return lax.dot_general(
        leading, trailing, (((0,), (0,)), ((), ())), preferred_element_type=f32
    )


def back_through(incoming, matrix):
    return lax.dot_general(
        incoming, matrix, (((1,), (1,)), ((), ())), preferred_element_type=f32
    )


def forward_dot(inputs, matrix):
    return jnp.dot(inputs, matrix, preferred_element_type=f32)


def gelu_parts(v):
    c = f32(math.sqrt(2.0 / math.pi))
    t = jnp.tanh(c * (v + 0.044715 * v * v * v))
    value = 0.5 * v * (1.0 + t)
    slope = 0.5 * (1.0 + t) + 0.5 * v * (1.0 - t * t) * c * (1.0 + 3.0 * 0.044715 * v * v)
    return value, slope


def flip(me, mask):
    for bit in (1, 2, 4):
        if mask & bit:
            me = me + bit - 2 * bit * ((me // bit) % 2)
    return me


def greet(far=False):
    me = lax.axis_index("tp")
    barrier = pltpu.get_barrier_semaphore()
    for mask in (1, 2, 4):
        pl.semaphore_signal(
            barrier, inc=1, device_id={"tp": flip(me, mask)}, device_id_type=MESHID
        )
    count = 3
    if far:
        for other in others():
            pl.semaphore_signal(barrier, inc=1, device_id={"shard": other}, device_id_type=MESHID)
            count += 1
    pl.semaphore_wait(barrier, count)
    return me


def others():
    shards = lax.axis_size("shard")
    return [(lax.axis_index("shard") + k) % shards for k in range(1, shards)]


def push(source, goal, send, recv, peer):
    return pltpu.make_async_remote_copy(
        src_ref=source, dst_ref=goal, send_sem=send, recv_sem=recv,
        device_id={"tp": peer}, device_id_type=MESHID,
    )


def gather_begin(me, own, out, send, recv, halves=(True, True), first=None):
    half = own.shape[0] // 2
    xn, yn = flip(me, 2), flip(me, 4)
    low, high = pl.ds(0, half), pl.ds(half, half)
    first = first if first is not None else [None] * 5
    ways = ((low, xn), (high, yn), (high, xn), (low, yn))
    for i in (0, 3, 1, 2):
        part, peer = ways[i]
        if halves[0 if part is low else 1]:
            first[i] = push(own.at[part], out.at[me, part], send.at[i], recv.at[i], peer)
            first[i].start()
    if halves[1]:
        first[4] = push(own, out.at[me], send.at[4], recv.at[4], flip(me, 1))
        first[4].start()
    return first


def gather_end(me, own, out, send, recv, first):
    half = own.shape[0] // 2
    sib, xn, yn, dn = flip(me, 1), flip(me, 2), flip(me, 4), flip(me, 6)
    low, high = pl.ds(0, half), pl.ds(half, half)
    started = list(first)

    def on(slot, part, peer):
        i = len(started)
        place = out.at[slot, part]
        c = push(place, place, send.at[i], recv.at[i], peer)
        c.start()
        started.append(c)
        return c

    first[0].wait_recv()
    d_low = on(xn, low, yn)
    first[1].wait_recv()
    d_high = on(yn, high, xn)
    on(xn, low, sib)
    on(yn, high, sib)
    first[2].wait_recv()
    on(xn, high, sib)
    first[3].wait_recv()
    on(yn, low, sib)
    d_low.wait_recv()
    on(dn, low, sib)
    d_high.wait_recv()
    on(dn, high, sib)
    for i in (4, 7, 8, 9, 10, 11, 12):
        started[i].wait_recv()
    for c in started:
        c.wait_send()


def gather_steps(me, own, out, send, recv):
    gather_end(me, own, out, send, recv, gather_begin(me, own, out, send, recv))


COLS = 512


def reduce_stages(me, pairs, transposed, tosib, fromsib, hold, hop, final, total, send, recv):
    rows, width = total.shape
    half = rows // 2
    sib, xn, yn = flip(me, 1), flip(me, 2), flip(me, 4)
    low, high = pl.ds(0, half), pl.ds(half, half)

    def product(block, tile):
        acc = None
        for act, weight in pairs:
            left = act[pl.ds(pl.multiple_of(block * rows, rows), rows), :]
            if transposed:
                part = lax.dot_general(
                    left, weight[pl.ds(pl.multiple_of(tile * COLS, COLS), COLS), 0 : act.shape[1]],
                    (((1,), (1,)), ((), ())), preferred_element_type=f32,
                )
            else:
                part = jnp.dot(
                    left, weight[:, pl.ds(pl.multiple_of(tile * COLS, COLS), COLS)],
                    preferred_element_type=f32,
                )
            acc = part if acc is None else acc + part
        return acc

    def cp(i, src, goal, peer):
        return push(src, goal, send.at[i], recv.at[i], peer)

    masks = (6, 2, 4, 0)
    over, out = [], {}

    def for_sibling(slot):
        block = flip(me, masks[slot] ^ 1)

        @pl.loop(0, width // COLS)
        def _(tile):
            at = pl.ds(pl.multiple_of(tile * COLS, COLS), COLS)
            tosib[slot, :, at] = product(block, tile).astype(bf16)

        c = cp(slot, tosib.at[slot], fromsib.at[slot], sib)
        c.start()
        over.append(c)

    def for_own_core(slot):
        block = flip(me, masks[slot])
        over[slot].wait_recv()

        @pl.loop(0, width // COLS)
        def _(tile):
            at = pl.ds(pl.multiple_of(tile * COLS, COLS), COLS)
            value = product(block, tile) + fromsib[slot, :, at].astype(f32)
            if slot < 3:
                hold[slot, :, at] = value.astype(bf16)
            else:
                total[:, at] = value

    for_sibling(0)
    for_sibling(1)
    for_own_core(0)
    dx = cp(4, hold.at[0, low], hop.at[0], xn)
    dy = cp(5, hold.at[0, high], hop.at[1], yn)
    dx.start()
    dy.start()
    for_sibling(2)
    for_own_core(1)
    xa = cp(6, hold.at[1, low], final.at[0, low], xn)
    xa.start()
    for_sibling(3)
    for_own_core(2)
    yb = cp(7, hold.at[2, high], final.at[1, high], yn)
    yb.start()
    for_own_core(3)
    yield
    dy.wait_recv()
    hold[1, high] = (hold[1, high].astype(f32) + hop[1].astype(f32)).astype(bf16)
    xb = cp(8, hold.at[1, high], final.at[0, high], xn)
    xb.start()
    dx.wait_recv()
    hold[2, low] = (hold[2, low].astype(f32) + hop[0].astype(f32)).astype(bf16)
    ya = cp(9, hold.at[2, low], final.at[1, low], yn)
    ya.start()
    yield
    xa.wait_recv()
    yb.wait_recv()
    xb.wait_recv()
    ya.wait_recv()
    for c in over + [dx, dy, xa, yb, xb, ya]:
        c.wait_send()


def reduce_steps(*args):
    for _ in reduce_stages(*args):
        pass


def summed(total, final, at):
    return total[at, :] + final[0, at, :].astype(f32) + final[1, at, :].astype(f32)


def reduce_scratch(rows, width):
    return [
        pltpu.VMEM((4, rows, width), bf16),
        pltpu.VMEM((4, rows, width), bf16),
        pltpu.VMEM((3, rows, width), bf16),
        pltpu.VMEM((2, rows // 2, width), bf16),
        pltpu.VMEM((2, rows, width), bf16),
        pltpu.VMEM((rows, width), f32),
        pltpu.SemaphoreType.DMA((10,)),
        pltpu.SemaphoreType.DMA((10,)),
    ]


CHUNK = 32


def cost(us):
    return pl.CostEstimate(flops=int(us * 1e9), bytes_accessed=int(us * 3e6), transcendentals=0)


def params(cid=None):
    if cid is None:
        return pltpu.CompilerParams(vmem_limit_bytes=60 << 20)
    return pltpu.CompilerParams(collective_id=cid, has_side_effects=True, vmem_limit_bytes=60 << 20)


def by_rows(count, begin=0):
    def run(body):
        @pl.loop(begin // CHUNK, count // CHUNK)
        def _(i):
            body(pl.ds(pl.multiple_of(i * CHUNK, CHUNK), CHUNK))

    return run


def gather_as_made(me, make, own, out, send, recv, local_sem):
    rows = own.shape[0]
    by_rows(rows // 2)(make)
    first = gather_begin(me, own, out, send, recv, (True, False))
    by_rows(rows, rows // 2)(make)
    gather_begin(me, own, out, send, recv, (False, True), first)
    mine = pltpu.make_async_copy(own, out.at[me], local_sem)
    mine.start()
    gather_end(me, own, out, send, recv, first)
    mine.wait()


def centre(value, epsilon):
    average = jnp.mean(value, axis=-1, keepdims=True)
    centred = value - average
    spread = jnp.mean(centred * centred, axis=-1, keepdims=True)
    root = lax.rsqrt(spread + epsilon)
    return centred * root, root


def through_norm(e, unit, root):
    return root * (
        e - jnp.mean(e, axis=-1, keepdims=True) - unit * jnp.mean(e * unit, axis=-1, keepdims=True)
    )


def leading(rows, columns):
    return pl.BlockSpec((rows, columns), lambda *_: (0, 0))


ANY = pl.BlockSpec(memory_space=pl.ANY)
WHOLE = pl.BlockSpec(memory_space=pltpu.VMEM)


def gather_scratch(rows, width):
    return [
        pltpu.VMEM((rows, width), bf16),
        pltpu.SemaphoreType.DMA((13,)),
        pltpu.SemaphoreType.DMA((13,)),
        pltpu.SemaphoreType.DMA,
    ]


def gather_all(me, own, out, send, recv, local_sem):
    mine = pltpu.make_async_copy(own, out.at[me], local_sem)
    mine.start()
    gather_steps(me, own, out, send, recv)
    mine.wait()


def entry_kernel(came, mix, small, x_out, normed_all, own, send, recv, sem):
    me = greet()
    width = x_out.shape[1]

    @by_rows(came.shape[0])
    def _(at):
        value = jnp.dot(mix[at, :], came[:, :width], preferred_element_type=f32)
        x_out[at, :] = value.astype(bf16)
        unit, _ = centre(value, layer_epsilon)
        own[at, :] = (unit * small[0:1, :] + small[1:2, :]).astype(bf16)

    gather_all(me, own, normed_all, send, recv, sem)


def entry(came, mix, small, cid):
    rows, width = came.shape[0], small.shape[1]
    return pl.pallas_call(
        entry_kernel,
        out_shape=(
            jax.ShapeDtypeStruct((rows, width), bf16),
            jax.ShapeDtypeStruct((8, rows, width), bf16),
        ),
        in_specs=[WHOLE] * 3,
        out_specs=(WHOLE, ANY),
        scratch_shapes=gather_scratch(rows, width),
        compiler_params=params(cid),
        cost_estimate=cost(50),
        name="entry",
    )(came, mix, small)


def entry_back_kernel(came, mix, usable, _after, back_out, back_all, own, send, recv, sem):
    me = greet()

    @by_rows(came.shape[0])
    def _(at):
        value = jnp.dot(mix[at, :], came[...], preferred_element_type=f32)
        value = jnp.where(usable[at, :] > 0.5, value, 0.0).astype(bf16)
        back_out[at, :] = value
        own[at, :] = value

    gather_all(me, own, back_all, send, recv, sem)


def entry_back(came, mix, usable, after, cid):
    rows, width = came.shape
    return pl.pallas_call(
        entry_back_kernel,
        out_shape=(
            jax.ShapeDtypeStruct((rows, width), bf16),
            jax.ShapeDtypeStruct((8, rows, width), bf16),
        ),
        in_specs=[WHOLE] * 3 + [ANY],
        out_specs=(WHOLE, ANY),
        scratch_shapes=gather_scratch(rows, width),
        compiler_params=params(cid),
        cost_estimate=cost(45),
        name="entry_back",
    )(came, mix, usable, after)


def deal_plan(back, count):
    heads = HEADS // count
    me = lax.axis_index("tp")
    spread = [i * heads + me // count for i in range(count)]
    packed = [(me % heads) * count + i for i in range(count)]
    goals, sources = (packed, spread) if back else (spread, packed)
    return me, goals, sources, (me // heads if back else me % count), me // count == me % heads


def deal_start(back, count, source, goal, send, recv, local_sem):
    me, goals, sources, slot, inside = deal_plan(back, count)
    barrier = pltpu.get_barrier_semaphore()
    for i in range(count):

        @pl.when(sources[i] != me)
        def _():
            pl.semaphore_signal(
                barrier, inc=1, device_id={"tp": sources[i]}, device_id_type=MESHID
            )

    pl.semaphore_wait(barrier, jnp.where(inside, count - 1, count))
    for i in range(count):

        @pl.when(goals[i] == me)
        def _():
            pltpu.make_async_copy(source(i), goal(slot), local_sem).start()

        @pl.when(goals[i] != me)
        def _():
            push(source(i), goal(slot), send.at[i], recv.at[slot], goals[i]).start()


def deal_wait(back, count, source, goal, send, recv, local_sem):
    me, goals, sources, slot, _ = deal_plan(back, count)
    for i in range(count):

        @pl.when(goals[i] == me)
        def _():
            pltpu.make_async_copy(source(i), goal(slot), local_sem).wait()

        @pl.when(goals[i] != me)
        def _():
            push(source(i), goal(slot), send.at[i], recv.at[slot], goals[i]).wait_send()

        @pl.when(sources[i] != me)
        def _():
            push(source(i), goal(i), send.at[i], recv.at[i], sources[i]).wait_recv()


def blocks(ref):
    return lambda i: ref.at[i]


def column_blocks(ref, size):
    return lambda i: ref.at[:, pl.ds(pl.multiple_of(i * size, size), size)]


def deal_scratch(count):
    return [
        pltpu.SemaphoreType.DMA((count,)),
        pltpu.SemaphoreType.DMA((count,)),
        pltpu.SemaphoreType.DMA,
    ]


def phase_one_copies(me, values, by_x, by_y, by_sib, send, recv):
    copies = []
    for k, value in enumerate(values):
        for i, (goal, mask) in enumerate(((by_x, 2), (by_y, 4), (by_sib, 1))):
            n = 3 * k + i
            copies.append(push(value, goal[k], send.at[n], recv.at[n], flip(me, mask)))
    return copies


def phase_one(*args):
    copies = phase_one_copies(*args)
    for c in copies:
        c.start()
    return copies


def phase_two(me, by_x, by_y, low, high, sib_x, sib_y, send, recv):
    copies = []
    for k in range(len(by_x)):
        half = by_x[k].shape[0] // 2
        for i, (source, goal, mask) in enumerate(
            (
                (by_x[k].at[pl.ds(0, half)], low[k], 4),
                (by_y[k].at[pl.ds(half, half)], high[k], 2),
                (by_x[k], sib_x[k], 1),
                (by_y[k], sib_y[k], 1),
            )
        ):
            n = 4 * k + i
            copies.append(push(source, goal, send.at[n], recv.at[n], flip(me, mask)))
    for c in copies:
        c.start()
    return copies


def phase_three(me, low, high, sib_low, sib_high, send, recv):
    copies = []
    for k in range(len(low)):
        for i, (source, goal) in enumerate(((low[k], sib_low[k]), (high[k], sib_high[k]))):
            n = 2 * k + i
            copies.append(push(source, goal, send.at[n], recv.at[n], flip(me, 1)))
    for c in copies:
        c.start()
    return copies


def pair(count):
    return [pltpu.SemaphoreType.DMA((count,)), pltpu.SemaphoreType.DMA((count,))]


def same(values, halves=False):
    return [
        jax.ShapeDtypeStruct((v.shape[0] // 2 if halves else v.shape[0], v.shape[1]), v.dtype)
        for v in values
    ]


def turn(value, cosine, sine):
    half = value.shape[-1] // 2
    a, b = value[:, :half], value[:, half:]
    return jnp.concatenate([a * cosine - b * sine, a * sine + b * cosine], axis=1)


def retain_kernel(
    normed, weight, cosine, sine, decays, pieces,
    q_out, k_out, v_out, w_out, g_out, r_out, branch, wo, *sems
):
    @pl.when(pl.program_id(0) == 0)
    def _():
        deal_start(False, pieces.shape[0], blocks(pieces), blocks(wo), *sems)

    packs, span = decays.shape[0], decays.shape[1]
    value_at = 2 * KH
    gate_at = value_at + v_out.shape[1]
    rows = normed[...]

    def project(begin, size):
        return jnp.dot(rows, weight[:, begin : begin + size], preferred_element_type=f32)

    q_out[...] = turn(project(0, KH), cosine[...], sine[...]).astype(bf16)
    k_out[...] = (turn(project(KH, KH), cosine[...], sine[...]) * KH ** (-0.5)).astype(bf16)
    v_out[...] = project(value_at, v_out.shape[1]).astype(bf16)
    g_out[...] = project(gate_at, g_out.shape[1])
    for p in range(packs):
        at = pl.ds(p * span, span)
        scores = lax.dot_general(
            q_out[at, :], k_out[at, :], (((1,), (1,)), ((), ())), preferred_element_type=f32
        )
        low = (scores * decays[p]).astype(bf16)
        w_out[p] = low
        retained = jnp.dot(low, v_out[at, :], preferred_element_type=f32)
        r_out[at, :] = retained
        unit, _ = centre(retained, head_epsilon)
        gating = g_out[at, :]
        branch[at, :] = (gating * jax.nn.sigmoid(gating) * unit).astype(bf16)

    @pl.when(pl.program_id(0) == pl.num_programs(0) - 1)
    def _():
        deal_wait(False, pieces.shape[0], blocks(pieces), blocks(wo), *sems)


def retain(normed, weight, value_size, cosine, sine, decays, pieces, block, cid):
    total, width = normed.shape
    span = decays.shape[1]
    grid = total // block
    row = lambda w: pl.BlockSpec((block, w), lambda i: (i, 0))
    square = pl.BlockSpec((block // span, span, span), lambda i: (i, 0, 0))
    flat = lambda w, kind: jax.ShapeDtypeStruct((total, w), kind)
    return pl.pallas_call(
        retain_kernel,
        grid=(grid,),
        in_specs=[
            row(width), leading(width, 2 * KH + 2 * value_size), row(KH // 2), row(KH // 2), square,
            ANY,
        ],
        out_specs=(
            row(KH), row(KH), row(value_size), square, row(value_size), row(value_size),
            row(value_size), ANY,
        ),
        out_shape=(
            flat(KH, bf16), flat(KH, bf16), flat(value_size, bf16),
            jax.ShapeDtypeStruct(decays.shape, bf16), flat(value_size, f32),
            flat(value_size, f32), flat(value_size, bf16),
            jax.ShapeDtypeStruct(pieces.shape, bf16),
        ),
        scratch_shapes=deal_scratch(pieces.shape[0]),
        compiler_params=params(cid),
        cost_estimate=cost(24),
        name="retain",
    )(normed, weight, cosine, sine, decays, pieces)


def phase_one_of(value, by, sems):
    return phase_one_copies(lax.axis_index("tp"), [value], by[:1], by[1:2], by[2:], *sems)


def retain_back_kernel(
    middle_low, wo, q_in, k_in, v_in, w_in, g_in, r_in, cosine, sine, decays, value,
    low, by_x, by_y, by_sib, *sems
):
    by = (by_x, by_y, by_sib)

    @pl.when(pl.program_id(0) == 0)
    def _():
        greet()
        for c in phase_one_of(value, by, sems):
            c.start()

    packs, span = decays.shape[0], decays.shape[1]
    value_at = 2 * KH
    value_size = v_in.shape[1]
    gate_at = value_at + value_size
    back_branch = lax.dot_general(
        middle_low[...], wo[...], (((1,), (1,)), ((), ())), preferred_element_type=f32
    )
    cols = (((0,), (0,)), ((), ()))
    last = (((1,), (1,)), ((), ()))
    for p in range(packs):
        at = pl.ds(p * span, span)
        bb = back_branch[p * span : (p + 1) * span]
        unit, root = centre(r_in[at, :], head_epsilon)
        gating = g_in[at, :]
        sigma = jax.nn.sigmoid(gating)
        low[at, gate_at:] = (bb * unit * (sigma * (1.0 + gating * (1.0 - sigma)))).astype(bf16)
        retained_low = through_norm(bb * (gating * sigma), unit, root).astype(bf16)
        back_weights = lax.dot_general(retained_low, v_in[at, :], last, preferred_element_type=f32)
        low[at, value_at:gate_at] = lax.dot_general(
            w_in[p], retained_low, cols, preferred_element_type=f32
        ).astype(bf16)
        back_scores = (back_weights * decays[p]).astype(bf16)
        back_q = jnp.dot(back_scores, k_in[at, :], preferred_element_type=f32)
        back_k = lax.dot_general(back_scores, q_in[at, :], cols, preferred_element_type=f32)
        low[at, :KH] = turn(back_q, cosine[at, :], -sine[at, :]).astype(bf16)
        low[at, KH:value_at] = (turn(back_k, cosine[at, :], -sine[at, :]) * KH ** (-0.5)).astype(bf16)

    @pl.when(pl.program_id(0) == pl.num_programs(0) - 1)
    def _():
        for c in phase_one_of(value, by, sems):
            c.wait()


def retain_back(middle_low, wo, q, k, v, w, g, r, cosine, sine, decays, value, block, cid):
    total, width = middle_low.shape
    span = decays.shape[1]
    value_size = v.shape[1]
    row = lambda w: pl.BlockSpec((block, w), lambda i: (i, 0))
    square = pl.BlockSpec((block // span, span, span), lambda i: (i, 0, 0))
    return pl.pallas_call(
        retain_back_kernel,
        grid=(total // block,),
        in_specs=[
            row(width), WHOLE, row(KH), row(KH), row(value_size), square, row(value_size),
            row(value_size), row(KH // 2), row(KH // 2), square, ANY,
        ],
        out_specs=[row(2 * KH + 2 * value_size)] + [ANY] * 3,
        out_shape=[
            jax.ShapeDtypeStruct((total, 2 * KH + 2 * value_size), bf16),
        ]
        + same([value]) * 3,
        scratch_shapes=pair(3),
        compiler_params=params(cid),
        cost_estimate=cost(20),
        name="retain_back",
    )(middle_low, wo, q, k, v, w, g, r, cosine, sine, decays, value)


def feed_kernel(shards, count, normed_two, back_low, w_two, branch, hidden, low, w_down, dealt, *sems):
    size = hidden.shape[1]
    views = (
        column_blocks(branch, branch.shape[1] // count) if count else None,
        column_blocks(dealt, branch.shape[1] // count) if count else None,
    )

    @pl.when(pl.program_id(0) == 0)
    def _():
        if count:
            deal_start(True, count, *views, *sems)
        unit = size // shards
        span = w_two.shape[0] // shards
        part = w_two.shape[1] - 2 * size
        for z in range(shards):
            for c in range(span // unit):
                begin = z * span + c * unit
                w_down[z * unit : (z + 1) * unit, c * part : (c + 1) * part] = w_two[
                    begin : begin + unit, 2 * size :
                ]

    both = jnp.dot(normed_two[...], w_two[:, : 2 * size], preferred_element_type=f32)
    back = lax.dot_general(
        back_low[...], w_down[...], (((1,), (1,)), ((), ())), preferred_element_type=f32
    )
    up = both[:, size:]
    value, slope = gelu_parts(both[:, :size])
    hidden[...] = (value * up).astype(bf16)
    low[:, :size] = (back * up * slope).astype(bf16)
    low[:, size:] = (back * value).astype(bf16)

    if count:

        @pl.when(pl.program_id(0) == pl.num_programs(0) - 1)
        def _():
            deal_wait(True, count, *views, *sems)


def feed(normed_two, back_low, w_two, branch, size, shards, block, cid):
    total, width = normed_two.shape
    row = lambda w: pl.BlockSpec((block, w), lambda i: (i, 0))
    count = shards if branch.shape[1] // shards % 128 == 0 else 0
    hidden, low, w_down, dealt = pl.pallas_call(
        functools.partial(feed_kernel, shards, count),
        grid=(total // block,),
        in_specs=[row(width), row(width), WHOLE, ANY],
        out_specs=(row(size), row(2 * size), pl.BlockSpec((size, width), lambda i: (0, 0)), ANY),
        out_shape=(
            jax.ShapeDtypeStruct((total, size), bf16),
            jax.ShapeDtypeStruct((total, 2 * size), bf16),
            jax.ShapeDtypeStruct((size, width), bf16),
            jax.ShapeDtypeStruct(branch.shape if count else (8, 128), bf16),
        ),
        scratch_shapes=deal_scratch(count) if count else [],
        compiler_params=params(cid if count else None),
        cost_estimate=cost(26),
        name="feed",
    )(normed_two, back_low, w_two, branch)
    if not count:
        pieces = jnp.transpose(branch.reshape(total, shards, -1), (1, 0, 2))
        pieces = lax.all_to_all(pieces, "tp", split_axis=0, concat_axis=0, tiled=True)
        dealt = jnp.transpose(pieces, (1, 0, 2)).reshape(total, -1)
    return hidden, low, w_down, dealt


def gram_kernel(left, right, value, out, by_x, by_y, by_sib, send, recv):
    by = (by_x, by_y, by_sib)

    @pl.when(pl.program_id(0) == 0)
    def _():
        greet()
        for c in phase_one_of(value, by, (send, recv)):
            c.start()

    out[...] = lax.dot_general(
        left[...], right[...], (((0,), (0,)), ((), ())), preferred_element_type=f32
    ).astype(bf16)

    @pl.when(pl.program_id(0) == pl.num_programs(0) - 1)
    def _():
        for c in phase_one_of(value, by, (send, recv)):
            c.wait()


def gram_beside(left, right, value, block, cid):
    total, width = left.shape
    columns = right.shape[1]
    return pl.pallas_call(
        gram_kernel,
        grid=(width // block,),
        in_specs=[pl.BlockSpec((total, block), lambda i: (0, i)), WHOLE, ANY],
        out_specs=[pl.BlockSpec((block, columns), lambda i: (i, 0))] + [ANY] * 3,
        out_shape=[jax.ShapeDtypeStruct((width, columns), bf16)] + same([value]) * 3,
        scratch_shapes=pair(3),
        compiler_params=params(cid),
        cost_estimate=cost(21),
        name="gram_beside",
    )(left, right, value)


def middle_kernel(branch, wo, x, small, middle, normed_all, own, send1, recv1, sem1, *scratch):
    me = greet()
    reduce_steps(me, [(branch, wo)], False, *scratch)
    final, total = scratch[4], scratch[5]

    def make(at):
        value = x[at, :].astype(f32) + summed(total, final, at)
        middle[at, :] = value
        unit, _ = centre(value, layer_epsilon)
        own[at, :] = (unit * small[2:3, :] + small[3:4, :]).astype(bf16)

    gather_as_made(me, make, own, normed_all, send1, recv1, sem1)


def make_middle(branch, wo, x, small, cid):
    rows, width = x.shape
    return pl.pallas_call(
        middle_kernel,
        out_shape=(
            jax.ShapeDtypeStruct((rows, width), f32),
            jax.ShapeDtypeStruct((8, rows, width), bf16),
        ),
        in_specs=[WHOLE] * 4,
        out_specs=(WHOLE, ANY),
        scratch_shapes=gather_scratch(rows, width) + reduce_scratch(rows, width),
        compiler_params=params(cid),
        cost_estimate=cost(85),
        name="make_middle",
    )(branch, wo, x, small)


def back_middle_kernel(
    low_in, weight_in, middle, back_out, small, _after, _more, back_middle, parts, middle_all,
    low, weight, load, own, send1, recv1, sem1, *scratch,
):
    loads = [
        pltpu.make_async_copy(low_in, low, load.at[0]),
        pltpu.make_async_copy(weight_in.at[:, pl.ds(0, weight.shape[1])], weight, load.at[1]),
    ]
    for c in loads:
        c.start()
    me = greet()
    parts[...] = jnp.zeros_like(parts)
    for c in loads:
        c.wait()
    reduce_steps(me, [(low, weight)], True, *scratch)
    final, total = scratch[4], scratch[5]

    def make(at):
        back = summed(total, final, at)
        unit, root = centre(middle[at, :], layer_epsilon)
        parts[0:1, :] += jnp.sum(back * unit, axis=0, keepdims=True)
        parts[1:2, :] += jnp.sum(back, axis=0, keepdims=True)
        value = back_out[at, :].astype(f32) + through_norm(back * small[2:3, :], unit, root)
        back_middle[at, :] = value
        own[at, :] = value.astype(bf16)

    gather_as_made(me, make, own, middle_all, send1, recv1, sem1)


def make_back_middle(low, weight, middle, back_out, small, after, more, cid):
    rows, width = middle.shape
    return pl.pallas_call(
        back_middle_kernel,
        out_shape=(
            jax.ShapeDtypeStruct((rows, width), f32),
            jax.ShapeDtypeStruct((8, width), f32),
            jax.ShapeDtypeStruct((8, rows, width), bf16),
        ),
        in_specs=[ANY, ANY] + [WHOLE] * 3 + [ANY, ANY],
        out_specs=(WHOLE, WHOLE, ANY),
        scratch_shapes=[
            pltpu.VMEM(low.shape, bf16),
            pltpu.VMEM((width, low.shape[1]), bf16),
            pltpu.SemaphoreType.DMA((2,)),
        ]
        + gather_scratch(rows, width)
        + reduce_scratch(rows, width),
        compiler_params=params(cid),
        cost_estimate=cost(90),
        name="make_back_middle",
    )(low, weight, middle, back_out, small, after, more)


def ending_kernel(
    count, low_in, weight_in, hidden_in, down_in, x, back_middle, middle, usable, small, *refs,
):
    refs = list(refs)

    def take(n):
        got = refs[:n]
        del refs[:n]
        return got

    by_x, by_y = take(count), take(count)
    back_input, out, parts = take(3)
    half_low, half_high, sib_x, sib_y, sib_low, sib_high = (take(count) for _ in range(6))
    low, weight, hidden, down, load = take(5)
    two, three = take(2), take(2)
    first, second = take(8), take(8)
    loads = [
        pltpu.make_async_copy(low_in, low, load.at[0]),
        pltpu.make_async_copy(weight_in.at[:, pl.ds(0, weight.shape[1])], weight, load.at[1]),
        pltpu.make_async_copy(hidden_in, hidden, load.at[2]),
        pltpu.make_async_copy(down_in, down, load.at[3]),
    ]
    for c in loads:
        c.start()
    me = greet()
    started = phase_two(me, by_x, by_y, half_low, half_high, sib_x, sib_y, *two)
    parts[...] = jnp.zeros_like(parts)
    loads[0].wait()
    loads[1].wait()
    one = reduce_stages(me, [(low, weight)], True, *first)
    other = reduce_stages(me, [(hidden, down)], False, *second)
    next(one)
    loads[2].wait()
    loads[3].wait()
    next(other)
    next(one)
    next(other)
    for _ in one:
        pass

    @by_rows(x.shape[0])
    def _(at):
        back = summed(first[5], first[4], at)
        unit, root = centre(x[at, :].astype(f32), layer_epsilon)
        parts[0:1, :] += jnp.sum(back * unit, axis=0, keepdims=True)
        parts[1:2, :] += jnp.sum(back, axis=0, keepdims=True)
        value = back_middle[at, :] + through_norm(back * small[0:1, :], unit, root)
        back_input[at, :] = value.astype(bf16)

    for _ in other:
        pass
    for c in started:
        c.wait()
    last = phase_three(me, half_low, half_high, sib_low, sib_high, *three)

    @by_rows(middle.shape[0])
    def _(at):
        value = middle[at, :] + summed(second[5], second[4], at)
        out[at, :] = jnp.where(usable[at, :] > 0.5, value, 0.0).astype(bf16)

    for c in last:
        c.wait()


def make_ending(
    low, weight, hidden, down, x, back_middle, middle, usable, small, by_x, by_y, cid
):
    rows, width = x.shape
    count = len(by_x)
    shapes = (
        [
            jax.ShapeDtypeStruct((rows, width), bf16),
            jax.ShapeDtypeStruct((rows, width), bf16),
            jax.ShapeDtypeStruct((8, width), f32),
        ]
        + same(by_x, True) * 2
        + same(by_x) * 2
        + same(by_x, True) * 2
    )
    out = pl.pallas_call(
        functools.partial(ending_kernel, count),
        out_shape=shapes,
        in_specs=[ANY] * 4 + [WHOLE] * 5 + [ANY] * (2 * count),
        out_specs=[WHOLE] * 3 + [ANY] * (len(shapes) - 3),
        scratch_shapes=[
            pltpu.VMEM(low.shape, bf16),
            pltpu.VMEM((width, low.shape[1]), bf16),
            pltpu.VMEM(hidden.shape, bf16),
            pltpu.VMEM(down.shape, bf16),
            pltpu.SemaphoreType.DMA((4,)),
        ]
        + pair(4 * count)
        + pair(2 * count)
        + reduce_scratch(rows, width)
        + reduce_scratch(rows, width),
        compiler_params=params(cid),
        cost_estimate=cost(100),
        name="make_ending",
    )(
        low, weight, hidden, down, x, back_middle, middle, usable, small,
        *by_x, *by_y,
    )
    rest = out[3:]
    return *out[:3], [rest[i * count : (i + 1) * count] for i in range(6)]


def small_sums_kernel(parts_one, parts_two, _after, sums, parts, turned, far, send_s, recv_s, send_f, recv_f):
    me = greet(True)
    z = lax.axis_index("shard")
    parts[...] = jnp.zeros_like(parts)
    parts[0:2, :] = parts_one[0:2, :]
    parts[2:4, :] = parts_two[0:2, :]
    for i, mask in enumerate((1, 2, 4)):
        c = push(parts, turned.at[i], send_s.at[i], recv_s.at[i], flip(me, mask))
        c.start()
        c.wait()
        parts[...] += turned[i]
    part = parts.shape[1] // lax.axis_size("shard")
    waiting = []
    for k, other in enumerate(others()):
        c = pltpu.make_async_remote_copy(
            src_ref=parts.at[:, pl.ds(pl.multiple_of(other * part, part), part)],
            dst_ref=far.at[k],
            send_sem=send_f.at[k],
            recv_sem=recv_f.at[k],
            device_id={"shard": other},
            device_id_type=MESHID,
        )
        c.start()
        waiting.append(c)
    value = parts[:, pl.ds(pl.multiple_of(z * part, part), part)]
    for k, c in enumerate(waiting):
        c.wait()
        value = value + far[k]
    sums[...] = value


def small_sums(parts_one, parts_two, after, cid):
    width = parts_one.shape[1]
    shards = lax.axis_size("shard")
    return pl.pallas_call(
        small_sums_kernel,
        out_shape=jax.ShapeDtypeStruct((8, width // shards), f32),
        in_specs=[WHOLE, WHOLE, ANY],
        out_specs=WHOLE,
        scratch_shapes=[
            pltpu.VMEM((8, width), f32),
            pltpu.VMEM((3, 8, width), f32),
            pltpu.VMEM((shards - 1, 8, width // shards), f32),
        ]
        + pair(3)
        + pair(shards - 1),
        compiler_params=params(cid),
        cost_estimate=cost(15),
        name="small_sums",
    )(parts_one, parts_two, after)


MASKS = (0, 2, 4, 6, 6, 1, 3, 5, 7, 7)
WHEN = (2, 2, 2, 0, 1, 2, 2, 2, 0, 1)


def in_order(parts):
    value, by_x, by_y, low, high, sib, sib_x, sib_y, sib_low, sib_high = parts
    corner, sib_corner = jnp.concatenate([low, high]), jnp.concatenate([sib_low, sib_high])
    stacked = jnp.stack([value, sib, by_x, sib_x, by_y, sib_y, corner, sib_corner])
    return jnp.take(stacked, jnp.arange(8) ^ lax.axis_index("tp"), axis=0)


def collect_kernel(own, _after, out, send, recv, local_sem):
    gather_all(greet(), own, out, send, recv, local_sem)


def plane_collect(value, after, cid):
    return pl.pallas_call(
        collect_kernel,
        out_shape=jax.ShapeDtypeStruct((8,) + value.shape, value.dtype),
        in_specs=[ANY, ANY],
        out_specs=ANY,
        scratch_shapes=gather_scratch(*value.shape)[1:],
        compiler_params=params(cid),
        cost_estimate=cost(22),
        name="plane_collect",
    )(value, after)


def widen_two_kernel(steps, shards, *refs):
    t = lax.axis_index("tp")
    late = (pl.program_id(0) >= steps // 2).astype(jnp.int32)
    seconds, downs, outs = refs[:10], refs[10:20], refs[20]
    gelu, up, down, out = refs[21:]
    out[...] = outs[...].astype(f32)
    unit = gelu.shape[1] // (8 * shards)

    def store(i):
        place = flip(t, MASKS[i])
        down[place] = downs[i][...].astype(f32)
        for z in range(shards):
            at = pl.ds(pl.multiple_of((8 * z + place) * unit, unit), unit)
            gelu[:, at] = seconds[i][:, z * unit : (z + 1) * unit].astype(f32)
            up[:, at] = seconds[i][:, (shards + z) * unit : (shards + z + 1) * unit].astype(f32)

    for i in range(10):
        if WHEN[i] == 2:
            store(i)
        else:

            @pl.when(late == WHEN[i])
            def _():
                store(i)


def widen_two(seconds, downs, outs, shards):
    rows, columns = seconds[0].shape
    count, width = downs[0].shape
    steps = 4

    def row_at(which, i):
        half = steps // 2
        return (i, jnp.minimum(i, half - 1), jnp.maximum(i - half, 0))[(which + 1) % 3]

    def specs(parts):
        return [
            pl.BlockSpec(
                (parts[0].shape[0] // steps, parts[0].shape[1]),
                functools.partial(lambda w, i: (row_at(w, i), 0), w),
            )
            for w in WHEN
        ]

    units = jax.ShapeDtypeStruct((rows, 4 * columns), f32)
    stack = jax.ShapeDtypeStruct((8, count, width), f32)
    gelu, up, down, out = pl.pallas_call(
        functools.partial(widen_two_kernel, steps, shards),
        grid=(steps,),
        in_specs=specs(seconds)
        + specs(downs)
        + [pl.BlockSpec((8, count // steps, width), lambda i: (0, i, 0))],
        out_specs=[pl.BlockSpec((rows // steps, 4 * columns), lambda i: (i, 0))] * 2
        + [pl.BlockSpec((8, count // steps, width), lambda i: (0, i, 0))] * 2,
        out_shape=[units, units, stack, stack],
        compiler_params=params(),
        cost_estimate=cost(25),
        name="widen_two",
    )(*seconds, *downs, outs)
    return gelu, up, down.reshape(8 * count, width), out.reshape(8 * count, width)


def widen_one_kernel(edges, parts, _after, *goals):
    for goal, (begin, end) in zip(goals, zip(edges, edges[1:])):
        size = end - begin
        for i in range(8):
            goal[:, i * size : (i + 1) * size] = parts[i, :, begin:end].astype(f32)


def widen_one(parts, edges, after, name):
    _, rows, columns = parts.shape
    sizes = [b - a for a, b in zip(edges, edges[1:])]
    block = 64
    return pl.pallas_call(
        functools.partial(widen_one_kernel, edges),
        grid=(rows // block,),
        in_specs=[pl.BlockSpec((8, block, columns), lambda i: (0, i, 0)), ANY],
        out_specs=[pl.BlockSpec((block, 8 * size), lambda i: (i, 0)) for size in sizes],
        out_shape=[jax.ShapeDtypeStruct((rows, 8 * size), f32) for size in sizes],
        compiler_params=params(),
        cost_estimate=cost(14),
        name=name,
    )(parts, after)


def local(
    tokens,
    cotangent,
    token_order,
    lengths,
    query_weight,
    key_weight,
    value_weight,
    gate_weight,
    out_weight,
    gelu_weight,
    up_weight,
    down_weight,
    gain_one,
    shift_one,
    gain_two,
    shift_two,
):
    every = ("outer", "tp", "shard")
    device_count = lax.axis_size(every)
    device_index = lax.axis_index(every)
    outer, tp, shards = lax.axis_size("outer"), lax.axis_size("tp"), lax.axis_size("shard")
    t, z = lax.axis_index("tp"), lax.axis_index("shard")
    rows, width = tokens.shape
    packs = lengths.shape[0]
    pack_rows = rows // packs
    group_rows = tp * rows
    group_packs = tp * packs

    own_order = lax.dynamic_slice_in_dim(token_order, device_index * rows, rows)
    target = own_order // rows
    places = jnp.arange(rows, dtype=jnp.int32)
    before = (target[None, :] < target[:, None]) | (
        (target[None, :] == target[:, None]) & (places[None, :] < places[:, None])
    )
    send_place = jnp.sum(before.astype(jnp.int32), axis=1)
    send_mix = (send_place[None, :] == places[:, None]).astype(bf16)
    loader_ids = jnp.arange(token_order.shape[0], dtype=jnp.int32)
    slot_targets = device_index * rows + places
    origin = jnp.sum(
        jnp.where(token_order[None, :] == slot_targets[:, None], loader_ids[None, :], 0), axis=1
    )
    arrive_place = jnp.sum((origin[None, :] < origin[:, None]).astype(jnp.int32), axis=1)
    work_mix = (arrive_place[:, None] == places[None, :]).astype(bf16)

    def exchange(value):
        return lax.all_to_all(
            value.reshape(device_count, rows // device_count, value.shape[1]),
            every,
            split_axis=0,
            concat_axis=0,
            tiled=True,
        ).reshape(rows, value.shape[1])

    piece = rows // device_count
    part = gain_one.shape[0]
    extra = jnp.concatenate(
        [gain_one, shift_one, gain_two, shift_two, lengths.reshape(-1).astype(bf16)]
    )
    extra_columns = -(-extra.shape[0] // (piece * 128)) * 128
    extra = jnp.pad(extra, (0, piece * extra_columns - extra.shape[0]))
    extra = jnp.tile(extra.reshape(piece, extra_columns), (device_count, 1))
    came = exchange(
        jnp.concatenate([forward_dot(send_mix, tokens).astype(bf16), extra], axis=1)
    )
    sent_back = forward_dot(send_mix, cotangent).astype(bf16)
    came_back = exchange(sent_back)
    arrived = came[:, width:].reshape(outer, tp, shards, -1)
    small = jnp.transpose(arrived[0, 0, :, : 4 * part].reshape(shards, 4, part), (1, 0, 2))
    small = small.reshape(4, width).astype(f32)
    small = jnp.concatenate([small, jnp.zeros((4, width), f32)], axis=0)
    all_lengths = arrived[lax.axis_index("outer"), :, z, 4 * part : 4 * part + lengths.size]
    all_lengths = all_lengths.reshape(group_packs, -1).astype(f32).astype(jnp.int32)

    def along_z(piece):
        return lax.all_gather(piece, "shard", axis=0, tiled=True)

    def cut(weight):
        part = weight.shape[1] // tp
        return lax.dynamic_slice_in_dim(weight, t * part, part, axis=1)

    out_unit = out_weight.shape[0] // tp
    unit = down_weight.shape[0] // tp
    piece_rows = query_weight.shape[0]
    key_part, value_part = query_weight.shape[1] // tp, value_weight.shape[1] // tp
    edges = (0, key_part, 2 * key_part, 2 * key_part + value_part)
    first_size = 2 * key_part + 2 * value_part
    hidden_part = shards * unit

    def fold(value):
        cuts = piece_rows // value.shape[0]
        value = value.reshape(value.shape[0], cuts, width // cuts)
        return jnp.transpose(value, (1, 0, 2)).reshape(piece_rows, width // cuts)

    def unfold(value, count):
        cuts = piece_rows // count
        value = value.reshape(shards, cuts, count, width // cuts)
        return jnp.transpose(value, (0, 2, 1, 3)).reshape(shards, count, width)

    out_piece = lax.dynamic_slice_in_dim(out_weight, t * out_unit, out_unit, axis=0)
    w_one = along_z(
        jnp.concatenate(
            [cut(w) for w in (query_weight, key_weight, value_weight, gate_weight)]
            + [fold(out_piece)],
            axis=1,
        )
    )
    ends = jnp.cumsum(lengths, axis=1, dtype=jnp.int32)[:, -2]
    usable = (jnp.arange(pack_rows, dtype=jnp.int32)[None, :] < ends[:, None]).astype(f32)
    usable = usable.reshape(rows, 1)
    x, normed = entry(came, work_mix, small, 0)
    def unit_columns(weight):
        return [
            lax.dynamic_slice_in_dim(weight, (k * tp + t) * unit, unit, axis=1)
            for k in range(shards)
        ]

    down_piece = lax.dynamic_slice_in_dim(down_weight, t * unit, unit, axis=0)
    second_piece = lax.optimization_barrier(
        jnp.concatenate(
            unit_columns(gelu_weight) + unit_columns(up_weight) + [fold(down_piece)], axis=1
        )
    )
    w_two = along_z(second_piece + jnp.isnan(x[0, 0]).astype(bf16))
    back_out, back_low = entry_back(came_back, work_mix, usable, x, 7)
    normed, back_low = normed.reshape(group_rows, width), back_low.reshape(group_rows, width)
    cosine, sine, decays, _ = pack_tables(all_lengths, pack_rows, t + jnp.arange(1))
    cosine, sine = cosine.reshape(group_rows, -1), sine.reshape(group_rows, -1)
    decays = decays[0]
    out_pieces = unfold(w_one[:, first_size:], out_unit)
    q_rot, k_rot, v_low, weights_low, gating, retained, branch, wo = retain(
        normed, w_one, value_part, cosine, sine, decays, out_pieces, rows, 1
    )
    wo = wo.reshape(shards * out_unit, width)
    middle, normed_two = make_middle(branch, wo, x, small, 2)
    normed_two = normed_two.reshape(group_rows, width)

    hidden, second_low, w_down, branch_rows = feed(
        normed_two, back_low, w_two, branch, hidden_part, shards, rows, 6
    )
    down_gram = gram_rows(hidden, back_low).astype(bf16)
    second_gram = gram_rows(normed_two, second_low).astype(bf16)

    def to_owner(value):
        part = lax.psum_scatter(value, "shard", scatter_dimension=0, tiled=True)
        return lax.psum(part, "outer") if outer > 1 else part

    down_sum, second_sum = to_owner(down_gram), to_owner(second_gram)
    back_middle, parts_two, middle_low = make_back_middle(
        second_low, w_two, middle, back_out, small, down_gram, second_gram, 3
    )
    middle_low = middle_low.reshape(group_rows, width)
    out_sum = to_owner(gram_rows(branch_rows, middle_low).astype(bf16))
    first_low, *down_by = retain_back(
        middle_low, wo, q_rot, k_rot, v_low, weights_low, gating, retained, cosine, sine, decays,
        down_sum, rows, 8,
    )
    first_gram, *second_by = gram_beside(normed, first_low, second_sum, 256, 9)
    first_sum = to_owner(first_gram)
    by_x, by_y, by_sib = ([a, b] for a, b in zip(second_by, down_by))
    back_inputs, ending, parts_one, groups = make_ending(
        first_low, w_one, hidden, w_down, x, back_middle, middle, usable, small, by_x, by_y, 5
    )
    outs = plane_collect(out_sum, ending, 10)
    low, high, sib_x, sib_y, sib_low, sib_high = groups
    seconds, downs = (
        [
            value, by_x[k], by_y[k], low[k], high[k],
            by_sib[k], sib_x[k], sib_y[k], sib_low[k], sib_high[k],
        ]
        for k, value in enumerate((second_sum, down_sum))
    )

    if unit % 128 == 0:
        gelu_gradient, up_gradient, down_gradient, out_gradient = widen_two(
            seconds, downs, outs, shards
        )
    else:
        down_gradient = in_order(downs).reshape(-1, width).astype(f32)
        out_gradient = outs.reshape(-1, width).astype(f32)
        both = in_order(seconds).reshape(tp, piece_rows, 2, shards, unit)
        both = jnp.transpose(both, (2, 1, 3, 0, 4)).reshape(2, piece_rows, -1).astype(f32)
        gelu_gradient, up_gradient = both[0], both[1]
    nothing = parts_one[5, 0].astype(bf16) + jnp.isnan(outs[0, 0, 0]).astype(bf16)
    firsts = lax.all_gather(first_sum + nothing, "tp", axis=0)
    sums = small_sums(parts_one, parts_two, down_gradient, 11)
    query_gradient, key_gradient, value_gradient, gate_gradient = widen_one(
        firsts, edges + (first_size,), sums, "widen_one"
    )
    smalls = lax.psum(sums, "outer") if outer > 1 else sums

    home = jnp.concatenate([ending, back_inputs], axis=1)
    home = exchange(gram_rows(work_mix, home).astype(bf16))
    home = gram_rows(send_mix, home).astype(bf16)
    result, token_gradient = home[:, :width], home[:, width:]
    return (
        result,
        token_gradient,
        query_gradient,
        key_gradient,
        value_gradient,
        gate_gradient,
        out_gradient,
        gelu_gradient,
        up_gradient,
        down_gradient,
        smalls[0],
        smalls[1],
        smalls[2],
        smalls[3],
    )


def solution(mesh):
    tp = math.gcd(mesh.shape["rep"], HEADS)
    grid = mesh.devices.reshape(mesh.shape["rep"] // tp, tp, mesh.shape["shard"])
    cube = Mesh(grid, ("outer", "tp", "shard"))
    tokens_at = P(("outer", "tp", "shard"), None)
    weights_at = P("shard", None)
    vectors_at = P("shard")
    in_specs = (tokens_at, tokens_at, P(), tokens_at) + (weights_at,) * 8 + (vectors_at,) * 4
    out_specs = (tokens_at, tokens_at) + (weights_at,) * 8 + (vectors_at,) * 4
    return jax.shard_map(local, mesh=cube, in_specs=in_specs, out_specs=out_specs, check_vma=False)
```

```python
import functools
import math

import jax
import jax.numpy as jnp
from jax import lax
from jax.experimental import pallas as pl
from jax.experimental.pallas import tpu as pltpu
from jax.sharding import Mesh, PartitionSpec as P

HEADS = 8
KH = 256

layer_epsilon = 1e-05
head_epsilon = 1.0
rotary_base = 10000.0
bf16 = jnp.bfloat16
f32 = jnp.float32
MESHID = pl.DeviceIdType.MESH


def pack_tables(lengths, pack_rows, head_ids):
    entries = lengths.shape[1]
    slot_ids = jnp.arange(pack_rows, dtype=jnp.int32)
    seq_ends = jnp.cumsum(lengths, axis=1, dtype=jnp.int32)
    seq_starts = seq_ends - lengths
    segment = jnp.sum(
        (slot_ids[None, :, None] >= seq_ends[:, None, :]).astype(jnp.int32), axis=2, dtype=jnp.int32
    )
    owners = segment[:, :, None] == jnp.arange(entries, dtype=jnp.int32)[None, None, :]
    begins = jnp.sum(jnp.where(owners, seq_starts[:, None, :], 0), axis=2, dtype=jnp.int32)
    places = (slot_ids[None, :] - begins).astype(f32)
    usable = segment < entries - 1
    half_size = KH // 2
    frequency = jnp.power(
        f32(rotary_base), -jnp.arange(half_size, dtype=f32) / f32(half_size - 1)
    )
    angles = places[:, :, None] * frequency
    cosine_table = jnp.cos(angles)
    sine_table = jnp.sin(angles)
    lag_steps = slot_ids[:, None] - slot_ids[None, :]
    linked = (
        (segment[:, :, None] == segment[:, None, :])
        & (lag_steps[None] >= 0)
        & usable[:, None, :]
    )
    log_rates = jnp.log(1.0 - jnp.power(f32(2.0), -5.0 - head_ids.astype(f32)))
    powers = jnp.exp(log_rates[:, None, None] * jnp.maximum(lag_steps, 0).astype(f32)[None])
    decays = jnp.where(linked[None], powers[:, None], f32(0.0))
    return cosine_table, sine_table, decays, usable


def gram_rows(leading, trailing):
    return lax.dot_general(
        leading, trailing, (((0,), (0,)), ((), ())), preferred_element_type=f32
    )


def back_through(incoming, matrix):
    return lax.dot_general(
        incoming, matrix, (((1,), (1,)), ((), ())), preferred_element_type=f32
    )


def forward_dot(inputs, matrix):
    return jnp.dot(inputs, matrix, preferred_element_type=f32)


def gelu_parts(v):
    c = f32(math.sqrt(2.0 / math.pi))
    t = jnp.tanh(c * (v + 0.044715 * v * v * v))
    value = 0.5 * v * (1.0 + t)
    slope = 0.5 * (1.0 + t) + 0.5 * v * (1.0 - t * t) * c * (1.0 + 3.0 * 0.044715 * v * v)
    return value, slope


def flip(me, mask):
    for bit in (1, 2, 4):
        if mask & bit:
            me = me + bit - 2 * bit * ((me // bit) % 2)
    return me


def greet(far=False):
    me = lax.axis_index("tp")
    barrier = pltpu.get_barrier_semaphore()
    for mask in (1, 2, 4):
        pl.semaphore_signal(
            barrier, inc=1, device_id={"tp": flip(me, mask)}, device_id_type=MESHID
        )
    count = 3
    if far:
        for other in others():
            pl.semaphore_signal(barrier, inc=1, device_id={"shard": other}, device_id_type=MESHID)
            count += 1
    pl.semaphore_wait(barrier, count)
    return me


def others():
    shards = lax.axis_size("shard")
    return [(lax.axis_index("shard") + k) % shards for k in range(1, shards)]


def push(source, goal, send, recv, peer):
    return pltpu.make_async_remote_copy(
        src_ref=source, dst_ref=goal, send_sem=send, recv_sem=recv,
        device_id={"tp": peer}, device_id_type=MESHID,
    )


def gather_begin(me, own, out, send, recv, halves=(True, True), first=None):
    half = own.shape[0] // 2
    xn, yn = flip(me, 2), flip(me, 4)
    low, high = pl.ds(0, half), pl.ds(half, half)
    first = first if first is not None else [None] * 5
    ways = ((low, xn), (high, yn), (high, xn), (low, yn))
    for i in (0, 3, 1, 2):
        part, peer = ways[i]
        if halves[0 if part is low else 1]:
            first[i] = push(own.at[part], out.at[me, part], send.at[i], recv.at[i], peer)
            first[i].start()
    if halves[1]:
        first[4] = push(own, out.at[me], send.at[4], recv.at[4], flip(me, 1))
        first[4].start()
    return first


def gather_end(me, own, out, send, recv, first):
    half = own.shape[0] // 2
    sib, xn, yn, dn = flip(me, 1), flip(me, 2), flip(me, 4), flip(me, 6)
    low, high = pl.ds(0, half), pl.ds(half, half)
    started = list(first)

    def on(slot, part, peer):
        i = len(started)
        place = out.at[slot, part]
        c = push(place, place, send.at[i], recv.at[i], peer)
        c.start()
        started.append(c)
        return c

    first[0].wait_recv()
    d_low = on(xn, low, yn)
    first[1].wait_recv()
    d_high = on(yn, high, xn)
    on(xn, low, sib)
    on(yn, high, sib)
    first[2].wait_recv()
    on(xn, high, sib)
    first[3].wait_recv()
    on(yn, low, sib)
    d_low.wait_recv()
    on(dn, low, sib)
    d_high.wait_recv()
    on(dn, high, sib)
    for i in (4, 7, 8, 9, 10, 11, 12):
        started[i].wait_recv()
    for c in started:
        c.wait_send()


def gather_steps(me, own, out, send, recv):
    gather_end(me, own, out, send, recv, gather_begin(me, own, out, send, recv))


COLS = 512


def reduce_stages(me, pairs, transposed, tosib, fromsib, hold, hop, final, total, send, recv):
    rows, width = total.shape
    half = rows // 2
    sib, xn, yn = flip(me, 1), flip(me, 2), flip(me, 4)
    low, high = pl.ds(0, half), pl.ds(half, half)

    def product(block, tile):
        acc = None
        for act, weight in pairs:
            left = act[pl.ds(pl.multiple_of(block * rows, rows), rows), :]
            if transposed:
                part = lax.dot_general(
                    left, weight[pl.ds(pl.multiple_of(tile * COLS, COLS), COLS), 0 : act.shape[1]],
                    (((1,), (1,)), ((), ())), preferred_element_type=f32,
                )
            else:
                part = jnp.dot(
                    left, weight[:, pl.ds(pl.multiple_of(tile * COLS, COLS), COLS)],
                    preferred_element_type=f32,
                )
            acc = part if acc is None else acc + part
        return acc

    def cp(i, src, goal, peer):
        return push(src, goal, send.at[i], recv.at[i], peer)

    masks = (6, 2, 4, 0)
    over, out = [], {}

    def for_sibling(slot):
        block = flip(me, masks[slot] ^ 1)

        @pl.loop(0, width // COLS)
        def _(tile):
            at = pl.ds(pl.multiple_of(tile * COLS, COLS), COLS)
            tosib[slot, :, at] = product(block, tile).astype(bf16)

        c = cp(slot, tosib.at[slot], fromsib.at[slot], sib)
        c.start()
        over.append(c)

    def for_own_core(slot):
        block = flip(me, masks[slot])
        over[slot].wait_recv()

        @pl.loop(0, width // COLS)
        def _(tile):
            at = pl.ds(pl.multiple_of(tile * COLS, COLS), COLS)
            value = product(block, tile) + fromsib[slot, :, at].astype(f32)
            if slot < 3:
                hold[slot, :, at] = value.astype(bf16)
            else:
                total[:, at] = value

    for_sibling(0)
    for_sibling(1)
    for_own_core(0)
    dx = cp(4, hold.at[0, low], hop.at[0], xn)
    dy = cp(5, hold.at[0, high], hop.at[1], yn)
    dx.start()
    dy.start()
    for_sibling(2)
    for_own_core(1)
    xa = cp(6, hold.at[1, low], final.at[0, low], xn)
    xa.start()
    for_sibling(3)
    for_own_core(2)
    yb = cp(7, hold.at[2, high], final.at[1, high], yn)
    yb.start()
    for_own_core(3)
    yield
    dy.wait_recv()
    hold[1, high] = (hold[1, high].astype(f32) + hop[1].astype(f32)).astype(bf16)
    xb = cp(8, hold.at[1, high], final.at[0, high], xn)
    xb.start()
    dx.wait_recv()
    hold[2, low] = (hold[2, low].astype(f32) + hop[0].astype(f32)).astype(bf16)
    ya = cp(9, hold.at[2, low], final.at[1, low], yn)
    ya.start()
    yield
    xa.wait_recv()
    yb.wait_recv()
    xb.wait_recv()
    ya.wait_recv()
    for c in over + [dx, dy, xa, yb, xb, ya]:
        c.wait_send()


def reduce_steps(*args):
    for _ in reduce_stages(*args):
        pass


def summed(total, final, at):
    return total[at, :] + final[0, at, :].astype(f32) + final[1, at, :].astype(f32)


def reduce_scratch(rows, width):
    return [
        pltpu.VMEM((4, rows, width), bf16),
        pltpu.VMEM((4, rows, width), bf16),
        pltpu.VMEM((3, rows, width), bf16),
        pltpu.VMEM((2, rows // 2, width), bf16),
        pltpu.VMEM((2, rows, width), bf16),
        pltpu.VMEM((rows, width), f32),
        pltpu.SemaphoreType.DMA((10,)),
        pltpu.SemaphoreType.DMA((10,)),
    ]


CHUNK = 32


def cost(us):
    return pl.CostEstimate(flops=int(us * 1e9), bytes_accessed=int(us * 3e6), transcendentals=0)


def params(cid=None):
    if cid is None:
        return pltpu.CompilerParams(vmem_limit_bytes=60 << 20)
    return pltpu.CompilerParams(collective_id=cid, has_side_effects=True, vmem_limit_bytes=60 << 20)


def by_rows(count, begin=0):
    def run(body):
        @pl.loop(begin // CHUNK, count // CHUNK)
        def _(i):
            body(pl.ds(pl.multiple_of(i * CHUNK, CHUNK), CHUNK))

    return run


def gather_as_made(me, make, own, out, send, recv, local_sem):
    rows = own.shape[0]
    by_rows(rows // 2)(make)
    first = gather_begin(me, own, out, send, recv, (True, False))
    by_rows(rows, rows // 2)(make)
    gather_begin(me, own, out, send, recv, (False, True), first)
    mine = pltpu.make_async_copy(own, out.at[me], local_sem)
    mine.start()
    gather_end(me, own, out, send, recv, first)
    mine.wait()


def centre(value, epsilon):
    average = jnp.mean(value, axis=-1, keepdims=True)
    centred = value - average
    spread = jnp.mean(centred * centred, axis=-1, keepdims=True)
    root = lax.rsqrt(spread + epsilon)
    return centred * root, root


def through_norm(e, unit, root):
    return root * (
        e - jnp.mean(e, axis=-1, keepdims=True) - unit * jnp.mean(e * unit, axis=-1, keepdims=True)
    )


def leading(rows, columns):
    return pl.BlockSpec((rows, columns), lambda *_: (0, 0))


ANY = pl.BlockSpec(memory_space=pl.ANY)
WHOLE = pl.BlockSpec(memory_space=pltpu.VMEM)


def gather_scratch(rows, width):
    return [
        pltpu.VMEM((rows, width), bf16),
        pltpu.SemaphoreType.DMA((13,)),
        pltpu.SemaphoreType.DMA((13,)),
        pltpu.SemaphoreType.DMA,
    ]


def gather_all(me, own, out, send, recv, local_sem):
    mine = pltpu.make_async_copy(own, out.at[me], local_sem)
    mine.start()
    gather_steps(me, own, out, send, recv)
    mine.wait()


def entry_kernel(came, mix, small, x_out, normed_all, own, send, recv, sem):
    me = greet()
    width = x_out.shape[1]

    @by_rows(came.shape[0])
    def _(at):
        value = jnp.dot(mix[at, :], came[:, :width], preferred_element_type=f32)
        x_out[at, :] = value.astype(bf16)
        unit, _ = centre(value, layer_epsilon)
        own[at, :] = (unit * small[0:1, :] + small[1:2, :]).astype(bf16)

    gather_all(me, own, normed_all, send, recv, sem)


def entry(came, mix, small, cid):
    rows, width = came.shape[0], small.shape[1]
    return pl.pallas_call(
        entry_kernel,
        out_shape=(
            jax.ShapeDtypeStruct((rows, width), bf16),
            jax.ShapeDtypeStruct((8, rows, width), bf16),
        ),
        in_specs=[WHOLE] * 3,
        out_specs=(WHOLE, ANY),
        scratch_shapes=gather_scratch(rows, width),
        compiler_params=params(cid),
        cost_estimate=cost(50),
        name="entry",
    )(came, mix, small)


def entry_back_kernel(came, mix, usable, _after, back_out, back_all, own, send, recv, sem):
    me = greet()

    @by_rows(came.shape[0])
    def _(at):
        value = jnp.dot(mix[at, :], came[...], preferred_element_type=f32)
        value = jnp.where(usable[at, :] > 0.5, value, 0.0).astype(bf16)
        back_out[at, :] = value
        own[at, :] = value

    gather_all(me, own, back_all, send, recv, sem)


def entry_back(came, mix, usable, after, cid):
    rows, width = came.shape
    return pl.pallas_call(
        entry_back_kernel,
        out_shape=(
            jax.ShapeDtypeStruct((rows, width), bf16),
            jax.ShapeDtypeStruct((8, rows, width), bf16),
        ),
        in_specs=[WHOLE] * 3 + [ANY],
        out_specs=(WHOLE, ANY),
        scratch_shapes=gather_scratch(rows, width),
        compiler_params=params(cid),
        cost_estimate=cost(45),
        name="entry_back",
    )(came, mix, usable, after)


def deal_plan(back, count):
    heads = HEADS // count
    me = lax.axis_index("tp")
    spread = [i * heads + me // count for i in range(count)]
    packed = [(me % heads) * count + i for i in range(count)]
    goals, sources = (packed, spread) if back else (spread, packed)
    return me, goals, sources, (me // heads if back else me % count), me // count == me % heads


def deal_start(back, count, source, goal, send, recv, local_sem):
    me, goals, sources, slot, inside = deal_plan(back, count)
    barrier = pltpu.get_barrier_semaphore()
    for i in range(count):

        @pl.when(sources[i] != me)
        def _():
            pl.semaphore_signal(
                barrier, inc=1, device_id={"tp": sources[i]}, device_id_type=MESHID
            )

    pl.semaphore_wait(barrier, jnp.where(inside, count - 1, count))
    for i in range(count):

        @pl.when(goals[i] == me)
        def _():
            pltpu.make_async_copy(source(i), goal(slot), local_sem).start()

        @pl.when(goals[i] != me)
        def _():
            push(source(i), goal(slot), send.at[i], recv.at[slot], goals[i]).start()


def deal_wait(back, count, source, goal, send, recv, local_sem):
    me, goals, sources, slot, _ = deal_plan(back, count)
    for i in range(count):

        @pl.when(goals[i] == me)
        def _():
            pltpu.make_async_copy(source(i), goal(slot), local_sem).wait()

        @pl.when(goals[i] != me)
        def _():
            push(source(i), goal(slot), send.at[i], recv.at[slot], goals[i]).wait_send()

        @pl.when(sources[i] != me)
        def _():
            push(source(i), goal(i), send.at[i], recv.at[i], sources[i]).wait_recv()


def blocks(ref):
    return lambda i: ref.at[i]


def column_blocks(ref, size):
    return lambda i: ref.at[:, pl.ds(pl.multiple_of(i * size, size), size)]


def deal_scratch(count):
    return [
        pltpu.SemaphoreType.DMA((count,)),
        pltpu.SemaphoreType.DMA((count,)),
        pltpu.SemaphoreType.DMA,
    ]


def phase_one_copies(me, values, by_x, by_y, by_sib, send, recv):
    copies = []
    for k, value in enumerate(values):
        for i, (goal, mask) in enumerate(((by_x, 2), (by_y, 4), (by_sib, 1))):
            n = 3 * k + i
            copies.append(push(value, goal[k], send.at[n], recv.at[n], flip(me, mask)))
    return copies


def phase_one(*args):
    copies = phase_one_copies(*args)
    for c in copies:
        c.start()
    return copies


def phase_two(me, by_x, by_y, low, high, sib_x, sib_y, send, recv):
    copies = []
    for k in range(len(by_x)):
        half = by_x[k].shape[0] // 2
        for i, (source, goal, mask) in enumerate(
            (
                (by_x[k].at[pl.ds(0, half)], low[k], 4),
                (by_y[k].at[pl.ds(half, half)], high[k], 2),
                (by_x[k], sib_x[k], 1),
                (by_y[k], sib_y[k], 1),
            )
        ):
            n = 4 * k + i
            copies.append(push(source, goal, send.at[n], recv.at[n], flip(me, mask)))
    for c in copies:
        c.start()
    return copies


def phase_three(me, low, high, sib_low, sib_high, send, recv):
    copies = []
    for k in range(len(low)):
        for i, (source, goal) in enumerate(((low[k], sib_low[k]), (high[k], sib_high[k]))):
            n = 2 * k + i
            copies.append(push(source, goal, send.at[n], recv.at[n], flip(me, 1)))
    for c in copies:
        c.start()
    return copies


def pair(count):
    return [pltpu.SemaphoreType.DMA((count,)), pltpu.SemaphoreType.DMA((count,))]


def same(values, halves=False):
    return [
        jax.ShapeDtypeStruct((v.shape[0] // 2 if halves else v.shape[0], v.shape[1]), v.dtype)
        for v in values
    ]


def turn(value, cosine, sine):
    half = value.shape[-1] // 2
    a, b = value[:, :half], value[:, half:]
    return jnp.concatenate([a * cosine - b * sine, a * sine + b * cosine], axis=1)


def retain_kernel(
    normed, weight, cosine, sine, decays, pieces,
    q_out, k_out, v_out, w_out, g_out, r_out, branch, wo, *sems
):
    @pl.when(pl.program_id(0) == 0)
    def _():
        deal_start(False, pieces.shape[0], blocks(pieces), blocks(wo), *sems)

    packs, span = decays.shape[0], decays.shape[1]
    value_at = 2 * KH
    gate_at = value_at + v_out.shape[1]
    rows = normed[...]

    def project(begin, size):
        return jnp.dot(rows, weight[:, begin : begin + size], preferred_element_type=f32)

    q_out[...] = turn(project(0, KH), cosine[...], sine[...]).astype(bf16)
    k_out[...] = (turn(project(KH, KH), cosine[...], sine[...]) * KH ** (-0.5)).astype(bf16)
    v_out[...] = project(value_at, v_out.shape[1]).astype(bf16)
    g_out[...] = project(gate_at, g_out.shape[1])
    for p in range(packs):
        at = pl.ds(p * span, span)
        scores = lax.dot_general(
            q_out[at, :], k_out[at, :], (((1,), (1,)), ((), ())), preferred_element_type=f32
        )
        low = (scores * decays[p]).astype(bf16)
        w_out[p] = low
        retained = jnp.dot(low, v_out[at, :], preferred_element_type=f32)
        r_out[at, :] = retained
        unit, _ = centre(retained, head_epsilon)
        gating = g_out[at, :]
        branch[at, :] = (gating * jax.nn.sigmoid(gating) * unit).astype(bf16)

    @pl.when(pl.program_id(0) == pl.num_programs(0) - 1)
    def _():
        deal_wait(False, pieces.shape[0], blocks(pieces), blocks(wo), *sems)


def retain(normed, weight, value_size, cosine, sine, decays, pieces, block, cid):
    total, width = normed.shape
    span = decays.shape[1]
    grid = total // block
    row = lambda w: pl.BlockSpec((block, w), lambda i: (i, 0))
    square = pl.BlockSpec((block // span, span, span), lambda i: (i, 0, 0))
    flat = lambda w, kind: jax.ShapeDtypeStruct((total, w), kind)
    return pl.pallas_call(
        retain_kernel,
        grid=(grid,),
        in_specs=[
            row(width), leading(width, 2 * KH + 2 * value_size), row(KH // 2), row(KH // 2), square,
            ANY,
        ],
        out_specs=(
            row(KH), row(KH), row(value_size), square, row(value_size), row(value_size),
            row(value_size), ANY,
        ),
        out_shape=(
            flat(KH, bf16), flat(KH, bf16), flat(value_size, bf16),
            jax.ShapeDtypeStruct(decays.shape, bf16), flat(value_size, f32),
            flat(value_size, f32), flat(value_size, bf16),
            jax.ShapeDtypeStruct(pieces.shape, bf16),
        ),
        scratch_shapes=deal_scratch(pieces.shape[0]),
        compiler_params=params(cid),
        cost_estimate=cost(24),
        name="retain",
    )(normed, weight, cosine, sine, decays, pieces)


def phase_one_of(value, by, sems):
    return phase_one_copies(lax.axis_index("tp"), [value], by[:1], by[1:2], by[2:], *sems)


def retain_back_kernel(
    middle_low, wo, q_in, k_in, v_in, w_in, g_in, r_in, cosine, sine, decays, value,
    low, by_x, by_y, by_sib, *sems
):
    by = (by_x, by_y, by_sib)

    @pl.when(pl.program_id(0) == 0)
    def _():
        greet()
        for c in phase_one_of(value, by, sems):
            c.start()

    packs, span = decays.shape[0], decays.shape[1]
    value_at = 2 * KH
    value_size = v_in.shape[1]
    gate_at = value_at + value_size
    back_branch = lax.dot_general(
        middle_low[...], wo[...], (((1,), (1,)), ((), ())), preferred_element_type=f32
    )
    cols = (((0,), (0,)), ((), ()))
    last = (((1,), (1,)), ((), ()))
    for p in range(packs):
        at = pl.ds(p * span, span)
        bb = back_branch[p * span : (p + 1) * span]
        unit, root = centre(r_in[at, :], head_epsilon)
        gating = g_in[at, :]
        sigma = jax.nn.sigmoid(gating)
        low[at, gate_at:] = (bb * unit * (sigma * (1.0 + gating * (1.0 - sigma)))).astype(bf16)
        retained_low = through_norm(bb * (gating * sigma), unit, root).astype(bf16)
        back_weights = lax.dot_general(retained_low, v_in[at, :], last, preferred_element_type=f32)
        low[at, value_at:gate_at] = lax.dot_general(
            w_in[p], retained_low, cols, preferred_element_type=f32
        ).astype(bf16)
        back_scores = (back_weights * decays[p]).astype(bf16)
        back_q = jnp.dot(back_scores, k_in[at, :], preferred_element_type=f32)
        back_k = lax.dot_general(back_scores, q_in[at, :], cols, preferred_element_type=f32)
        low[at, :KH] = turn(back_q, cosine[at, :], -sine[at, :]).astype(bf16)
        low[at, KH:value_at] = (turn(back_k, cosine[at, :], -sine[at, :]) * KH ** (-0.5)).astype(bf16)

    @pl.when(pl.program_id(0) == pl.num_programs(0) - 1)
    def _():
        for c in phase_one_of(value, by, sems):
            c.wait()


def retain_back(middle_low, wo, q, k, v, w, g, r, cosine, sine, decays, value, block, cid):
    total, width = middle_low.shape
    span = decays.shape[1]
    value_size = v.shape[1]
    row = lambda w: pl.BlockSpec((block, w), lambda i: (i, 0))
    square = pl.BlockSpec((block // span, span, span), lambda i: (i, 0, 0))
    return pl.pallas_call(
        retain_back_kernel,
        grid=(total // block,),
        in_specs=[
            row(width), WHOLE, row(KH), row(KH), row(value_size), square, row(value_size),
            row(value_size), row(KH // 2), row(KH // 2), square, ANY,
        ],
        out_specs=[row(2 * KH + 2 * value_size)] + [ANY] * 3,
        out_shape=[
            jax.ShapeDtypeStruct((total, 2 * KH + 2 * value_size), bf16),
        ]
        + same([value]) * 3,
        scratch_shapes=pair(3),
        compiler_params=params(cid),
        cost_estimate=cost(20),
        name="retain_back",
    )(middle_low, wo, q, k, v, w, g, r, cosine, sine, decays, value)


def half_views(branch, dealt, count, begin):
    size = branch.shape[1] // count
    rows = dealt.shape[0]
    return (
        lambda i: branch.at[pl.ds(begin, rows), pl.ds(pl.multiple_of(i * size, size), size)],
        column_blocks(dealt, size),
    )


def gram_deal_kernel(count, begin, left, right, branch, out, dealt, *sems):
    views = half_views(branch, dealt, count, begin)

    @pl.when(pl.program_id(0) == 0)
    def _():
        deal_start(True, count, *views, *sems)

    out[...] = lax.dot_general(
        left[...], right[...], (((0,), (0,)), ((), ())), preferred_element_type=f32
    ).astype(bf16)

    @pl.when(pl.program_id(0) == pl.num_programs(0) - 1)
    def _():
        deal_wait(True, count, *views, *sems)


def gram_deal(left, right, branch, count, cid):
    total, width = left.shape
    columns = right.shape[1]
    rows = branch.shape[0] // 2
    return pl.pallas_call(
        functools.partial(gram_deal_kernel, count, rows),
        grid=(width // 256,),
        in_specs=[pl.BlockSpec((total, 256), lambda i: (0, i)), WHOLE, ANY],
        out_specs=(pl.BlockSpec((256, columns), lambda i: (i, 0)), ANY),
        out_shape=(
            jax.ShapeDtypeStruct((width, columns), bf16),
            jax.ShapeDtypeStruct((rows, branch.shape[1]), bf16),
        ),
        scratch_shapes=deal_scratch(count),
        compiler_params=params(cid),
        cost_estimate=cost(16),
        name="gram_deal",
    )(left, right, branch)


def feed_kernel(shards, count, normed_two, back_low, w_two, branch, hidden, low, w_down, dealt, *sems):
    size = hidden.shape[1]
    views = half_views(branch, dealt, count, 0) if count else ()

    @pl.when(pl.program_id(0) == 0)
    def _():
        if count:
            deal_start(True, count, *views, *sems)
        unit = size // shards
        span = w_two.shape[0] // shards
        part = w_two.shape[1] - 2 * size
        for z in range(shards):
            for c in range(span // unit):
                begin = z * span + c * unit
                w_down[z * unit : (z + 1) * unit, c * part : (c + 1) * part] = w_two[
                    begin : begin + unit, 2 * size :
                ]

    both = jnp.dot(normed_two[...], w_two[:, : 2 * size], preferred_element_type=f32)
    back = lax.dot_general(
        back_low[...], w_down[...], (((1,), (1,)), ((), ())), preferred_element_type=f32
    )
    up = both[:, size:]
    value, slope = gelu_parts(both[:, :size])
    hidden[...] = (value * up).astype(bf16)
    low[:, :size] = (back * up * slope).astype(bf16)
    low[:, size:] = (back * value).astype(bf16)

    if count:

        @pl.when(pl.program_id(0) == pl.num_programs(0) - 1)
        def _():
            deal_wait(True, count, *views, *sems)


def feed(normed_two, back_low, w_two, branch, size, shards, block, cid):
    total, width = normed_two.shape
    row = lambda w: pl.BlockSpec((block, w), lambda i: (i, 0))
    count = shards if branch.shape[1] // shards % 128 == 0 else 0
    hidden, low, w_down, dealt = pl.pallas_call(
        functools.partial(feed_kernel, shards, count),
        grid=(total // block,),
        in_specs=[row(width), row(width), WHOLE, ANY],
        out_specs=(row(size), row(2 * size), pl.BlockSpec((size, width), lambda i: (0, 0)), ANY),
        out_shape=(
            jax.ShapeDtypeStruct((total, size), bf16),
            jax.ShapeDtypeStruct((total, 2 * size), bf16),
            jax.ShapeDtypeStruct((size, width), bf16),
            jax.ShapeDtypeStruct((total // 2, branch.shape[1]) if count else (8, 128), bf16),
        ),
        scratch_shapes=deal_scratch(count) if count else [],
        compiler_params=params(cid if count else None),
        cost_estimate=cost(26),
        name="feed",
    )(normed_two, back_low, w_two, branch)
    if not count:
        pieces = jnp.transpose(branch.reshape(total, shards, -1), (1, 0, 2))
        pieces = lax.all_to_all(pieces, "tp", split_axis=0, concat_axis=0, tiled=True)
        dealt = jnp.transpose(pieces, (1, 0, 2)).reshape(total, -1)
    return hidden, low, w_down, dealt, count


def gram_kernel(left, right, value, out_a, out_b, by_x, by_y, by_sib, send, recv):
    by = (by_x, by_y, by_sib)

    @pl.when(pl.program_id(0) == 0)
    def _():
        greet()
        for c in phase_one_of(value, by, (send, recv)):
            c.start()

    both = lax.dot_general(
        left[...], right[...], (((0,), (0,)), ((), ())), preferred_element_type=f32
    ).astype(bf16)
    out_a[...] = both[:, : out_a.shape[1]]
    out_b[...] = both[:, out_a.shape[1] :]

    @pl.when(pl.program_id(0) == pl.num_programs(0) - 1)
    def _():
        for c in phase_one_of(value, by, (send, recv)):
            c.wait()


def gram_beside(left, right, value, first, block, cid):
    total, width = left.shape
    sizes = (first, right.shape[1] - first)
    return pl.pallas_call(
        gram_kernel,
        grid=(width // block,),
        in_specs=[pl.BlockSpec((total, block), lambda i: (0, i)), WHOLE, ANY],
        out_specs=[pl.BlockSpec((block, size), lambda i: (i, 0)) for size in sizes] + [ANY] * 3,
        out_shape=[jax.ShapeDtypeStruct((width, size), bf16) for size in sizes]
        + same([value]) * 3,
        scratch_shapes=pair(3),
        compiler_params=params(cid),
        cost_estimate=cost(28),
        name="gram_beside",
    )(left, right, value)


def middle_kernel(branch, wo, x, small, middle, normed_all, own, send1, recv1, sem1, *scratch):
    me = greet()
    reduce_steps(me, [(branch, wo)], False, *scratch)
    final, total = scratch[4], scratch[5]

    def make(at):
        value = x[at, :].astype(f32) + summed(total, final, at)
        middle[at, :] = value
        unit, _ = centre(value, layer_epsilon)
        own[at, :] = (unit * small[2:3, :] + small[3:4, :]).astype(bf16)

    gather_as_made(me, make, own, normed_all, send1, recv1, sem1)


def make_middle(branch, wo, x, small, cid):
    rows, width = x.shape
    return pl.pallas_call(
        middle_kernel,
        out_shape=(
            jax.ShapeDtypeStruct((rows, width), f32),
            jax.ShapeDtypeStruct((8, rows, width), bf16),
        ),
        in_specs=[WHOLE] * 4,
        out_specs=(WHOLE, ANY),
        scratch_shapes=gather_scratch(rows, width) + reduce_scratch(rows, width),
        compiler_params=params(cid),
        cost_estimate=cost(85),
        name="make_middle",
    )(branch, wo, x, small)


def back_middle_kernel(
    low_in, weight_in, middle, back_out, small, _after, _more, back_middle, parts, middle_all,
    low, weight, load, own, send1, recv1, sem1, *scratch,
):
    loads = [
        pltpu.make_async_copy(low_in, low, load.at[0]),
        pltpu.make_async_copy(weight_in.at[:, pl.ds(0, weight.shape[1])], weight, load.at[1]),
    ]
    for c in loads:
        c.start()
    me = greet()
    parts[...] = jnp.zeros_like(parts)
    for c in loads:
        c.wait()
    reduce_steps(me, [(low, weight)], True, *scratch)
    final, total = scratch[4], scratch[5]

    def make(at):
        back = summed(total, final, at)
        unit, root = centre(middle[at, :], layer_epsilon)
        parts[0:1, :] += jnp.sum(back * unit, axis=0, keepdims=True)
        parts[1:2, :] += jnp.sum(back, axis=0, keepdims=True)
        value = back_out[at, :].astype(f32) + through_norm(back * small[2:3, :], unit, root)
        back_middle[at, :] = value
        own[at, :] = value.astype(bf16)

    gather_as_made(me, make, own, middle_all, send1, recv1, sem1)


def make_back_middle(low, weight, middle, back_out, small, after, more, cid):
    rows, width = middle.shape
    return pl.pallas_call(
        back_middle_kernel,
        out_shape=(
            jax.ShapeDtypeStruct((rows, width), f32),
            jax.ShapeDtypeStruct((8, width), f32),
            jax.ShapeDtypeStruct((8, rows, width), bf16),
        ),
        in_specs=[ANY, ANY] + [WHOLE] * 3 + [ANY, ANY],
        out_specs=(WHOLE, WHOLE, ANY),
        scratch_shapes=[
            pltpu.VMEM(low.shape, bf16),
            pltpu.VMEM((width, low.shape[1]), bf16),
            pltpu.SemaphoreType.DMA((2,)),
        ]
        + gather_scratch(rows, width)
        + reduce_scratch(rows, width),
        compiler_params=params(cid),
        cost_estimate=cost(90),
        name="make_back_middle",
    )(low, weight, middle, back_out, small, after, more)


def ending_kernel(
    count, low_in, weight_in, hidden_in, down_in, x, back_middle, middle, usable, small, *refs,
):
    refs = list(refs)

    def take(n):
        got = refs[:n]
        del refs[:n]
        return got

    by_x, by_y = take(count), take(count)
    back_input, out, parts = take(3)
    half_low, half_high, sib_x, sib_y, sib_low, sib_high = (take(count) for _ in range(6))
    low, weight, hidden, down, load = take(5)
    two, three = take(2), take(2)
    first, second = take(8), take(8)
    loads = [
        pltpu.make_async_copy(low_in, low, load.at[0]),
        pltpu.make_async_copy(weight_in.at[:, pl.ds(0, weight.shape[1])], weight, load.at[1]),
        pltpu.make_async_copy(hidden_in, hidden, load.at[2]),
        pltpu.make_async_copy(down_in, down, load.at[3]),
    ]
    for c in loads:
        c.start()
    me = greet()
    started = phase_two(me, by_x, by_y, half_low, half_high, sib_x, sib_y, *two)
    parts[...] = jnp.zeros_like(parts)
    loads[0].wait()
    loads[1].wait()
    one = reduce_stages(me, [(low, weight)], True, *first)
    other = reduce_stages(me, [(hidden, down)], False, *second)
    next(one)
    loads[2].wait()
    loads[3].wait()
    next(other)
    next(one)
    next(other)
    for _ in one:
        pass

    @by_rows(x.shape[0])
    def _(at):
        back = summed(first[5], first[4], at)
        unit, root = centre(x[at, :].astype(f32), layer_epsilon)
        parts[0:1, :] += jnp.sum(back * unit, axis=0, keepdims=True)
        parts[1:2, :] += jnp.sum(back, axis=0, keepdims=True)
        value = back_middle[at, :] + through_norm(back * small[0:1, :], unit, root)
        back_input[at, :] = value.astype(bf16)

    for _ in other:
        pass
    for c in started:
        c.wait()
    last = phase_three(me, half_low, half_high, sib_low, sib_high, *three)

    @by_rows(middle.shape[0])
    def _(at):
        value = middle[at, :] + summed(second[5], second[4], at)
        out[at, :] = jnp.where(usable[at, :] > 0.5, value, 0.0).astype(bf16)

    for c in last:
        c.wait()


def make_ending(
    low, weight, hidden, down, x, back_middle, middle, usable, small, by_x, by_y, cid
):
    rows, width = x.shape
    count = len(by_x)
    shapes = (
        [
            jax.ShapeDtypeStruct((rows, width), bf16),
            jax.ShapeDtypeStruct((rows, width), bf16),
            jax.ShapeDtypeStruct((8, width), f32),
        ]
        + same(by_x, True) * 2
        + same(by_x) * 2
        + same(by_x, True) * 2
    )
    out = pl.pallas_call(
        functools.partial(ending_kernel, count),
        out_shape=shapes,
        in_specs=[ANY] * 4 + [WHOLE] * 5 + [ANY] * (2 * count),
        out_specs=[WHOLE] * 3 + [ANY] * (len(shapes) - 3),
        scratch_shapes=[
            pltpu.VMEM(low.shape, bf16),
            pltpu.VMEM((width, low.shape[1]), bf16),
            pltpu.VMEM(hidden.shape, bf16),
            pltpu.VMEM(down.shape, bf16),
            pltpu.SemaphoreType.DMA((4,)),
        ]
        + pair(4 * count)
        + pair(2 * count)
        + reduce_scratch(rows, width)
        + reduce_scratch(rows, width),
        compiler_params=params(cid),
        cost_estimate=cost(100),
        name="make_ending",
    )(
        low, weight, hidden, down, x, back_middle, middle, usable, small,
        *by_x, *by_y,
    )
    rest = out[3:]
    return *out[:3], [rest[i * count : (i + 1) * count] for i in range(6)]


def last_collect_kernel(count, parts_one, parts_two, *refs):
    fresh, refs = refs[:count], refs[count:]
    sums, refs = refs[0], refs[1:]
    fresh_all, refs = refs[:count], refs[count:]
    parts, turned, far, send_s, recv_s, send_f, recv_f = refs[:7]
    sems = [refs[7 + 3 * k : 10 + 3 * k] for k in range(count)]
    me = greet(True)
    z = lax.axis_index("shard")
    shards = lax.axis_size("shard")
    parts[...] = jnp.zeros_like(parts)
    parts[0:2, :] = parts_one[0:2, :]
    parts[2:4, :] = parts_two[0:2, :]
    turns = [
        push(parts, turned.at[i], send_s.at[i], recv_s.at[i], flip(me, mask))
        for i, mask in enumerate((2, 4, 1))
    ]
    mine = [pltpu.make_async_copy(a, b.at[me], s[2]) for a, b, s in zip(fresh, fresh_all, sems)]
    turns[0].start()
    for c in mine:
        c.start()
    started = [
        gather_begin(me, fresh[0], fresh_all[0], sems[0][0], sems[0][1])
    ]
    turns[0].wait()
    parts[...] += turned[0]
    turns[1].start()
    for a, b, s in list(zip(fresh, fresh_all, sems))[1:]:
        started.append(gather_begin(me, a, b, s[0], s[1]))
    turns[1].wait()
    parts[...] += turned[1]
    turns[2].start()
    turns[2].wait()
    parts[...] += turned[2]
    part = parts.shape[1] // shards
    waiting = []
    for k, other in enumerate(others()):
        c = pltpu.make_async_remote_copy(
            src_ref=parts.at[:, pl.ds(pl.multiple_of(other * part, part), part)],
            dst_ref=far.at[k],
            send_sem=send_f.at[k],
            recv_sem=recv_f.at[k],
            device_id={"shard": other},
            device_id_type=MESHID,
        )
        c.start()
        waiting.append(c)
    for a, b, s, first in zip(fresh, fresh_all, sems, started):
        gather_end(me, a, b, s[0], s[1], first)
    value = parts[:, pl.ds(pl.multiple_of(z * part, part), part)]
    for k, c in enumerate(waiting):
        c.wait()
        value = value + far[k]
    sums[...] = value
    for c in mine:
        c.wait()


def last_collect(parts_one, parts_two, fresh, cid):
    width = parts_one.shape[1]
    shards = lax.axis_size("shard")
    count = len(fresh)
    out = pl.pallas_call(
        functools.partial(last_collect_kernel, count),
        out_shape=[jax.ShapeDtypeStruct((8, width // shards), f32)]
        + [jax.ShapeDtypeStruct((8,) + a.shape, bf16) for a in fresh],
        in_specs=[WHOLE, WHOLE] + [ANY] * count,
        out_specs=[WHOLE] + [ANY] * count,
        scratch_shapes=[
            pltpu.VMEM((8, width), f32),
            pltpu.VMEM((3, 8, width), f32),
            pltpu.VMEM((shards - 1, 8, width // shards), f32),
        ]
        + pair(3)
        + pair(shards - 1)
        + gather_scratch(8, 128)[1:] * count,
        compiler_params=params(cid),
        cost_estimate=cost(5),
        name="last_collect",
    )(parts_one, parts_two, *fresh)
    return out[0], out[1:]


MASKS = (0, 2, 4, 6, 6, 1, 3, 5, 7, 7)
WHEN = (2, 2, 2, 0, 1, 2, 2, 2, 0, 1)


def in_order(parts):
    value, by_x, by_y, low, high, sib, sib_x, sib_y, sib_low, sib_high = parts
    corner, sib_corner = jnp.concatenate([low, high]), jnp.concatenate([sib_low, sib_high])
    stacked = jnp.stack([value, sib, by_x, sib_x, by_y, sib_y, corner, sib_corner])
    return jnp.take(stacked, jnp.arange(8) ^ lax.axis_index("tp"), axis=0)


def widen_two_kernel(steps, shards, *refs):
    t = lax.axis_index("tp")
    late = (pl.program_id(0) >= steps // 2).astype(jnp.int32)
    seconds, downs, outs = refs[:10], refs[10:20], refs[20]
    gelu, up, down, out = refs[21:]
    out[...] = outs[...].astype(f32)
    unit = gelu.shape[1] // (8 * shards)

    def store(i):
        place = flip(t, MASKS[i])
        down[place] = downs[i][...].astype(f32)
        for z in range(shards):
            at = pl.ds(pl.multiple_of((8 * z + place) * unit, unit), unit)
            gelu[:, at] = seconds[i][:, z * unit : (z + 1) * unit].astype(f32)
            up[:, at] = seconds[i][:, (shards + z) * unit : (shards + z + 1) * unit].astype(f32)

    for i in range(10):
        if WHEN[i] == 2:
            store(i)
        else:

            @pl.when(late == WHEN[i])
            def _():
                store(i)


def widen_two(seconds, downs, outs, shards):
    rows, columns = seconds[0].shape
    count, width = downs[0].shape
    steps = 4

    def row_at(which, i):
        half = steps // 2
        return (i, jnp.minimum(i, half - 1), jnp.maximum(i - half, 0))[(which + 1) % 3]

    def specs(parts):
        return [
            pl.BlockSpec(
                (parts[0].shape[0] // steps, parts[0].shape[1]),
                functools.partial(lambda w, i: (row_at(w, i), 0), w),
            )
            for w in WHEN
        ]

    units = jax.ShapeDtypeStruct((rows, 4 * columns), f32)
    stack = jax.ShapeDtypeStruct((8, count, width), f32)
    gelu, up, down, out = pl.pallas_call(
        functools.partial(widen_two_kernel, steps, shards),
        grid=(steps,),
        in_specs=specs(seconds)
        + specs(downs)
        + [pl.BlockSpec((8, count // steps, width), lambda i: (0, i, 0))],
        out_specs=[pl.BlockSpec((rows // steps, 4 * columns), lambda i: (i, 0))] * 2
        + [pl.BlockSpec((8, count // steps, width), lambda i: (0, i, 0))] * 2,
        out_shape=[units, units, stack, stack],
        compiler_params=params(),
        cost_estimate=cost(25),
        name="widen_two",
    )(*seconds, *downs, outs)
    return gelu, up, down.reshape(8 * count, width), out.reshape(8 * count, width)


def widen_one_kernel(edges, parts, _after, *goals):
    for goal, (begin, end) in zip(goals, zip(edges, edges[1:])):
        size = end - begin
        for i in range(8):
            goal[:, i * size : (i + 1) * size] = parts[i, :, begin:end].astype(f32)


def widen_one(parts, edges, after, name):
    _, rows, columns = parts.shape
    sizes = [b - a for a, b in zip(edges, edges[1:])]
    block = 64
    return pl.pallas_call(
        functools.partial(widen_one_kernel, edges),
        grid=(rows // block,),
        in_specs=[pl.BlockSpec((8, block, columns), lambda i: (0, i, 0)), ANY],
        out_specs=[pl.BlockSpec((block, 8 * size), lambda i: (i, 0)) for size in sizes],
        out_shape=[jax.ShapeDtypeStruct((rows, 8 * size), f32) for size in sizes],
        compiler_params=params(),
        cost_estimate=cost(14),
        name=name,
    )(parts, after)


def local(
    tokens,
    cotangent,
    token_order,
    lengths,
    query_weight,
    key_weight,
    value_weight,
    gate_weight,
    out_weight,
    gelu_weight,
    up_weight,
    down_weight,
    gain_one,
    shift_one,
    gain_two,
    shift_two,
):
    every = ("outer", "tp", "shard")
    device_count = lax.axis_size(every)
    device_index = lax.axis_index(every)
    outer, tp, shards = lax.axis_size("outer"), lax.axis_size("tp"), lax.axis_size("shard")
    t, z = lax.axis_index("tp"), lax.axis_index("shard")
    rows, width = tokens.shape
    packs = lengths.shape[0]
    pack_rows = rows // packs
    group_rows = tp * rows
    group_packs = tp * packs

    own_order = lax.dynamic_slice_in_dim(token_order, device_index * rows, rows)
    target = own_order // rows
    places = jnp.arange(rows, dtype=jnp.int32)
    before = (target[None, :] < target[:, None]) | (
        (target[None, :] == target[:, None]) & (places[None, :] < places[:, None])
    )
    send_place = jnp.sum(before.astype(jnp.int32), axis=1)
    send_mix = (send_place[None, :] == places[:, None]).astype(bf16)
    loader_ids = jnp.arange(token_order.shape[0], dtype=jnp.int32)
    slot_targets = device_index * rows + places
    origin = jnp.sum(
        jnp.where(token_order[None, :] == slot_targets[:, None], loader_ids[None, :], 0), axis=1
    )
    arrive_place = jnp.sum((origin[None, :] < origin[:, None]).astype(jnp.int32), axis=1)
    work_mix = (arrive_place[:, None] == places[None, :]).astype(bf16)

    def exchange(value):
        return lax.all_to_all(
            value.reshape(device_count, rows // device_count, value.shape[1]),
            every,
            split_axis=0,
            concat_axis=0,
            tiled=True,
        ).reshape(rows, value.shape[1])

    piece = rows // device_count
    part = gain_one.shape[0]
    extra = jnp.concatenate(
        [gain_one, shift_one, gain_two, shift_two, lengths.reshape(-1).astype(bf16)]
    )
    extra_columns = -(-extra.shape[0] // (piece * 128)) * 128
    extra = jnp.pad(extra, (0, piece * extra_columns - extra.shape[0]))
    extra = jnp.tile(extra.reshape(piece, extra_columns), (device_count, 1))
    came = exchange(
        jnp.concatenate([forward_dot(send_mix, tokens).astype(bf16), extra], axis=1)
    )
    sent_back = forward_dot(send_mix, cotangent).astype(bf16)
    came_back = exchange(sent_back)
    arrived = came[:, width:].reshape(outer, tp, shards, -1)
    small = jnp.transpose(arrived[0, 0, :, : 4 * part].reshape(shards, 4, part), (1, 0, 2))
    small = small.reshape(4, width).astype(f32)
    small = jnp.concatenate([small, jnp.zeros((4, width), f32)], axis=0)
    all_lengths = arrived[lax.axis_index("outer"), :, z, 4 * part : 4 * part + lengths.size]
    all_lengths = all_lengths.reshape(group_packs, -1).astype(f32).astype(jnp.int32)

    def along_z(piece):
        return lax.all_gather(piece, "shard", axis=0, tiled=True)

    def cut(weight):
        part = weight.shape[1] // tp
        return lax.dynamic_slice_in_dim(weight, t * part, part, axis=1)

    out_unit = out_weight.shape[0] // tp
    unit = down_weight.shape[0] // tp
    piece_rows = query_weight.shape[0]
    key_part, value_part = query_weight.shape[1] // tp, value_weight.shape[1] // tp
    edges = (0, key_part, 2 * key_part, 2 * key_part + value_part)
    first_size = 2 * key_part + 2 * value_part
    hidden_part = shards * unit

    def fold(value):
        cuts = piece_rows // value.shape[0]
        value = value.reshape(value.shape[0], cuts, width // cuts)
        return jnp.transpose(value, (1, 0, 2)).reshape(piece_rows, width // cuts)

    def unfold(value, count):
        cuts = piece_rows // count
        value = value.reshape(shards, cuts, count, width // cuts)
        return jnp.transpose(value, (0, 2, 1, 3)).reshape(shards, count, width)

    out_piece = lax.dynamic_slice_in_dim(out_weight, t * out_unit, out_unit, axis=0)
    w_one = along_z(
        jnp.concatenate(
            [cut(w) for w in (query_weight, key_weight, value_weight, gate_weight)]
            + [fold(out_piece)],
            axis=1,
        )
    )
    ends = jnp.cumsum(lengths, axis=1, dtype=jnp.int32)[:, -2]
    usable = (jnp.arange(pack_rows, dtype=jnp.int32)[None, :] < ends[:, None]).astype(f32)
    usable = usable.reshape(rows, 1)
    x, normed = entry(came, work_mix, small, 0)
    def unit_columns(weight):
        return [
            lax.dynamic_slice_in_dim(weight, (k * tp + t) * unit, unit, axis=1)
            for k in range(shards)
        ]

    down_piece = lax.dynamic_slice_in_dim(down_weight, t * unit, unit, axis=0)
    second_piece = lax.optimization_barrier(
        jnp.concatenate(
            unit_columns(gelu_weight) + unit_columns(up_weight) + [fold(down_piece)], axis=1
        )
    )
    w_two = along_z(second_piece + jnp.isnan(x[0, 0]).astype(bf16))
    back_out, back_low = entry_back(came_back, work_mix, usable, x, 7)
    normed, back_low = normed.reshape(group_rows, width), back_low.reshape(group_rows, width)
    cosine, sine, decays, _ = pack_tables(all_lengths, pack_rows, t + jnp.arange(1))
    cosine, sine = cosine.reshape(group_rows, -1), sine.reshape(group_rows, -1)
    decays = decays[0]
    out_pieces = unfold(w_one[:, first_size:], out_unit)
    q_rot, k_rot, v_low, weights_low, gating, retained, branch, wo = retain(
        normed, w_one, value_part, cosine, sine, decays, out_pieces, rows, 1
    )
    wo = wo.reshape(shards * out_unit, width)
    middle, normed_two = make_middle(branch, wo, x, small, 2)
    normed_two = normed_two.reshape(group_rows, width)

    hidden, second_low, w_down, branch_rows, halved = feed(
        normed_two, back_low, w_two, branch, hidden_part, shards, rows, 6
    )
    down_gram = gram_rows(hidden, back_low).astype(bf16)
    if halved:
        second_gram, branch_more = gram_deal(normed_two, second_low, branch, shards, 12)
        branch_rows = jnp.concatenate([branch_rows, branch_more])
    else:
        second_gram = gram_rows(normed_two, second_low).astype(bf16)

    def to_owner(value):
        part = lax.psum_scatter(value, "shard", scatter_dimension=0, tiled=True)
        return lax.psum(part, "outer") if outer > 1 else part

    down_sum, second_sum = to_owner(down_gram), to_owner(second_gram)
    back_middle, parts_two, middle_low = make_back_middle(
        second_low, w_two, middle, back_out, small, down_gram, second_gram, 3
    )
    middle_low = middle_low.reshape(group_rows, width)
    out_sum = to_owner(gram_rows(branch_rows, middle_low).astype(bf16))
    first_low, *down_by = retain_back(
        middle_low, wo, q_rot, k_rot, v_low, weights_low, gating, retained, cosine, sine, decays,
        down_sum, rows, 8,
    )
    first_gram, third_gram, *second_by = gram_beside(
        normed, first_low, second_sum, edges[3], 256, 9
    )
    first_sum, third_sum = to_owner(first_gram), to_owner(third_gram)
    by_x, by_y, by_sib = ([a, b] for a, b in zip(second_by, down_by))
    back_inputs, ending, parts_one, groups = make_ending(
        first_low, w_one, hidden, w_down, x, back_middle, middle, usable, small, by_x, by_y, 5
    )
    sums, (outs, firsts) = last_collect(parts_one, parts_two, [out_sum, first_sum], 10)
    low, high, sib_x, sib_y, sib_low, sib_high = groups
    seconds, downs = (
        [
            value, by_x[k], by_y[k], low[k], high[k],
            by_sib[k], sib_x[k], sib_y[k], sib_low[k], sib_high[k],
        ]
        for k, value in enumerate((second_sum, down_sum))
    )

    if unit % 128 == 0:
        gelu_gradient, up_gradient, down_gradient, out_gradient = widen_two(
            seconds, downs, outs, shards
        )
    else:
        down_gradient = in_order(downs).reshape(-1, width).astype(f32)
        out_gradient = outs.reshape(-1, width).astype(f32)
        both = in_order(seconds).reshape(tp, piece_rows, 2, shards, unit)
        both = jnp.transpose(both, (2, 1, 3, 0, 4)).reshape(2, piece_rows, -1).astype(f32)
        gelu_gradient, up_gradient = both[0], both[1]
    nothing = jnp.isnan(outs[0, 0, 0]).astype(bf16)
    thirds = lax.all_gather(third_sum + nothing, "tp", axis=0)
    query_gradient, key_gradient, value_gradient = widen_one(
        firsts, edges, down_gradient, "widen_one"
    )
    (gate_gradient,) = widen_one(thirds, (0, value_part), query_gradient, "widen_three")
    smalls = lax.psum(sums, "outer") if outer > 1 else sums

    home = jnp.concatenate([ending, back_inputs], axis=1)
    home = exchange(gram_rows(work_mix + nothing, home).astype(bf16))
    home = gram_rows(send_mix, home).astype(bf16)
    result, token_gradient = home[:, :width], home[:, width:]
    return (
        result,
        token_gradient,
        query_gradient,
        key_gradient,
        value_gradient,
        gate_gradient,
        out_gradient,
        gelu_gradient,
        up_gradient,
        down_gradient,
        smalls[0],
        smalls[1],
        smalls[2],
        smalls[3],
    )


def solution(mesh):
    tp = math.gcd(mesh.shape["rep"], HEADS)
    grid = mesh.devices.reshape(mesh.shape["rep"] // tp, tp, mesh.shape["shard"])
    cube = Mesh(grid, ("outer", "tp", "shard"))
    tokens_at = P(("outer", "tp", "shard"), None)
    weights_at = P("shard", None)
    vectors_at = P("shard")
    in_specs = (tokens_at, tokens_at, P(), tokens_at) + (weights_at,) * 8 + (vectors_at,) * 4
    out_specs = (tokens_at, tokens_at) + (weights_at,) * 8 + (vectors_at,) * 4
    return jax.shard_map(local, mesh=cube, in_specs=in_specs, out_specs=out_specs, check_vma=False)
```

```python
import functools
import math

import jax
import jax.numpy as jnp
from jax import lax
from jax.experimental import pallas as pl
from jax.experimental.pallas import tpu as pltpu
from jax.sharding import Mesh, PartitionSpec as P

HEADS = 8
KH = 256

layer_epsilon = 1e-05
head_epsilon = 1.0
rotary_base = 10000.0
bf16 = jnp.bfloat16
f32 = jnp.float32
MESHID = pl.DeviceIdType.MESH


def pack_tables(lengths, pack_rows, head_ids):
    entries = lengths.shape[1]
    slot_ids = jnp.arange(pack_rows, dtype=jnp.int32)
    seq_ends = jnp.cumsum(lengths, axis=1, dtype=jnp.int32)
    seq_starts = seq_ends - lengths
    segment = jnp.sum(
        (slot_ids[None, :, None] >= seq_ends[:, None, :]).astype(jnp.int32), axis=2, dtype=jnp.int32
    )
    owners = segment[:, :, None] == jnp.arange(entries, dtype=jnp.int32)[None, None, :]
    begins = jnp.sum(jnp.where(owners, seq_starts[:, None, :], 0), axis=2, dtype=jnp.int32)
    places = (slot_ids[None, :] - begins).astype(f32)
    usable = segment < entries - 1
    half_size = KH // 2
    frequency = jnp.power(
        f32(rotary_base), -jnp.arange(half_size, dtype=f32) / f32(half_size - 1)
    )
    angles = places[:, :, None] * frequency
    cosine_table = jnp.cos(angles)
    sine_table = jnp.sin(angles)
    lag_steps = slot_ids[:, None] - slot_ids[None, :]
    linked = (
        (segment[:, :, None] == segment[:, None, :])
        & (lag_steps[None] >= 0)
        & usable[:, None, :]
    )
    log_rates = jnp.log(1.0 - jnp.power(f32(2.0), -5.0 - head_ids.astype(f32)))
    powers = jnp.exp(log_rates[:, None, None] * jnp.maximum(lag_steps, 0).astype(f32)[None])
    decays = jnp.where(linked[None], powers[:, None], f32(0.0))
    return cosine_table, sine_table, decays, usable


def gram_rows(leading, trailing):
    return lax.dot_general(
        leading, trailing, (((0,), (0,)), ((), ())), preferred_element_type=f32
    )


def back_through(incoming, matrix):
    return lax.dot_general(
        incoming, matrix, (((1,), (1,)), ((), ())), preferred_element_type=f32
    )


def forward_dot(inputs, matrix):
    return jnp.dot(inputs, matrix, preferred_element_type=f32)


def gelu_parts(v):
    c = f32(math.sqrt(2.0 / math.pi))
    t = jnp.tanh(c * (v + 0.044715 * v * v * v))
    value = 0.5 * v * (1.0 + t)
    slope = 0.5 * (1.0 + t) + 0.5 * v * (1.0 - t * t) * c * (1.0 + 3.0 * 0.044715 * v * v)
    return value, slope


def flip(me, mask):
    for bit in (1, 2, 4):
        if mask & bit:
            me = me + bit - 2 * bit * ((me // bit) % 2)
    return me


def greet(far=False):
    me = lax.axis_index("tp")
    barrier = pltpu.get_barrier_semaphore()
    for mask in (1, 2, 4):
        pl.semaphore_signal(
            barrier, inc=1, device_id={"tp": flip(me, mask)}, device_id_type=MESHID
        )
    count = 3
    if far:
        for other in others():
            pl.semaphore_signal(barrier, inc=1, device_id={"shard": other}, device_id_type=MESHID)
            count += 1
    pl.semaphore_wait(barrier, count)
    return me


def others():
    shards = lax.axis_size("shard")
    return [(lax.axis_index("shard") + k) % shards for k in range(1, shards)]


def push(source, goal, send, recv, peer):
    return pltpu.make_async_remote_copy(
        src_ref=source, dst_ref=goal, send_sem=send, recv_sem=recv,
        device_id={"tp": peer}, device_id_type=MESHID,
    )


def gather_begin(me, own, out, send, recv, halves=(True, True), first=None):
    half = own.shape[0] // 2
    xn, yn = flip(me, 2), flip(me, 4)
    low, high = pl.ds(0, half), pl.ds(half, half)
    first = first if first is not None else [None] * 5
    ways = ((low, xn), (high, yn), (high, xn), (low, yn))
    for i in (0, 3, 1, 2):
        part, peer = ways[i]
        if halves[0 if part is low else 1]:
            first[i] = push(own.at[part], out.at[me, part], send.at[i], recv.at[i], peer)
            first[i].start()
    if halves[1]:
        first[4] = push(own, out.at[me], send.at[4], recv.at[4], flip(me, 1))
        first[4].start()
    return first


def gather_end(me, own, out, send, recv, first):
    half = own.shape[0] // 2
    sib, xn, yn, dn = flip(me, 1), flip(me, 2), flip(me, 4), flip(me, 6)
    low, high = pl.ds(0, half), pl.ds(half, half)
    started = list(first)

    def on(slot, part, peer):
        i = len(started)
        place = out.at[slot, part]
        c = push(place, place, send.at[i], recv.at[i], peer)
        c.start()
        started.append(c)
        return c

    first[0].wait_recv()
    d_low = on(xn, low, yn)
    first[1].wait_recv()
    d_high = on(yn, high, xn)
    on(xn, low, sib)
    on(yn, high, sib)
    first[2].wait_recv()
    on(xn, high, sib)
    first[3].wait_recv()
    on(yn, low, sib)
    d_low.wait_recv()
    on(dn, low, sib)
    d_high.wait_recv()
    on(dn, high, sib)
    for i in (4, 7, 8, 9, 10, 11, 12):
        started[i].wait_recv()
    for c in started:
        c.wait_send()


def gather_steps(me, own, out, send, recv):
    gather_end(me, own, out, send, recv, gather_begin(me, own, out, send, recv))


COLS = 1024


def reduce_stages(me, pairs, transposed, tosib, fromsib, hold, hop, final, total, send, recv):
    rows, width = total.shape
    half = rows // 2
    sib, xn, yn = flip(me, 1), flip(me, 2), flip(me, 4)
    low, high = pl.ds(0, half), pl.ds(half, half)

    def product(block, tile):
        acc = None
        for act, weight in pairs:
            left = act[pl.ds(pl.multiple_of(block * rows, rows), rows), :]
            if transposed:
                part = lax.dot_general(
                    left, weight[pl.ds(pl.multiple_of(tile * COLS, COLS), COLS), 0 : act.shape[1]],
                    (((1,), (1,)), ((), ())), preferred_element_type=f32,
                )
            else:
                part = jnp.dot(
                    left, weight[:, pl.ds(pl.multiple_of(tile * COLS, COLS), COLS)],
                    preferred_element_type=f32,
                )
            acc = part if acc is None else acc + part
        return acc

    def cp(i, src, goal, peer):
        return push(src, goal, send.at[i], recv.at[i], peer)

    masks = (6, 2, 4, 0)
    over, out = [], {}

    def for_sibling(slot):
        block = flip(me, masks[slot] ^ 1)

        @pl.loop(0, width // COLS)
        def _(tile):
            at = pl.ds(pl.multiple_of(tile * COLS, COLS), COLS)
            tosib[slot, :, at] = product(block, tile).astype(bf16)

        c = cp(slot, tosib.at[slot], fromsib.at[slot], sib)
        c.start()
        over.append(c)

    def for_own_core(slot):
        block = flip(me, masks[slot])
        over[slot].wait_recv()

        @pl.loop(0, width // COLS)
        def _(tile):
            at = pl.ds(pl.multiple_of(tile * COLS, COLS), COLS)
            value = product(block, tile) + fromsib[slot, :, at].astype(f32)
            if slot < 3:
                hold[slot, :, at] = value.astype(bf16)
            else:
                total[:, at] = value

    for_sibling(0)
    for_sibling(1)
    for_own_core(0)
    dx = cp(4, hold.at[0, low], hop.at[0], xn)
    dy = cp(5, hold.at[0, high], hop.at[1], yn)
    dx.start()
    dy.start()
    for_sibling(2)
    for_own_core(1)
    xa = cp(6, hold.at[1, low], final.at[0, low], xn)
    xa.start()
    for_sibling(3)
    for_own_core(2)
    yb = cp(7, hold.at[2, high], final.at[1, high], yn)
    yb.start()
    for_own_core(3)
    yield
    dy.wait_recv()
    hold[1, high] = (hold[1, high].astype(f32) + hop[1].astype(f32)).astype(bf16)
    xb = cp(8, hold.at[1, high], final.at[0, high], xn)
    xb.start()
    dx.wait_recv()
    hold[2, low] = (hold[2, low].astype(f32) + hop[0].astype(f32)).astype(bf16)
    ya = cp(9, hold.at[2, low], final.at[1, low], yn)
    ya.start()
    yield
    xa.wait_recv()
    yb.wait_recv()
    xb.wait_recv()
    ya.wait_recv()
    for c in over + [dx, dy, xa, yb, xb, ya]:
        c.wait_send()


def reduce_steps(*args):
    for _ in reduce_stages(*args):
        pass


def summed(total, final, at):
    return total[at, :] + final[0, at, :].astype(f32) + final[1, at, :].astype(f32)


def reduce_scratch(rows, width):
    return [
        pltpu.VMEM((4, rows, width), bf16),
        pltpu.VMEM((4, rows, width), bf16),
        pltpu.VMEM((3, rows, width), bf16),
        pltpu.VMEM((2, rows // 2, width), bf16),
        pltpu.VMEM((2, rows, width), bf16),
        pltpu.VMEM((rows, width), f32),
        pltpu.SemaphoreType.DMA((10,)),
        pltpu.SemaphoreType.DMA((10,)),
    ]


CHUNK = 64


def cost(us):
    return pl.CostEstimate(flops=int(us * 1e9), bytes_accessed=int(us * 3e6), transcendentals=0)


def params(cid=None):
    if cid is None:
        return pltpu.CompilerParams(vmem_limit_bytes=60 << 20)
    return pltpu.CompilerParams(collective_id=cid, has_side_effects=True, vmem_limit_bytes=60 << 20)


def by_rows(count, begin=0):
    def run(body):
        @pl.loop(begin // CHUNK, count // CHUNK)
        def _(i):
            body(pl.ds(pl.multiple_of(i * CHUNK, CHUNK), CHUNK))

    return run


def gather_as_made(me, make, own, out, send, recv, local_sem):
    rows = own.shape[0]
    by_rows(rows // 2)(make)
    first = gather_begin(me, own, out, send, recv, (True, False))
    by_rows(rows, rows // 2)(make)
    gather_begin(me, own, out, send, recv, (False, True), first)
    mine = pltpu.make_async_copy(own, out.at[me], local_sem)
    mine.start()
    gather_end(me, own, out, send, recv, first)
    mine.wait()


def centre(value, epsilon):
    average = jnp.mean(value, axis=-1, keepdims=True)
    centred = value - average
    spread = jnp.mean(centred * centred, axis=-1, keepdims=True)
    root = lax.rsqrt(spread + epsilon)
    return centred * root, root


def through_norm(e, unit, root):
    return root * (
        e - jnp.mean(e, axis=-1, keepdims=True) - unit * jnp.mean(e * unit, axis=-1, keepdims=True)
    )


def leading(rows, columns):
    return pl.BlockSpec((rows, columns), lambda *_: (0, 0))


ANY = pl.BlockSpec(memory_space=pl.ANY)
WHOLE = pl.BlockSpec(memory_space=pltpu.VMEM)


def gather_scratch(rows, width):
    return [
        pltpu.VMEM((rows, width), bf16),
        pltpu.SemaphoreType.DMA((13,)),
        pltpu.SemaphoreType.DMA((13,)),
        pltpu.SemaphoreType.DMA,
    ]


def gather_all(me, own, out, send, recv, local_sem):
    mine = pltpu.make_async_copy(own, out.at[me], local_sem)
    mine.start()
    gather_steps(me, own, out, send, recv)
    mine.wait()


def entry_kernel(came, mix, small, x_out, normed_all, own, send, recv, sem):
    me = greet()
    width = x_out.shape[1]

    @by_rows(came.shape[0])
    def _(at):
        value = jnp.dot(mix[at, :], came[:, :width], preferred_element_type=f32)
        x_out[at, :] = value.astype(bf16)
        unit, _ = centre(value, layer_epsilon)
        own[at, :] = (unit * small[0:1, :] + small[1:2, :]).astype(bf16)

    gather_all(me, own, normed_all, send, recv, sem)


def entry(came, mix, small, cid):
    rows, width = came.shape[0], small.shape[1]
    return pl.pallas_call(
        entry_kernel,
        out_shape=(
            jax.ShapeDtypeStruct((rows, width), bf16),
            jax.ShapeDtypeStruct((8, rows, width), bf16),
        ),
        in_specs=[WHOLE] * 3,
        out_specs=(WHOLE, ANY),
        scratch_shapes=gather_scratch(rows, width),
        compiler_params=params(cid),
        cost_estimate=cost(50),
        name="entry",
    )(came, mix, small)


def entry_back_kernel(came, mix, usable, _after, back_out, back_all, own, send, recv, sem):
    me = greet()

    @by_rows(came.shape[0])
    def _(at):
        value = jnp.dot(mix[at, :], came[...], preferred_element_type=f32)
        value = jnp.where(usable[at, :] > 0.5, value, 0.0).astype(bf16)
        back_out[at, :] = value
        own[at, :] = value

    gather_all(me, own, back_all, send, recv, sem)


def entry_back(came, mix, usable, after, cid):
    rows, width = came.shape
    return pl.pallas_call(
        entry_back_kernel,
        out_shape=(
            jax.ShapeDtypeStruct((rows, width), bf16),
            jax.ShapeDtypeStruct((8, rows, width), bf16),
        ),
        in_specs=[WHOLE] * 3 + [ANY],
        out_specs=(WHOLE, ANY),
        scratch_shapes=gather_scratch(rows, width),
        compiler_params=params(cid),
        cost_estimate=cost(45),
        name="entry_back",
    )(came, mix, usable, after)


def deal_plan(back, count):
    heads = HEADS // count
    me = lax.axis_index("tp")
    spread = [i * heads + me // count for i in range(count)]
    packed = [(me % heads) * count + i for i in range(count)]
    goals, sources = (packed, spread) if back else (spread, packed)
    return me, goals, sources, (me // heads if back else me % count), me // count == me % heads


def deal_start(back, count, source, goal, send, recv, local_sem):
    me, goals, sources, slot, inside = deal_plan(back, count)
    barrier = pltpu.get_barrier_semaphore()
    for i in range(count):

        @pl.when(sources[i] != me)
        def _():
            pl.semaphore_signal(
                barrier, inc=1, device_id={"tp": sources[i]}, device_id_type=MESHID
            )

    pl.semaphore_wait(barrier, jnp.where(inside, count - 1, count))
    for i in range(count):

        @pl.when(goals[i] == me)
        def _():
            pltpu.make_async_copy(source(i), goal(slot), local_sem).start()

        @pl.when(goals[i] != me)
        def _():
            push(source(i), goal(slot), send.at[i], recv.at[slot], goals[i]).start()


def deal_wait(back, count, source, goal, send, recv, local_sem):
    me, goals, sources, slot, _ = deal_plan(back, count)
    for i in range(count):

        @pl.when(goals[i] == me)
        def _():
            pltpu.make_async_copy(source(i), goal(slot), local_sem).wait()

        @pl.when(goals[i] != me)
        def _():
            push(source(i), goal(slot), send.at[i], recv.at[slot], goals[i]).wait_send()

        @pl.when(sources[i] != me)
        def _():
            push(source(i), goal(i), send.at[i], recv.at[i], sources[i]).wait_recv()


def blocks(ref):
    return lambda i: ref.at[i]


def column_blocks(ref, size):
    return lambda i: ref.at[:, pl.ds(pl.multiple_of(i * size, size), size)]


def deal_scratch(count):
    return [
        pltpu.SemaphoreType.DMA((count,)),
        pltpu.SemaphoreType.DMA((count,)),
        pltpu.SemaphoreType.DMA,
    ]


def phase_one_copies(me, values, by_x, by_y, by_sib, send, recv):
    copies = []
    for k, value in enumerate(values):
        for i, (goal, mask) in enumerate(((by_x, 2), (by_y, 4), (by_sib, 1))):
            n = 3 * k + i
            copies.append(push(value, goal[k], send.at[n], recv.at[n], flip(me, mask)))
    return copies


def phase_one(*args):
    copies = phase_one_copies(*args)
    for c in copies:
        c.start()
    return copies


def phase_two(me, by_x, by_y, low, high, sib_x, sib_y, send, recv):
    copies = []
    for k in range(len(by_x)):
        half = by_x[k].shape[0] // 2
        for i, (source, goal, mask) in enumerate(
            (
                (by_x[k].at[pl.ds(0, half)], low[k], 4),
                (by_y[k].at[pl.ds(half, half)], high[k], 2),
                (by_x[k], sib_x[k], 1),
                (by_y[k], sib_y[k], 1),
            )
        ):
            n = 4 * k + i
            copies.append(push(source, goal, send.at[n], recv.at[n], flip(me, mask)))
    for c in copies:
        c.start()
    return copies


def phase_three(me, low, high, sib_low, sib_high, send, recv):
    copies = []
    for k in range(len(low)):
        for i, (source, goal) in enumerate(((low[k], sib_low[k]), (high[k], sib_high[k]))):
            n = 2 * k + i
            copies.append(push(source, goal, send.at[n], recv.at[n], flip(me, 1)))
    for c in copies:
        c.start()
    return copies


def pair(count):
    return [pltpu.SemaphoreType.DMA((count,)), pltpu.SemaphoreType.DMA((count,))]


def same(values, halves=False):
    return [
        jax.ShapeDtypeStruct((v.shape[0] // 2 if halves else v.shape[0], v.shape[1]), v.dtype)
        for v in values
    ]


def turn(value, cosine, sine):
    half = value.shape[-1] // 2
    a, b = value[:, :half], value[:, half:]
    return jnp.concatenate([a * cosine - b * sine, a * sine + b * cosine], axis=1)


def retain_kernel(
    normed, weight, cosine, sine, decays, pieces,
    q_out, k_out, v_out, w_out, g_out, r_out, branch, wo, *sems
):
    @pl.when(pl.program_id(0) == 0)
    def _():
        deal_start(False, pieces.shape[0], blocks(pieces), blocks(wo), *sems)

    packs, span = decays.shape[0], decays.shape[1]
    value_at = 2 * KH
    gate_at = value_at + v_out.shape[1]
    rows = normed[...]

    def project(begin, size):
        return jnp.dot(rows, weight[:, begin : begin + size], preferred_element_type=f32)

    q_out[...] = turn(project(0, KH), cosine[...], sine[...]).astype(bf16)
    k_out[...] = (turn(project(KH, KH), cosine[...], sine[...]) * KH ** (-0.5)).astype(bf16)
    v_out[...] = project(value_at, v_out.shape[1]).astype(bf16)
    g_out[...] = project(gate_at, g_out.shape[1])
    for p in range(packs):
        at = pl.ds(p * span, span)
        scores = lax.dot_general(
            q_out[at, :], k_out[at, :], (((1,), (1,)), ((), ())), preferred_element_type=f32
        )
        low = (scores * decays[p]).astype(bf16)
        w_out[p] = low
        retained = jnp.dot(low, v_out[at, :], preferred_element_type=f32)
        r_out[at, :] = retained
        unit, _ = centre(retained, head_epsilon)
        gating = g_out[at, :]
        branch[at, :] = (gating * jax.nn.sigmoid(gating) * unit).astype(bf16)

    @pl.when(pl.program_id(0) == pl.num_programs(0) - 1)
    def _():
        deal_wait(False, pieces.shape[0], blocks(pieces), blocks(wo), *sems)


def retain(normed, weight, value_size, cosine, sine, decays, pieces, block, cid):
    total, width = normed.shape
    span = decays.shape[1]
    grid = total // block
    row = lambda w: pl.BlockSpec((block, w), lambda i: (i, 0))
    square = pl.BlockSpec((block // span, span, span), lambda i: (i, 0, 0))
    flat = lambda w, kind: jax.ShapeDtypeStruct((total, w), kind)
    return pl.pallas_call(
        retain_kernel,
        grid=(grid,),
        in_specs=[
            row(width), leading(width, 2 * KH + 2 * value_size), row(KH // 2), row(KH // 2), square,
            ANY,
        ],
        out_specs=(
            row(KH), row(KH), row(value_size), square, row(value_size), row(value_size),
            row(value_size), ANY,
        ),
        out_shape=(
            flat(KH, bf16), flat(KH, bf16), flat(value_size, bf16),
            jax.ShapeDtypeStruct(decays.shape, bf16), flat(value_size, f32),
            flat(value_size, f32), flat(value_size, bf16),
            jax.ShapeDtypeStruct(pieces.shape, bf16),
        ),
        scratch_shapes=deal_scratch(pieces.shape[0]),
        compiler_params=params(cid),
        cost_estimate=cost(24),
        name="retain",
    )(normed, weight, cosine, sine, decays, pieces)


def phase_one_of(value, by, sems):
    return phase_one_copies(lax.axis_index("tp"), [value], by[:1], by[1:2], by[2:], *sems)


def retain_back_kernel(
    middle_low, wo, q_in, k_in, v_in, w_in, g_in, r_in, cosine, sine, decays, value,
    low, by_x, by_y, by_sib, *sems
):
    by = (by_x, by_y, by_sib)

    @pl.when(pl.program_id(0) == 0)
    def _():
        greet()
        for c in phase_one_of(value, by, sems):
            c.start()

    packs, span = decays.shape[0], decays.shape[1]
    value_at = 2 * KH
    value_size = v_in.shape[1]
    gate_at = value_at + value_size
    back_branch = lax.dot_general(
        middle_low[...], wo[...], (((1,), (1,)), ((), ())), preferred_element_type=f32
    )
    cols = (((0,), (0,)), ((), ()))
    last = (((1,), (1,)), ((), ()))
    for p in range(packs):
        at = pl.ds(p * span, span)
        bb = back_branch[p * span : (p + 1) * span]
        unit, root = centre(r_in[at, :], head_epsilon)
        gating = g_in[at, :]
        sigma = jax.nn.sigmoid(gating)
        low[at, gate_at:] = (bb * unit * (sigma * (1.0 + gating * (1.0 - sigma)))).astype(bf16)
        retained_low = through_norm(bb * (gating * sigma), unit, root).astype(bf16)
        back_weights = lax.dot_general(retained_low, v_in[at, :], last, preferred_element_type=f32)
        low[at, value_at:gate_at] = lax.dot_general(
            w_in[p], retained_low, cols, preferred_element_type=f32
        ).astype(bf16)
        back_scores = (back_weights * decays[p]).astype(bf16)
        back_q = jnp.dot(back_scores, k_in[at, :], preferred_element_type=f32)
        back_k = lax.dot_general(back_scores, q_in[at, :], cols, preferred_element_type=f32)
        low[at, :KH] = turn(back_q, cosine[at, :], -sine[at, :]).astype(bf16)
        low[at, KH:value_at] = (turn(back_k, cosine[at, :], -sine[at, :]) * KH ** (-0.5)).astype(bf16)

    @pl.when(pl.program_id(0) == pl.num_programs(0) - 1)
    def _():
        for c in phase_one_of(value, by, sems):
            c.wait()


def retain_back(middle_low, wo, q, k, v, w, g, r, cosine, sine, decays, value, block, cid):
    total, width = middle_low.shape
    span = decays.shape[1]
    value_size = v.shape[1]
    row = lambda w: pl.BlockSpec((block, w), lambda i: (i, 0))
    square = pl.BlockSpec((block // span, span, span), lambda i: (i, 0, 0))
    return pl.pallas_call(
        retain_back_kernel,
        grid=(total // block,),
        in_specs=[
            row(width), WHOLE, row(KH), row(KH), row(value_size), square, row(value_size),
            row(value_size), row(KH // 2), row(KH // 2), square, ANY,
        ],
        out_specs=[row(2 * KH + 2 * value_size)] + [ANY] * 3,
        out_shape=[
            jax.ShapeDtypeStruct((total, 2 * KH + 2 * value_size), bf16),
        ]
        + same([value]) * 3,
        scratch_shapes=pair(3),
        compiler_params=params(cid),
        cost_estimate=cost(20),
        name="retain_back",
    )(middle_low, wo, q, k, v, w, g, r, cosine, sine, decays, value)


def half_views(branch, dealt, count, begin):
    size = branch.shape[1] // count
    rows = dealt.shape[0]
    return (
        lambda i: branch.at[pl.ds(begin, rows), pl.ds(pl.multiple_of(i * size, size), size)],
        column_blocks(dealt, size),
    )


def gram_deal_kernel(count, begin, left, right, branch, out, dealt, *sems):
    views = half_views(branch, dealt, count, begin)

    @pl.when(pl.program_id(0) == 0)
    def _():
        deal_start(True, count, *views, *sems)

    out[...] = lax.dot_general(
        left[...], right[...], (((0,), (0,)), ((), ())), preferred_element_type=f32
    ).astype(bf16)

    @pl.when(pl.program_id(0) == pl.num_programs(0) - 1)
    def _():
        deal_wait(True, count, *views, *sems)


def gram_deal(left, right, branch, count, cid):
    total, width = left.shape
    columns = right.shape[1]
    rows = branch.shape[0] // 2
    return pl.pallas_call(
        functools.partial(gram_deal_kernel, count, rows),
        grid=(width // 256,),
        in_specs=[pl.BlockSpec((total, 256), lambda i: (0, i)), WHOLE, ANY],
        out_specs=(pl.BlockSpec((256, columns), lambda i: (i, 0)), ANY),
        out_shape=(
            jax.ShapeDtypeStruct((width, columns), bf16),
            jax.ShapeDtypeStruct((rows, branch.shape[1]), bf16),
        ),
        scratch_shapes=deal_scratch(count),
        compiler_params=params(cid),
        cost_estimate=cost(16),
        name="gram_deal",
    )(left, right, branch)


def feed_kernel(shards, count, normed_two, back_low, w_two, branch, hidden, low, w_down, dealt, *sems):
    size = hidden.shape[1]
    views = half_views(branch, dealt, count, 0) if count else ()

    @pl.when(pl.program_id(0) == 0)
    def _():
        if count:
            deal_start(True, count, *views, *sems)
        unit = size // shards
        span = w_two.shape[0] // shards
        part = w_two.shape[1] - 2 * size
        for z in range(shards):
            for c in range(span // unit):
                begin = z * span + c * unit
                w_down[z * unit : (z + 1) * unit, c * part : (c + 1) * part] = w_two[
                    begin : begin + unit, 2 * size :
                ]

    both = jnp.dot(normed_two[...], w_two[:, : 2 * size], preferred_element_type=f32)
    back = lax.dot_general(
        back_low[...], w_down[...], (((1,), (1,)), ((), ())), preferred_element_type=f32
    )
    up = both[:, size:]
    value, slope = gelu_parts(both[:, :size])
    hidden[...] = (value * up).astype(bf16)
    low[:, :size] = (back * up * slope).astype(bf16)
    low[:, size:] = (back * value).astype(bf16)

    if count:

        @pl.when(pl.program_id(0) == pl.num_programs(0) - 1)
        def _():
            deal_wait(True, count, *views, *sems)


def feed(normed_two, back_low, w_two, branch, size, shards, block, cid):
    total, width = normed_two.shape
    row = lambda w: pl.BlockSpec((block, w), lambda i: (i, 0))
    count = shards if branch.shape[1] // shards % 128 == 0 else 0
    hidden, low, w_down, dealt = pl.pallas_call(
        functools.partial(feed_kernel, shards, count),
        grid=(total // block,),
        in_specs=[row(width), row(width), WHOLE, ANY],
        out_specs=(row(size), row(2 * size), pl.BlockSpec((size, width), lambda i: (0, 0)), ANY),
        out_shape=(
            jax.ShapeDtypeStruct((total, size), bf16),
            jax.ShapeDtypeStruct((total, 2 * size), bf16),
            jax.ShapeDtypeStruct((size, width), bf16),
            jax.ShapeDtypeStruct((total // 2, branch.shape[1]) if count else (8, 128), bf16),
        ),
        scratch_shapes=deal_scratch(count) if count else [],
        compiler_params=params(cid if count else None),
        cost_estimate=cost(26),
        name="feed",
    )(normed_two, back_low, w_two, branch)
    if not count:
        pieces = jnp.transpose(branch.reshape(total, shards, -1), (1, 0, 2))
        pieces = lax.all_to_all(pieces, "tp", split_axis=0, concat_axis=0, tiled=True)
        dealt = jnp.transpose(pieces, (1, 0, 2)).reshape(total, -1)
    return hidden, low, w_down, dealt, count


def gram_kernel(left, right, value, out_a, out_b, by_x, by_y, by_sib, send, recv):
    by = (by_x, by_y, by_sib)

    @pl.when(pl.program_id(0) == 0)
    def _():
        greet()
        for c in phase_one_of(value, by, (send, recv)):
            c.start()

    both = lax.dot_general(
        left[...], right[...], (((0,), (0,)), ((), ())), preferred_element_type=f32
    ).astype(bf16)
    out_a[...] = both[:, : out_a.shape[1]]
    out_b[...] = both[:, out_a.shape[1] :]

    @pl.when(pl.program_id(0) == pl.num_programs(0) - 1)
    def _():
        for c in phase_one_of(value, by, (send, recv)):
            c.wait()


def gram_beside(left, right, value, first, block, cid):
    total, width = left.shape
    sizes = (first, right.shape[1] - first)
    return pl.pallas_call(
        gram_kernel,
        grid=(width // block,),
        in_specs=[pl.BlockSpec((total, block), lambda i: (0, i)), WHOLE, ANY],
        out_specs=[pl.BlockSpec((block, size), lambda i: (i, 0)) for size in sizes] + [ANY] * 3,
        out_shape=[jax.ShapeDtypeStruct((width, size), bf16) for size in sizes]
        + same([value]) * 3,
        scratch_shapes=pair(3),
        compiler_params=params(cid),
        cost_estimate=cost(28),
        name="gram_beside",
    )(left, right, value)


def middle_kernel(branch, wo, x, small, middle, normed_all, own, send1, recv1, sem1, *scratch):
    me = greet()
    reduce_steps(me, [(branch, wo)], False, *scratch)
    final, total = scratch[4], scratch[5]

    def make(at):
        value = x[at, :].astype(f32) + summed(total, final, at)
        middle[at, :] = value
        unit, _ = centre(value, layer_epsilon)
        own[at, :] = (unit * small[2:3, :] + small[3:4, :]).astype(bf16)

    gather_as_made(me, make, own, normed_all, send1, recv1, sem1)


def make_middle(branch, wo, x, small, cid):
    rows, width = x.shape
    return pl.pallas_call(
        middle_kernel,
        out_shape=(
            jax.ShapeDtypeStruct((rows, width), f32),
            jax.ShapeDtypeStruct((8, rows, width), bf16),
        ),
        in_specs=[WHOLE] * 4,
        out_specs=(WHOLE, ANY),
        scratch_shapes=gather_scratch(rows, width) + reduce_scratch(rows, width),
        compiler_params=params(cid),
        cost_estimate=cost(85),
        name="make_middle",
    )(branch, wo, x, small)


def back_middle_kernel(
    low_in, weight_in, middle, back_out, small, _after, _more, back_middle, parts, middle_all,
    low, weight, load, own, send1, recv1, sem1, *scratch,
):
    loads = [
        pltpu.make_async_copy(low_in, low, load.at[0]),
        pltpu.make_async_copy(weight_in.at[:, pl.ds(0, weight.shape[1])], weight, load.at[1]),
    ]
    for c in loads:
        c.start()
    me = greet()
    parts[...] = jnp.zeros_like(parts)
    for c in loads:
        c.wait()
    reduce_steps(me, [(low, weight)], True, *scratch)
    final, total = scratch[4], scratch[5]

    def make(at):
        back = summed(total, final, at)
        unit, root = centre(middle[at, :], layer_epsilon)
        parts[0:1, :] += jnp.sum(back * unit, axis=0, keepdims=True)
        parts[1:2, :] += jnp.sum(back, axis=0, keepdims=True)
        value = back_out[at, :].astype(f32) + through_norm(back * small[2:3, :], unit, root)
        back_middle[at, :] = value
        own[at, :] = value.astype(bf16)

    gather_as_made(me, make, own, middle_all, send1, recv1, sem1)


def make_back_middle(low, weight, middle, back_out, small, after, more, cid):
    rows, width = middle.shape
    return pl.pallas_call(
        back_middle_kernel,
        out_shape=(
            jax.ShapeDtypeStruct((rows, width), f32),
            jax.ShapeDtypeStruct((8, width), f32),
            jax.ShapeDtypeStruct((8, rows, width), bf16),
        ),
        in_specs=[ANY, ANY] + [WHOLE] * 3 + [ANY, ANY],
        out_specs=(WHOLE, WHOLE, ANY),
        scratch_shapes=[
            pltpu.VMEM(low.shape, bf16),
            pltpu.VMEM((width, low.shape[1]), bf16),
            pltpu.SemaphoreType.DMA((2,)),
        ]
        + gather_scratch(rows, width)
        + reduce_scratch(rows, width),
        compiler_params=params(cid),
        cost_estimate=cost(90),
        name="make_back_middle",
    )(low, weight, middle, back_out, small, after, more)


def ending_kernel(
    count, low_in, weight_in, hidden_in, down_in, x, back_middle, middle, usable, small, *refs,
):
    refs = list(refs)

    def take(n):
        got = refs[:n]
        del refs[:n]
        return got

    by_x, by_y = take(count), take(count)
    back_input, out, parts = take(3)
    half_low, half_high, sib_x, sib_y, sib_low, sib_high = (take(count) for _ in range(6))
    low, weight, hidden, down, load = take(5)
    two, three = take(2), take(2)
    first, second = take(8), take(8)
    loads = [
        pltpu.make_async_copy(low_in, low, load.at[0]),
        pltpu.make_async_copy(weight_in.at[:, pl.ds(0, weight.shape[1])], weight, load.at[1]),
        pltpu.make_async_copy(hidden_in, hidden, load.at[2]),
        pltpu.make_async_copy(down_in, down, load.at[3]),
    ]
    for c in loads:
        c.start()
    me = greet()
    started = phase_two(me, by_x, by_y, half_low, half_high, sib_x, sib_y, *two)
    parts[...] = jnp.zeros_like(parts)
    loads[0].wait()
    loads[1].wait()
    one = reduce_stages(me, [(low, weight)], True, *first)
    other = reduce_stages(me, [(hidden, down)], False, *second)
    next(one)
    loads[2].wait()
    loads[3].wait()
    next(other)
    next(one)
    next(other)
    for _ in one:
        pass

    @by_rows(x.shape[0])
    def _(at):
        back = summed(first[5], first[4], at)
        unit, root = centre(x[at, :].astype(f32), layer_epsilon)
        parts[0:1, :] += jnp.sum(back * unit, axis=0, keepdims=True)
        parts[1:2, :] += jnp.sum(back, axis=0, keepdims=True)
        value = back_middle[at, :] + through_norm(back * small[0:1, :], unit, root)
        back_input[at, :] = value.astype(bf16)

    for _ in other:
        pass
    for c in started:
        c.wait()
    last = phase_three(me, half_low, half_high, sib_low, sib_high, *three)

    @by_rows(middle.shape[0])
    def _(at):
        value = middle[at, :] + summed(second[5], second[4], at)
        out[at, :] = jnp.where(usable[at, :] > 0.5, value, 0.0).astype(bf16)

    for c in last:
        c.wait()


def make_ending(
    low, weight, hidden, down, x, back_middle, middle, usable, small, by_x, by_y, cid
):
    rows, width = x.shape
    count = len(by_x)
    shapes = (
        [
            jax.ShapeDtypeStruct((rows, width), bf16),
            jax.ShapeDtypeStruct((rows, width), bf16),
            jax.ShapeDtypeStruct((8, width), f32),
        ]
        + same(by_x, True) * 2
        + same(by_x) * 2
        + same(by_x, True) * 2
    )
    out = pl.pallas_call(
        functools.partial(ending_kernel, count),
        out_shape=shapes,
        in_specs=[ANY] * 4 + [WHOLE] * 5 + [ANY] * (2 * count),
        out_specs=[WHOLE] * 3 + [ANY] * (len(shapes) - 3),
        scratch_shapes=[
            pltpu.VMEM(low.shape, bf16),
            pltpu.VMEM((width, low.shape[1]), bf16),
            pltpu.VMEM(hidden.shape, bf16),
            pltpu.VMEM(down.shape, bf16),
            pltpu.SemaphoreType.DMA((4,)),
        ]
        + pair(4 * count)
        + pair(2 * count)
        + reduce_scratch(rows, width)
        + reduce_scratch(rows, width),
        compiler_params=params(cid),
        cost_estimate=cost(100),
        name="make_ending",
    )(
        low, weight, hidden, down, x, back_middle, middle, usable, small,
        *by_x, *by_y,
    )
    rest = out[3:]
    return *out[:3], [rest[i * count : (i + 1) * count] for i in range(6)]


def last_collect_kernel(count, parts_one, parts_two, *refs):
    fresh, refs = refs[:count], refs[count:]
    sums, refs = refs[0], refs[1:]
    fresh_all, refs = refs[:count], refs[count:]
    parts, turned, far, send_s, recv_s, send_f, recv_f = refs[:7]
    sems = [refs[7 + 3 * k : 10 + 3 * k] for k in range(count)]
    me = greet(True)
    z = lax.axis_index("shard")
    shards = lax.axis_size("shard")
    parts[...] = jnp.zeros_like(parts)
    parts[0:2, :] = parts_one[0:2, :]
    parts[2:4, :] = parts_two[0:2, :]
    turns = [
        push(parts, turned.at[i], send_s.at[i], recv_s.at[i], flip(me, mask))
        for i, mask in enumerate((2, 4, 1))
    ]
    mine = [pltpu.make_async_copy(a, b.at[me], s[2]) for a, b, s in zip(fresh, fresh_all, sems)]
    turns[0].start()
    for c in mine:
        c.start()
    started = [
        gather_begin(me, fresh[0], fresh_all[0], sems[0][0], sems[0][1])
    ]
    turns[0].wait()
    parts[...] += turned[0]
    turns[1].start()
    for a, b, s in list(zip(fresh, fresh_all, sems))[1:]:
        started.append(gather_begin(me, a, b, s[0], s[1]))
    turns[1].wait()
    parts[...] += turned[1]
    turns[2].start()
    turns[2].wait()
    parts[...] += turned[2]
    part = parts.shape[1] // shards
    waiting = []
    for k, other in enumerate(others()):
        c = pltpu.make_async_remote_copy(
            src_ref=parts.at[:, pl.ds(pl.multiple_of(other * part, part), part)],
            dst_ref=far.at[k],
            send_sem=send_f.at[k],
            recv_sem=recv_f.at[k],
            device_id={"shard": other},
            device_id_type=MESHID,
        )
        c.start()
        waiting.append(c)
    for a, b, s, first in zip(fresh, fresh_all, sems, started):
        gather_end(me, a, b, s[0], s[1], first)
    value = parts[:, pl.ds(pl.multiple_of(z * part, part), part)]
    for k, c in enumerate(waiting):
        c.wait()
        value = value + far[k]
    sums[...] = value
    for c in mine:
        c.wait()


def last_collect(parts_one, parts_two, fresh, cid):
    width = parts_one.shape[1]
    shards = lax.axis_size("shard")
    count = len(fresh)
    out = pl.pallas_call(
        functools.partial(last_collect_kernel, count),
        out_shape=[jax.ShapeDtypeStruct((8, width // shards), f32)]
        + [jax.ShapeDtypeStruct((8,) + a.shape, bf16) for a in fresh],
        in_specs=[WHOLE, WHOLE] + [ANY] * count,
        out_specs=[WHOLE] + [ANY] * count,
        scratch_shapes=[
            pltpu.VMEM((8, width), f32),
            pltpu.VMEM((3, 8, width), f32),
            pltpu.VMEM((shards - 1, 8, width // shards), f32),
        ]
        + pair(3)
        + pair(shards - 1)
        + gather_scratch(8, 128)[1:] * count,
        compiler_params=params(cid),
        cost_estimate=cost(5),
        name="last_collect",
    )(parts_one, parts_two, *fresh)
    return out[0], out[1:]


MASKS = (0, 2, 4, 6, 6, 1, 3, 5, 7, 7)
WHEN = (2, 2, 2, 0, 1, 2, 2, 2, 0, 1)


def in_order(parts):
    value, by_x, by_y, low, high, sib, sib_x, sib_y, sib_low, sib_high = parts
    corner, sib_corner = jnp.concatenate([low, high]), jnp.concatenate([sib_low, sib_high])
    stacked = jnp.stack([value, sib, by_x, sib_x, by_y, sib_y, corner, sib_corner])
    return jnp.take(stacked, jnp.arange(8) ^ lax.axis_index("tp"), axis=0)


def widen_two_kernel(steps, shards, *refs):
    t = lax.axis_index("tp")
    late = (pl.program_id(0) >= steps // 2).astype(jnp.int32)
    seconds, downs, outs = refs[:10], refs[10:20], refs[20]
    gelu, up, down, out = refs[21:]
    out[...] = outs[...].astype(f32)
    unit = gelu.shape[1] // (8 * shards)

    def store(i):
        place = flip(t, MASKS[i])
        down[place] = downs[i][...].astype(f32)
        for z in range(shards):
            at = pl.ds(pl.multiple_of((8 * z + place) * unit, unit), unit)
            gelu[:, at] = seconds[i][:, z * unit : (z + 1) * unit].astype(f32)
            up[:, at] = seconds[i][:, (shards + z) * unit : (shards + z + 1) * unit].astype(f32)

    for i in range(10):
        if WHEN[i] == 2:
            store(i)
        else:

            @pl.when(late == WHEN[i])
            def _():
                store(i)


def widen_two(seconds, downs, outs, shards):
    rows, columns = seconds[0].shape
    count, width = downs[0].shape
    steps = 4

    def row_at(which, i):
        half = steps // 2
        return (i, jnp.minimum(i, half - 1), jnp.maximum(i - half, 0))[(which + 1) % 3]

    def specs(parts):
        return [
            pl.BlockSpec(
                (parts[0].shape[0] // steps, parts[0].shape[1]),
                functools.partial(lambda w, i: (row_at(w, i), 0), w),
            )
            for w in WHEN
        ]

    units = jax.ShapeDtypeStruct((rows, 4 * columns), f32)
    stack = jax.ShapeDtypeStruct((8, count, width), f32)
    gelu, up, down, out = pl.pallas_call(
        functools.partial(widen_two_kernel, steps, shards),
        grid=(steps,),
        in_specs=specs(seconds)
        + specs(downs)
        + [pl.BlockSpec((8, count // steps, width), lambda i: (0, i, 0))],
        out_specs=[pl.BlockSpec((rows // steps, 4 * columns), lambda i: (i, 0))] * 2
        + [pl.BlockSpec((8, count // steps, width), lambda i: (0, i, 0))] * 2,
        out_shape=[units, units, stack, stack],
        compiler_params=params(),
        cost_estimate=cost(25),
        name="widen_two",
    )(*seconds, *downs, outs)
    return gelu, up, down.reshape(8 * count, width), out.reshape(8 * count, width)


def widen_one_kernel(edges, parts, _after, *goals):
    for goal, (begin, end) in zip(goals, zip(edges, edges[1:])):
        size = end - begin
        for i in range(8):
            goal[:, i * size : (i + 1) * size] = parts[i, :, begin:end].astype(f32)


def widen_one(parts, edges, after, name):
    _, rows, columns = parts.shape
    sizes = [b - a for a, b in zip(edges, edges[1:])]
    block = 128
    return pl.pallas_call(
        functools.partial(widen_one_kernel, edges),
        grid=(rows // block,),
        in_specs=[pl.BlockSpec((8, block, columns), lambda i: (0, i, 0)), ANY],
        out_specs=[pl.BlockSpec((block, 8 * size), lambda i: (i, 0)) for size in sizes],
        out_shape=[jax.ShapeDtypeStruct((rows, 8 * size), f32) for size in sizes],
        compiler_params=params(),
        cost_estimate=cost(14),
        name=name,
    )(parts, after)


def local(
    tokens,
    cotangent,
    token_order,
    lengths,
    query_weight,
    key_weight,
    value_weight,
    gate_weight,
    out_weight,
    gelu_weight,
    up_weight,
    down_weight,
    gain_one,
    shift_one,
    gain_two,
    shift_two,
):
    every = ("outer", "tp", "shard")
    device_count = lax.axis_size(every)
    device_index = lax.axis_index(every)
    outer, tp, shards = lax.axis_size("outer"), lax.axis_size("tp"), lax.axis_size("shard")
    t, z = lax.axis_index("tp"), lax.axis_index("shard")
    rows, width = tokens.shape
    packs = lengths.shape[0]
    pack_rows = rows // packs
    group_rows = tp * rows
    group_packs = tp * packs

    own_order = lax.dynamic_slice_in_dim(token_order, device_index * rows, rows)
    target = own_order // rows
    places = jnp.arange(rows, dtype=jnp.int32)
    before = (target[None, :] < target[:, None]) | (
        (target[None, :] == target[:, None]) & (places[None, :] < places[:, None])
    )
    send_place = jnp.sum(before.astype(jnp.int32), axis=1)
    send_mix = (send_place[None, :] == places[:, None]).astype(bf16)
    loader_ids = jnp.arange(token_order.shape[0], dtype=jnp.int32)
    slot_targets = device_index * rows + places
    origin = jnp.sum(
        jnp.where(token_order[None, :] == slot_targets[:, None], loader_ids[None, :], 0), axis=1
    )
    arrive_place = jnp.sum((origin[None, :] < origin[:, None]).astype(jnp.int32), axis=1)
    work_mix = (arrive_place[:, None] == places[None, :]).astype(bf16)

    def exchange(value):
        return lax.all_to_all(
            value.reshape(device_count, rows // device_count, value.shape[1]),
            every,
            split_axis=0,
            concat_axis=0,
            tiled=True,
        ).reshape(rows, value.shape[1])

    piece = rows // device_count
    part = gain_one.shape[0]
    extra = jnp.concatenate(
        [gain_one, shift_one, gain_two, shift_two, lengths.reshape(-1).astype(bf16)]
    )
    extra_columns = -(-extra.shape[0] // (piece * 128)) * 128
    extra = jnp.pad(extra, (0, piece * extra_columns - extra.shape[0]))
    extra = jnp.tile(extra.reshape(piece, extra_columns), (device_count, 1))
    came = exchange(
        jnp.concatenate([forward_dot(send_mix, tokens).astype(bf16), extra], axis=1)
    )
    sent_back = forward_dot(send_mix, cotangent).astype(bf16)
    came_back = exchange(sent_back)
    arrived = came[:, width:].reshape(outer, tp, shards, -1)
    small = jnp.transpose(arrived[0, 0, :, : 4 * part].reshape(shards, 4, part), (1, 0, 2))
    small = small.reshape(4, width).astype(f32)
    small = jnp.concatenate([small, jnp.zeros((4, width), f32)], axis=0)
    all_lengths = arrived[lax.axis_index("outer"), :, z, 4 * part : 4 * part + lengths.size]
    all_lengths = all_lengths.reshape(group_packs, -1).astype(f32).astype(jnp.int32)

    def along_z(piece):
        return lax.all_gather(piece, "shard", axis=0, tiled=True)

    def cut(weight):
        part = weight.shape[1] // tp
        return lax.dynamic_slice_in_dim(weight, t * part, part, axis=1)

    out_unit = out_weight.shape[0] // tp
    unit = down_weight.shape[0] // tp
    piece_rows = query_weight.shape[0]
    key_part, value_part = query_weight.shape[1] // tp, value_weight.shape[1] // tp
    edges = (0, key_part, 2 * key_part, 2 * key_part + value_part)
    first_size = 2 * key_part + 2 * value_part
    hidden_part = shards * unit

    def fold(value):
        cuts = piece_rows // value.shape[0]
        value = value.reshape(value.shape[0], cuts, width // cuts)
        return jnp.transpose(value, (1, 0, 2)).reshape(piece_rows, width // cuts)

    def unfold(value, count):
        cuts = piece_rows // count
        value = value.reshape(shards, cuts, count, width // cuts)
        return jnp.transpose(value, (0, 2, 1, 3)).reshape(shards, count, width)

    out_piece = lax.dynamic_slice_in_dim(out_weight, t * out_unit, out_unit, axis=0)
    w_one = along_z(
        jnp.concatenate(
            [cut(w) for w in (query_weight, key_weight, value_weight, gate_weight)]
            + [fold(out_piece)],
            axis=1,
        )
    )
    ends = jnp.cumsum(lengths, axis=1, dtype=jnp.int32)[:, -2]
    usable = (jnp.arange(pack_rows, dtype=jnp.int32)[None, :] < ends[:, None]).astype(f32)
    usable = usable.reshape(rows, 1)
    x, normed = entry(came, work_mix, small, 0)
    def unit_columns(weight):
        return [
            lax.dynamic_slice_in_dim(weight, (k * tp + t) * unit, unit, axis=1)
            for k in range(shards)
        ]

    down_piece = lax.dynamic_slice_in_dim(down_weight, t * unit, unit, axis=0)
    second_piece = lax.optimization_barrier(
        jnp.concatenate(
            unit_columns(gelu_weight) + unit_columns(up_weight) + [fold(down_piece)], axis=1
        )
    )
    w_two = along_z(second_piece + jnp.isnan(x[0, 0]).astype(bf16))
    back_out, back_low = entry_back(came_back, work_mix, usable, x, 7)
    normed, back_low = normed.reshape(group_rows, width), back_low.reshape(group_rows, width)
    cosine, sine, decays, _ = pack_tables(all_lengths, pack_rows, t + jnp.arange(1))
    cosine, sine = cosine.reshape(group_rows, -1), sine.reshape(group_rows, -1)
    decays = decays[0]
    out_pieces = unfold(w_one[:, first_size:], out_unit)
    q_rot, k_rot, v_low, weights_low, gating, retained, branch, wo = retain(
        normed, w_one, value_part, cosine, sine, decays, out_pieces, rows, 1
    )
    wo = wo.reshape(shards * out_unit, width)
    middle, normed_two = make_middle(branch, wo, x, small, 2)
    normed_two = normed_two.reshape(group_rows, width)

    hidden, second_low, w_down, branch_rows, halved = feed(
        normed_two, back_low, w_two, branch, hidden_part, shards, rows, 6
    )
    down_gram = gram_rows(hidden, back_low).astype(bf16)
    if halved:
        second_gram, branch_more = gram_deal(normed_two, second_low, branch, shards, 12)
        branch_rows = jnp.concatenate([branch_rows, branch_more])
    else:
        second_gram = gram_rows(normed_two, second_low).astype(bf16)

    def to_owner(value):
        part = lax.psum_scatter(value, "shard", scatter_dimension=0, tiled=True)
        return lax.psum(part, "outer") if outer > 1 else part

    down_sum, second_sum = to_owner(down_gram), to_owner(second_gram)
    back_middle, parts_two, middle_low = make_back_middle(
        second_low, w_two, middle, back_out, small, down_gram, second_gram, 3
    )
    middle_low = middle_low.reshape(group_rows, width)
    out_sum = to_owner(gram_rows(branch_rows, middle_low).astype(bf16))
    first_low, *down_by = retain_back(
        middle_low, wo, q_rot, k_rot, v_low, weights_low, gating, retained, cosine, sine, decays,
        down_sum, rows, 8,
    )
    first_gram, third_gram, *second_by = gram_beside(
        normed, first_low, second_sum, edges[3], 256, 9
    )
    first_sum, third_sum = to_owner(first_gram), to_owner(third_gram)
    by_x, by_y, by_sib = ([a, b] for a, b in zip(second_by, down_by))
    back_inputs, ending, parts_one, groups = make_ending(
        first_low, w_one, hidden, w_down, x, back_middle, middle, usable, small, by_x, by_y, 5
    )
    sums, (outs, firsts) = last_collect(parts_one, parts_two, [out_sum, first_sum], 10)
    low, high, sib_x, sib_y, sib_low, sib_high = groups
    seconds, downs = (
        [
            value, by_x[k], by_y[k], low[k], high[k],
            by_sib[k], sib_x[k], sib_y[k], sib_low[k], sib_high[k],
        ]
        for k, value in enumerate((second_sum, down_sum))
    )

    if unit % 128 == 0:
        gelu_gradient, up_gradient, down_gradient, out_gradient = widen_two(
            seconds, downs, outs, shards
        )
    else:
        down_gradient = in_order(downs).reshape(-1, width).astype(f32)
        out_gradient = outs.reshape(-1, width).astype(f32)
        both = in_order(seconds).reshape(tp, piece_rows, 2, shards, unit)
        both = jnp.transpose(both, (2, 1, 3, 0, 4)).reshape(2, piece_rows, -1).astype(f32)
        gelu_gradient, up_gradient = both[0], both[1]
    nothing = jnp.isnan(outs[0, 0, 0]).astype(bf16)
    thirds = lax.all_gather(third_sum + nothing, "tp", axis=0)
    query_gradient, key_gradient, value_gradient = widen_one(
        firsts, edges, down_gradient, "widen_one"
    )
    (gate_gradient,) = widen_one(thirds, (0, value_part), query_gradient, "widen_three")
    smalls = lax.psum(sums, "outer") if outer > 1 else sums

    home = jnp.concatenate([ending, back_inputs], axis=1)
    home = exchange(gram_rows(work_mix + nothing, home).astype(bf16))
    home = gram_rows(send_mix, home).astype(bf16)
    result, token_gradient = home[:, :width], home[:, width:]
    return (
        result,
        token_gradient,
        query_gradient,
        key_gradient,
        value_gradient,
        gate_gradient,
        out_gradient,
        gelu_gradient,
        up_gradient,
        down_gradient,
        smalls[0],
        smalls[1],
        smalls[2],
        smalls[3],
    )


def solution(mesh):
    tp = math.gcd(mesh.shape["rep"], HEADS)
    grid = mesh.devices.reshape(mesh.shape["rep"] // tp, tp, mesh.shape["shard"])
    cube = Mesh(grid, ("outer", "tp", "shard"))
    tokens_at = P(("outer", "tp", "shard"), None)
    weights_at = P("shard", None)
    vectors_at = P("shard")
    in_specs = (tokens_at, tokens_at, P(), tokens_at) + (weights_at,) * 8 + (vectors_at,) * 4
    out_specs = (tokens_at, tokens_at) + (weights_at,) * 8 + (vectors_at,) * 4
    return jax.shard_map(local, mesh=cube, in_specs=in_specs, out_specs=out_specs, check_vma=False)
```
